128 devices in a mesh: fsdp: 4 (over y_lo, core), dp: 32 (over z, x, y_hi).
Axes of the slice: x: 4, y: 4 (y_hi: 2, y_lo: 2; y = y_hi * 2 + y_lo), z: 4, core: 2. Of those that a mesh axis runs over, the one named last changes fastest.
Arguments:
- tokens: bfloat16 [65536, 1024], P(('fsdp', 'dp')), may hold values from -6 to 6
- norm_gain: bfloat16 [1024], P('fsdp'), may hold values from 0.25 to 1.75
- in_proj: bfloat16 [1024, 4384], P('fsdp'), may hold values from -0.1875 to 0.1875
- conv_weight: bfloat16 [4, 2304], P(None, 'fsdp'), may hold values from -0.796875 to 0.796875
- conv_bias: bfloat16 [2304], P('fsdp'), may hold values from -0.5 to 0.5
- dt_bias: bfloat16 [32], P('fsdp'), may hold values from -6 to -1
- a_log: bfloat16 [32], P('fsdp'), may hold values from 0 to 2.6875
- d_skip: bfloat16 [32], P('fsdp'), may hold values from 0.29882812 to 1.5
- gate_gain: bfloat16 [2048], P('fsdp'), may hold values from 0.25 to 1.75
- out_proj: bfloat16 [2048, 1024], P('fsdp'), may hold values from -0.125 to 0.125
- out_grad: bfloat16 [65536, 1024], P(('fsdp', 'dp')), may hold values from -6 to 6
- lengths: int32 [256], P(('fsdp', 'dp')), may hold values from 1 to 256, as said below
Outputs:
- block_out: bfloat16 [65536, 1024], P(('fsdp', 'dp'))
- tokens_grad: float32 [65536, 1024], P(('fsdp', 'dp'))
- norm_gain_grad: float32 [1024], P('fsdp')
- in_proj_grad: float32 [1024, 4384], P('fsdp')
- conv_weight_grad: float32 [4, 2304], P(None, 'fsdp')
- conv_bias_grad: float32 [2304], P('fsdp')
- dt_bias_grad: float32 [32], P('fsdp')
- a_log_grad: float32 [32], P('fsdp')
- d_skip_grad: float32 [32], P('fsdp')
- gate_gain_grad: float32 [2048], P('fsdp')
- out_proj_grad: float32 [2048, 1024], P('fsdp')
The draws below stay inside these ranges and needn't reach their ends.
Inputs may be any that keep to these rules, and one draw needn't show every extreme that they name: `lengths`: every slot holds between one and 256 live rows; some slot is full in every draw.
All inputs are finite; a program needn't handle non-finite values.
Results may differ from the reference program's by a relative error of at most 0.025.
Values may be sent and summed in bfloat16 or wider, within the bound.
No kernel may reach another device: no remote copies, remote signals or barrier semaphores. Data moves between devices by JAX's collectives and lax.ppermute only.
A program may use at most 192 MiB of HBM per device.

```python
import math
import jax
import jax.numpy as jnp
from jax import lax

D = 1024
INNER = 2048
CONV = 4
LEN = 256
HEADS = 32
CONVCH = 2304
PROJ = 4384
TOKENS = 65536


def draw_lengths(key, part):
    key = jax.random.fold_in(key, 7)
    first, second = jax.random.split(key)
    count = TOKENS // LEN
    drawn = jax.random.randint(first, (count,), 1, LEN + 1)
    where_full = jax.random.randint(second, (), 0, count)
    return jnp.where(jnp.arange(count) == where_full, LEN, drawn).astype(jnp.int32)


def levels(stream_key, dims, cuts, low, largest):
    gain = 1.0
    for axis_at, parts in cuts:
        steps = jax.random.uniform(jax.random.fold_in(jax.random.fold_in(stream_key, 6), axis_at), (parts,), jnp.float32, low / len(cuts), largest / len(cuts))
        gain = gain * jnp.repeat(jnp.exp(steps), dims[axis_at] // parts).reshape((-1,) + (1,) * (len(dims) - 1 - axis_at))
    return gain


def bell_draw(own_key, shape, scale, most, cuts=(), kind=jnp.bfloat16):
    entries = jax.random.normal(own_key, shape, jnp.float32) * scale
    if len(cuts) > 0:
        entries = levels(own_key, shape, cuts, -0.22, 0.18) * entries
    return jnp.clip(entries, min=-most, max=most).astype(kind)


def setup_inputs(seed: int = 0) -> dict:
    keys = jax.random.split(jax.random.key(seed), 13)
    tokens = bell_draw(keys[0], (TOKENS, D), 1.0, 6.0, ((0, 128),))
    norm_gain = jnp.clip(1.0 + 0.15 * jax.random.normal(keys[1], (D,), jnp.float32), 0.25, 1.75).astype(jnp.bfloat16)
    in_proj = bell_draw(keys[2], (D, PROJ), D ** -0.5, 0.1875, ((0, 4),))
    conv_weight = jnp.clip(jax.random.uniform(keys[3], (CONV, CONVCH), jnp.float32, -0.796875, 0.796875) * levels(keys[3], (CONV, CONVCH), ((1, 4),), -0.4, 0.0), -0.796875, 0.796875).astype(jnp.bfloat16)
    conv_bias = jnp.clip(jax.random.uniform(keys[4], (CONVCH,), jnp.float32, -0.5, 0.5) * levels(keys[4], (CONVCH,), ((0, 4),), -0.4, 0.0), -0.5, 0.5).astype(jnp.bfloat16)
    dt_bias = jnp.clip(-6.0 + 5.0 * jax.random.uniform(keys[5], (HEADS,), jnp.float32) ** levels(keys[5], (HEADS,), ((0, 4),), -0.2, 0.2), -6.0, -1.0).astype(jnp.bfloat16)
    a_log = jnp.clip(2.6875 * jax.random.uniform(keys[6], (HEADS,), jnp.float32) ** levels(keys[6], (HEADS,), ((0, 4),), -0.2, 0.2), 0.0, 2.6875).astype(jnp.bfloat16)
    d_skip = jnp.clip(0.29882812 + 1.2011719 * jax.random.uniform(keys[7], (HEADS,), jnp.float32) ** levels(keys[7], (HEADS,), ((0, 4),), -0.2, 0.2), 0.29882812, 1.5).astype(jnp.bfloat16)
    gate_gain = jnp.clip(1.0 + 0.15 * jax.random.normal(keys[8], (INNER,), jnp.float32), 0.25, 1.75).astype(jnp.bfloat16)
    out_proj = bell_draw(keys[9], (INNER, D), INNER ** -0.5, 0.125, ((0, 4),))
    out_grad = bell_draw(keys[10], (TOKENS, D), 1.0, 6.0, ((0, 128),))
    lengths = draw_lengths(jax.random.fold_in(keys[12], 71), 0)
    return dict(tokens=tokens, norm_gain=norm_gain, in_proj=in_proj, conv_weight=conv_weight, conv_bias=conv_bias, dt_bias=dt_bias, a_log=a_log, d_skip=d_skip, gate_gain=gate_gain, out_proj=out_proj, out_grad=out_grad, lengths=lengths)


@jax.custom_vjp
def low(v):
    return lax.optimization_barrier(v.astype(jnp.bfloat16)).astype(jnp.float32)

@jax.custom_vjp
def low_back(v):
    return v

def low_keep(v):
    return (low(v), None)

def low_pass(kept, grad):
    return (grad,)

def back_keep(v):
    return (v, None)

def back_low(kept, grad):
    return (low(grad),)
low.defvjp(low_keep, low_pass)
low_back.defvjp(back_keep, back_low)
EXACT = lax.Precision.HIGHEST

def slot_out(params, inputs, count):
    norm_gain, in_proj, conv_weight, conv_bias, dt_bias, a_log, d_skip, gate_gain, out_proj = params
    rows = inputs.shape[0]
    inner = out_proj.shape[0]
    heads = a_log.shape[0]
    channels = conv_weight.shape[1]
    state = (channels - inner) // 2
    taps = conv_weight.shape[0]
    normed_in = low(inputs * lax.rsqrt(lax.optimization_barrier(jnp.mean(inputs * inputs, axis=1, keepdims=True)) + 1e-05) * norm_gain)
    proj = low_back(jnp.dot(normed_in, in_proj, precision=EXACT))
    gate_part = proj[:, :inner]
    conv_in = proj[:, inner:inner + channels]
    step_raw = proj[:, inner + channels:]
    padded = jnp.concatenate([jnp.zeros((taps - 1, channels), jnp.float32), conv_in], axis=0)
    conv_sum = conv_bias[None, :] + padded[0:rows] * conv_weight[0][None, :]
    for index in range(1, taps):
        conv_sum = conv_sum + padded[index:index + rows] * conv_weight[index][None, :]
    conv_act = jax.nn.silu(conv_sum)
    values = low(conv_act[:, :inner])
    bmat = low(conv_act[:, inner:inner + state])
    cmat = low(conv_act[:, inner + state:])
    step = jax.nn.softplus(step_raw + dt_bias[None, :])
    logdecay = -step * jnp.exp(a_log)[None, :]
    cum = jnp.cumsum(logdecay, axis=0).T
    causal = (jnp.arange(rows)[:, None] >= jnp.arange(rows)[None, :])[None, :, :]
    spread = jnp.where(causal, cum[:, :, None] - cum[:, None, :], 0.0)
    decay = jnp.where(causal, jnp.exp(spread), 0.0)
    scores = low_back(jnp.dot(cmat, bmat.T, precision=EXACT))
    mix = low(scores[None, :, :] * decay * step.T[:, None, :])
    heads_in = values.reshape(rows, heads, inner // heads)
    summed = low_back(jnp.einsum('hij,jhp->ihp', mix, heads_in, precision=EXACT))
    scanned = (summed + d_skip[None, :, None] * heads_in).reshape(rows, inner)
    gated = scanned * jax.nn.silu(gate_part)
    mixed_in = low(gated * lax.rsqrt(lax.optimization_barrier(jnp.mean(gated * gated, axis=1, keepdims=True)) + 1e-05) * gate_gain)
    result = inputs + jnp.dot(mixed_in, out_proj, precision=EXACT)
    live = jnp.arange(rows) < count
    return jnp.where(live[:, None], result, 0.0)

def reference(tokens, norm_gain, in_proj, conv_weight, conv_bias, dt_bias, a_log, d_skip, gate_gain, out_proj, out_grad, lengths):
    params = tuple((weight.astype(jnp.float32) for weight in (norm_gain, in_proj, conv_weight, conv_bias, dt_bias, a_log, d_skip, gate_gain, out_proj)))
    inputs = tokens.astype(jnp.float32)
    slots = lengths.shape[0]
    width = inputs.shape[1]
    group = math.gcd(slots, 16)

    def forward(weights, rows_in):
        blocks = rows_in.reshape(slots // group, group, LEN, width)
        counts = lengths.reshape(slots // group, group)

        def one_group(item):
            return jax.vmap(lambda block, count: slot_out(weights, block, count))(item[0], item[1])
        result = lax.map(jax.checkpoint(one_group), (blocks, counts))
        return result.reshape(slots * LEN, width)
    result, pullback = jax.vjp(forward, params, inputs)
    grads, tokens_grad = pullback(out_grad.astype(jnp.float32))
    return (result.astype(jnp.bfloat16), tokens_grad, grads[0], grads[1], grads[2], grads[3], grads[4], grads[5], grads[6], grads[7], grads[8])
```

```python
import functools
import jax
import jax.numpy as jnp
from jax import lax
from jax.experimental import pallas as pl
from jax.experimental.pallas import tpu as pltpu
from jax.sharding import Mesh, PartitionSpec as P

D = 1024
INNER = 2048
CONV = 4
LEN = 256
HEADS = 32
STATE = 128
CONVCH = 2304
HALF = 128
GROUPS = 4
GCOLS = INNER // GROUPS
GHEADS = HEADS // GROUPS
BF = jnp.bfloat16
F32 = jnp.float32
LOG2E = 1.4426950408889634
VMEM_LIMIT = 50 * 1024 * 1024


def dot(a, b):
    return lax.dot_general(a, b, (((1,), (0,)), ((), ())), preferred_element_type=F32)


def dot_nt(a, b):
    return lax.dot_general(a, b, (((1,), (1,)), ((), ())), preferred_element_type=F32)


def dot_tn(a, b):
    return lax.dot_general(a, b, (((0,), (0,)), ((), ())), preferred_element_type=F32)


def dot_exact(ones, v):
    hi = v.astype(BF)
    rest = v - hi.astype(F32)
    mid = rest.astype(BF)
    low = (rest - mid.astype(F32)).astype(BF)
    return dot(ones, hi) + dot(ones, mid) + dot(ones, low)


def dot_split(v, ones):
    hi = v.astype(BF)
    low = (v - hi.astype(F32)).astype(BF)
    return dot(hi, ones) + dot(low, ones)


def sigmoid(v):
    return 0.5 * jnp.tanh(0.5 * v) + 0.5


def rows_down(v, count):
    row = lax.broadcasted_iota(jnp.int32, v.shape, 0)
    return jnp.where(row >= count, pltpu.roll(v, count, axis=0), 0.0)


def rows_up(v, count):
    rows = v.shape[0]
    row = lax.broadcasted_iota(jnp.int32, v.shape, 0)
    return jnp.where(row < rows - count, pltpu.roll(v, rows - count, axis=0), 0.0)


def conv_forward(x, taps, bias):
    total = bias + taps[3:4] * x
    for back in range(1, CONV):
        total = total + taps[3 - back : 4 - back] * rows_down(x, back)
    return total


def conv_backward(x, taps, bias, dact, dtaps_ref, columns):
    v = conv_forward(x, taps, bias)
    sg = sigmoid(v)
    dv = dact * (sg * (1.0 + v * (1.0 - sg)))
    dx = taps[3:4] * dv
    sums = [jnp.sum(dv * x, axis=0, keepdims=True)]
    for back in range(1, CONV):
        dx = dx + taps[3 - back : 4 - back] * rows_up(dv, back)
        sums.insert(0, jnp.sum(dv * rows_down(x, back), axis=0, keepdims=True))
    sums.append(jnp.sum(dv, axis=0, keepdims=True))
    sums.append(jnp.zeros((3, x.shape[1]), F32))
    dtaps_ref[0, :, columns] = jnp.concatenate(sums, axis=0)
    return dx


def step_of(raw, bias):
    z = raw + bias
    return jnp.maximum(z, 0.0) + jnp.log1p(jnp.exp(-jnp.abs(z)))


def tri_masks():
    down = lax.broadcasted_iota(jnp.int32, (HALF, HALF), 0)
    across = lax.broadcasted_iota(jnp.int32, (HALF, HALF), 1)
    return down, across


def head_lanes(v, first):
    lane = lax.broadcasted_iota(jnp.int32, v.shape, 1)
    zero = jnp.zeros_like(v)
    return jnp.where(lane < 64, v, zero) if first else jnp.where(lane < 64, zero, v)


def scan_forward_kernel(
    xv_ref, xbc_ref, raw_ref, tv_ref, tbc_ref, dtb_ref, alog_ref,
    summed_ref, v_ref, bc_ref, step_ref, cum_ref,
    s_ref, cumt_ref, stept_ref,
):
    group = pl.program_id(1)

    @pl.when(group == 0)
    def _():
        act = conv_forward(xbc_ref[...], tbc_ref[0:4, :], tbc_ref[4:5, :])
        bc = (act * sigmoid(act)).astype(BF)
        bc_ref[...] = bc
        s_ref[...] = dot_nt(bc[:, STATE:], bc[:, :STATE])
        step = step_of(raw_ref[...], dtb_ref[...])
        logdecay = -step * jnp.exp(alog_ref[...])
        row = lax.broadcasted_iota(jnp.int32, (LEN, LEN), 0)
        col = lax.broadcasted_iota(jnp.int32, (LEN, LEN), 1)
        lower = jnp.where(row >= col, 1.0, 0.0).astype(BF)
        cum = dot_exact(lower, logdecay) * LOG2E
        step_ref[...] = step
        cum_ref[...] = cum
        cumt_ref[...] = cum.T
        stept_ref[...] = step.T

    act = conv_forward(xv_ref[...], tv_ref[0:4, :], tv_ref[4:5, :])
    v_ref[...] = (act * sigmoid(act)).astype(BF)
    cols = pltpu.roll(cum_ref[...], lax.rem(128 - GHEADS * group, 128), axis=1)
    first = pl.multiple_of(GHEADS * group, GHEADS)
    cum_rows = cumt_ref[pl.ds(first, GHEADS), :]
    step_rows = stept_ref[pl.ds(first, GHEADS), :]
    down, across = tri_masks()
    live = down >= across
    for pair in range(GHEADS // 2):
        lanes = slice(128 * pair, 128 * pair + 128)
        vp = v_ref[:, lanes]
        top = jnp.zeros((HALF, 128), F32)
        bottom = jnp.zeros((HALF, 128), F32)
        for side in range(2):
            head = 2 * pair + side
            vm = head_lanes(vp, side == 0)
            ci = cols[:, head : head + 1]
            cj = cum_rows[head : head + 1, :]
            sj = step_rows[head : head + 1, :]
            w00 = jnp.where(live, jnp.exp2(ci[:HALF] - cj[:, :HALF]), 0.0) * sj[:, :HALF]
            w10 = jnp.exp2(ci[HALF:] - cj[:, :HALF]) * sj[:, :HALF]
            w11 = jnp.where(live, jnp.exp2(ci[HALF:] - cj[:, HALF:]), 0.0) * sj[:, HALF:]
            m00 = (s_ref[:HALF, :HALF] * w00).astype(BF)
            m10 = (s_ref[HALF:, :HALF] * w10).astype(BF)
            m11 = (s_ref[HALF:, HALF:] * w11).astype(BF)
            top = top + dot(m00, vm[:HALF])
            bottom = bottom + dot(jnp.concatenate([m10, m11], axis=1), vm)
        summed_ref[:HALF, lanes] = top
        summed_ref[HALF:, lanes] = bottom


def scan_forward(xconv, raw, taps, dtb, alog, slots):
    rows = slots * LEN
    by_slot = lambda slot, group: (slot, 0)
    fixed = lambda slot, group: (0, 0)
    return pl.pallas_call(
        scan_forward_kernel,
        grid=(slots, GROUPS),
        in_specs=[
            pl.BlockSpec((LEN, GCOLS), lambda slot, group: (slot, group)),
            pl.BlockSpec((LEN, 2 * STATE), lambda slot, group: (slot, INNER // (2 * STATE))),
            pl.BlockSpec((LEN, 128), by_slot),
            pl.BlockSpec((8, GCOLS), lambda slot, group: (0, group)),
            pl.BlockSpec((8, 2 * STATE), lambda slot, group: (0, INNER // (2 * STATE))),
            pl.BlockSpec((1, 128), fixed),
            pl.BlockSpec((1, 128), fixed),
        ],
        out_specs=[
            pl.BlockSpec((LEN, GCOLS), lambda slot, group: (slot, group)),
            pl.BlockSpec((LEN, GCOLS), lambda slot, group: (slot, group)),
            pl.BlockSpec((LEN, 2 * STATE), by_slot),
            pl.BlockSpec((LEN, 128), by_slot),
            pl.BlockSpec((LEN, 128), by_slot),
        ],
        out_shape=[
            jax.ShapeDtypeStruct((rows, INNER), F32),
            jax.ShapeDtypeStruct((rows, INNER), BF),
            jax.ShapeDtypeStruct((rows, 2 * STATE), BF),
            jax.ShapeDtypeStruct((rows, 128), F32),
            jax.ShapeDtypeStruct((rows, 128), F32),
        ],
        scratch_shapes=[
            pltpu.VMEM((LEN, LEN), F32),
            pltpu.VMEM((128, LEN), F32),
            pltpu.VMEM((128, LEN), F32),
        ],
        compiler_params=pltpu.CompilerParams(
            dimension_semantics=("arbitrary", "arbitrary"), vmem_limit_bytes=VMEM_LIMIT
        ),
        name="scan_forward",
    )(xconv, xconv, raw, taps, taps, dtb, alog)


def middle_kernel(
    index_ref, len_ref, summed_ref, v_ref, gate_ref, tok_ref, og_ref, gain_ref, skip_ref,
    own_ref, core_ref, up_ref, down_ref, cup_ref, cdown_ref,
    out_ref, m_ref, do_ref, dscan_ref, dgate_ref, rowsum_ref, sums_ref, dm_ref,
):
    me = index_ref[0]
    part = own_ref.shape[0]
    weights = [
        own_ref[...],
        core_ref[...],
        jnp.concatenate([up_ref[...], down_ref[...]], axis=0),
        jnp.concatenate([cup_ref[...], cdown_ref[...]], axis=0),
    ]
    channels = [pl.ds(pl.multiple_of((me ^ k) * part, part), part) for k in range(4)]
    step = pl.program_id(0)
    block = summed_ref.shape[0]
    per_slot = LEN // block
    count = len_ref[step // per_slot]
    row = lax.broadcasted_iota(jnp.int32, (block, 1), 0) + lax.rem(step, per_slot) * block
    live = row < count

    @pl.when(step == 0)
    def _():
        sums_ref[...] = jnp.zeros_like(sums_ref)

    summed = summed_ref[...]
    v = v_ref[...].astype(F32)
    gate = gate_ref[...]
    gain = gain_ref[...]
    skip = skip_ref[...]
    scanned = summed + skip * v
    sg = sigmoid(gate)
    act = gate * sg
    gated = scanned * act
    scale = lax.rsqrt(jnp.mean(gated * gated, axis=1, keepdims=True) + 1e-05)
    unit = gated * scale
    mixed = (unit * gain).astype(BF)
    m_ref[...] = mixed
    result = tok_ref[...].astype(F32)
    for lanes, weight in zip(channels, weights):
        result = result + dot(m_ref[:, lanes], weight)
    out_ref[...] = jnp.where(live, result, 0.0).astype(BF)
    dout = jnp.where(live, og_ref[...].astype(F32), 0.0).astype(BF)
    do_ref[...] = dout
    for lanes, weight in zip(channels, weights):
        dm_ref[:, lanes] = dot_nt(dout, weight)
    dmixed = dm_ref[...]
    sums_ref[0:1, :] += jnp.sum(dmixed * unit, axis=0, keepdims=True)
    dunit = dmixed * gain
    dgated = scale * (dunit - unit * jnp.mean(dunit * unit, axis=1, keepdims=True))
    dscan = dgated * act
    dscan_ref[...] = dscan
    dgate_ref[...] = (dgated * scanned * (sg * (1.0 + gate * (1.0 - sg)))).astype(BF)
    sums_ref[1:2, :] += jnp.sum(dscan * v, axis=0, keepdims=True)
    channel = lax.broadcasted_iota(jnp.int32, (INNER, 128), 0)
    lane = lax.broadcasted_iota(jnp.int32, (INNER, 128), 1)
    heads = jnp.where(channel // 64 == lane, 1.0, 0.0).astype(BF)
    rowsum_ref[...] = dot_split(dscan.astype(BF).astype(F32) * summed, heads)


def middle(index, lengths, summed, v, gate, tokens, out_grad, shards, gain, skip, block=128):
    rows = summed.shape[0]
    wide = pl.BlockSpec((block, INNER), lambda step, index, lens: (step, 0))
    narrow = pl.BlockSpec((block, D), lambda step, index, lens: (step, 0))
    vector = pl.BlockSpec((1, INNER), lambda step, index, lens: (0, 0))
    return pl.pallas_call(
        middle_kernel,
        grid_spec=pltpu.PrefetchScalarGridSpec(
            num_scalar_prefetch=2,
            grid=(rows // block,),
            in_specs=[wide, wide, wide, narrow, narrow, vector, vector]
            + [pl.BlockSpec(s.shape, lambda step, index, lens: (0, 0)) for s in shards],
            out_specs=[
                narrow, wide, narrow, wide, wide,
                pl.BlockSpec((block, 128), lambda step, index, lens: (step, 0)),
                pl.BlockSpec((8, INNER), lambda step, index, lens: (0, 0)),
            ],
            scratch_shapes=[pltpu.VMEM((block, INNER), F32)],
        ),
        out_shape=[
            jax.ShapeDtypeStruct((rows, D), BF),
            jax.ShapeDtypeStruct((rows, INNER), BF),
            jax.ShapeDtypeStruct((rows, D), BF),
            jax.ShapeDtypeStruct((rows, INNER), F32),
            jax.ShapeDtypeStruct((rows, INNER), BF),
            jax.ShapeDtypeStruct((rows, 128), F32),
            jax.ShapeDtypeStruct((8, INNER), F32),
        ],
        compiler_params=pltpu.CompilerParams(
            dimension_semantics=("arbitrary",), vmem_limit_bytes=VMEM_LIMIT
        ),
        name="middle",
    )(index, lengths, summed, v, gate, tokens, out_grad, gain, skip, *shards)


def scan_backward_kernel(
    xv_ref, xbc_ref, raw_ref, tv_ref, tbc_ref, dtb_ref, alog_ref, skip_ref,
    v_ref, bc_ref, step_ref, cum_ref, dscan_ref, rowsum_ref,
    dx_ref, dtaps_ref, dsmall_ref,
    st_ref, dst_ref, cumt_ref, colsum_ref,
):
    group = pl.program_id(1)

    @pl.when(group == 0)
    def _():
        bc = bc_ref[...]
        st_ref[...] = dot_nt(bc[:, :STATE], bc[:, STATE:])
        dst_ref[...] = jnp.zeros_like(dst_ref)
        colsum_ref[...] = jnp.zeros_like(colsum_ref)
        cumt_ref[...] = cum_ref[...].T

    shift = lax.rem(128 - GHEADS * group, 128)
    cum_cols = pltpu.roll(cum_ref[...], shift, axis=1)
    step_cols = pltpu.roll(step_ref[...], shift, axis=1)
    cum_rows = cumt_ref[pl.ds(pl.multiple_of(GHEADS * group, GHEADS), GHEADS), :]
    down, across = tri_masks()
    live = across >= down
    dvs = []
    for pair in range(GHEADS // 2):
        lanes = slice(128 * pair, 128 * pair + 128)
        vp = v_ref[:, lanes]
        dsp = dscan_ref[:, lanes].astype(BF)
        top = jnp.zeros((HALF, 128), F32)
        bottom = jnp.zeros((HALF, 128), F32)
        d00 = dst_ref[:HALF, :HALF]
        d01 = dst_ref[:HALF, HALF:]
        d11 = dst_ref[HALF:, HALF:]
        for side in range(2):
            head = 2 * pair + side
            vm = head_lanes(vp, side == 0)
            dsm = head_lanes(dsp, side == 0)
            ci = cum_rows[head : head + 1, :]
            cj = cum_cols[:, head : head + 1]
            sj = step_cols[:, head : head + 1]
            w00 = jnp.where(live, jnp.exp2(ci[:, :HALF] - cj[:HALF]), 0.0) * sj[:HALF]
            w01 = jnp.exp2(ci[:, HALF:] - cj[:HALF]) * sj[:HALF]
            w11 = jnp.where(live, jnp.exp2(ci[:, HALF:] - cj[HALF:]), 0.0) * sj[HALF:]
            dtop = dot_nt(vm[:HALF], dsp)
            dbottom = dot_nt(vm[HALF:], dsp[HALF:])
            d00 = d00 + dtop[:, :HALF] * w00
            d01 = d01 + dtop[:, HALF:] * w01
            d11 = d11 + dbottom * w11
            m00 = (st_ref[:HALF, :HALF] * w00).astype(BF)
            m01 = (st_ref[:HALF, HALF:] * w01).astype(BF)
            m11 = (st_ref[HALF:, HALF:] * w11).astype(BF)
            top = top + dot(jnp.concatenate([m00, m01], axis=1), dsm)
            bottom = bottom + dot(m11, dsm[HALF:])
        dst_ref[:HALF, :HALF] = d00
        dst_ref[:HALF, HALF:] = d01
        dst_ref[HALF:, HALF:] = d11
        dvs.append(jnp.concatenate([top, bottom], axis=0))
    dv = jnp.concatenate(dvs, axis=1)
    channel = lax.broadcasted_iota(jnp.int32, (GCOLS, 128), 0)
    lane = lax.broadcasted_iota(jnp.int32, (GCOLS, 128), 1)
    heads = jnp.where(channel // 64 + GHEADS * group == lane, 1.0, 0.0).astype(BF)
    colsum_ref[...] += dot_split(v_ref[...].astype(F32) * dv, heads)
    dact = dv + skip_ref[...] * dscan_ref[...]
    columns = pl.ds(pl.multiple_of(GCOLS * group, GCOLS), GCOLS)
    dx = conv_backward(
        xv_ref[...], tv_ref[0:4, :], tv_ref[4:5, :], dact, dtaps_ref, columns
    )
    dx_ref[:, columns] = dx.astype(BF)

    @pl.when(group == GROUPS - 1)
    def _():
        bc = bc_ref[...]
        dst = dst_ref[...].astype(BF)
        db = dot(dst, bc[:, STATE:])
        dc = dot_tn(dst, bc[:, :STATE])
        dbc = conv_backward(
            xbc_ref[...], tbc_ref[0:4, :], tbc_ref[4:5, :],
            jnp.concatenate([db, dc], axis=1), dtaps_ref, slice(INNER, CONVCH),
        )
        dx_ref[:, INNER:CONVCH] = dbc.astype(BF)
        row = lax.broadcasted_iota(jnp.int32, (LEN, LEN), 0)
        col = lax.broadcasted_iota(jnp.int32, (LEN, LEN), 1)
        upper = jnp.where(col >= row, 1.0, 0.0).astype(BF)
        colsum = colsum_ref[...]
        dlog = dot_exact(upper, rowsum_ref[...] - colsum)
        step = step_ref[...]
        rate = jnp.exp(alog_ref[...])
        z = raw_ref[...] + dtb_ref[...]
        sg = 1.0 / (1.0 + jnp.exp(-z))
        tiny = z < -20.0
        ratio = jnp.where(tiny, 1.0, sg / jnp.where(tiny, 1.0, step))
        draw = colsum * ratio - dlog * rate * sg
        lane32 = lax.broadcasted_iota(jnp.int32, (LEN, 128), 1)
        draw = jnp.where(lane32 < HEADS, draw, 0.0)
        dx_ref[:, CONVCH:] = draw.astype(BF)
        dalog = -dlog * step * rate
        dsmall_ref[0] = jnp.concatenate(
            [
                jnp.sum(draw, axis=0, keepdims=True),
                jnp.sum(dalog, axis=0, keepdims=True),
                jnp.zeros((6, 128), F32),
            ],
            axis=0,
        )


def scan_backward(xconv, raw, taps, dtb, alog, skip, v, bc, step, cum, dscan, rowsum, slots):
    rows = slots * LEN
    by_slot = lambda slot, group: (slot, 0)
    fixed = lambda slot, group: (0, 0)
    by_group = pl.BlockSpec((LEN, GCOLS), lambda slot, group: (slot, group))
    last = INNER // (2 * STATE)
    return pl.pallas_call(
        scan_backward_kernel,
        grid=(slots, GROUPS),
        in_specs=[
            by_group,
            pl.BlockSpec((LEN, 2 * STATE), lambda slot, group: (slot, last)),
            pl.BlockSpec((LEN, 128), by_slot),
            pl.BlockSpec((8, GCOLS), lambda slot, group: (0, group)),
            pl.BlockSpec((8, 2 * STATE), lambda slot, group: (0, last)),
            pl.BlockSpec((1, 128), fixed),
            pl.BlockSpec((1, 128), fixed),
            pl.BlockSpec((1, GCOLS), lambda slot, group: (0, group)),
            by_group,
            pl.BlockSpec((LEN, 2 * STATE), by_slot),
            pl.BlockSpec((LEN, 128), by_slot),
            pl.BlockSpec((LEN, 128), by_slot),
            by_group,
            pl.BlockSpec((LEN, 128), by_slot),
        ],
        out_specs=[
            pl.BlockSpec((LEN, CONVCH + 128), by_slot),
            pl.BlockSpec((1, 8, CONVCH), lambda slot, group: (slot, 0, 0)),
            pl.BlockSpec((1, 8, 128), lambda slot, group: (slot, 0, 0)),
        ],
        out_shape=[
            jax.ShapeDtypeStruct((rows, CONVCH + 128), BF),
            jax.ShapeDtypeStruct((slots, 8, CONVCH), F32),
            jax.ShapeDtypeStruct((slots, 8, 128), F32),
        ],
        scratch_shapes=[
            pltpu.VMEM((LEN, LEN), F32),
            pltpu.VMEM((LEN, LEN), F32),
            pltpu.VMEM((128, LEN), F32),
            pltpu.VMEM((LEN, 128), F32),
        ],
        compiler_params=pltpu.CompilerParams(
            dimension_semantics=("arbitrary", "arbitrary"), vmem_limit_bytes=VMEM_LIMIT
        ),
        name="scan_backward",
    )(xconv, xconv, raw, taps, taps, dtb, alog, skip, v, bc, step, cum, dscan, rowsum)


def project_kernel(index_ref, n_ref, own_ref, core_ref, up_ref, down_ref, cup_ref, cdown_ref, out_ref):
    me = index_ref[0]
    part = own_ref.shape[0]

    def columns(k):
        return n_ref[:, pl.ds(pl.multiple_of((me ^ k) * part, part), part)]

    out_ref[...] = (
        dot(columns(0), own_ref[...])
        + dot(columns(1), core_ref[...])
        + dot(columns(2), jnp.concatenate([up_ref[...], down_ref[...]], axis=0))
        + dot(columns(3), jnp.concatenate([cup_ref[...], cdown_ref[...]], axis=0))
    )


def project(index, normed, shards, block):
    rows = normed.shape[0]
    columns = shards[0].shape[1]
    return pl.pallas_call(
        project_kernel,
        grid_spec=pltpu.PrefetchScalarGridSpec(
            num_scalar_prefetch=1,
            grid=(columns // block,),
            in_specs=[pl.BlockSpec(normed.shape, lambda step, index: (0, 0))]
            + [pl.BlockSpec((s.shape[0], block), lambda step, index: (0, step)) for s in shards],
            out_specs=pl.BlockSpec((rows, block), lambda step, index: (0, step)),
        ),
        out_shape=jax.ShapeDtypeStruct((rows, columns), F32),
        compiler_params=pltpu.CompilerParams(
            dimension_semantics=("arbitrary",), vmem_limit_bytes=VMEM_LIMIT
        ),
        name="project",
    )(index, normed, *shards)


def input_grad_kernel(index_ref, tok_ref, do_ref, dgate_ref, dx_ref, gain_ref, wstep_ref, *refs):
    gate_refs, conv_refs = refs[0:6], refs[6:12]
    out_ref, dgain_ref, dn_ref = refs[12:15]
    me = index_ref[0]
    part = gate_refs[0].shape[0]
    dgate = dgate_ref[...]
    dconv = dx_ref[:, :CONVCH]
    draw = dx_ref[:, CONVCH:]

    @pl.when(pl.program_id(0) == 0)
    def _():
        dgain_ref[...] = jnp.zeros_like(dgain_ref)

    def pieces(refs):
        return [
            refs[0][...],
            refs[1][...],
            jnp.concatenate([refs[2][...], refs[3][...]], axis=0),
            jnp.concatenate([refs[4][...], refs[5][...]], axis=0),
        ]

    for k, (wg, wc) in enumerate(zip(pieces(gate_refs), pieces(conv_refs))):
        lanes = pl.ds(pl.multiple_of((me ^ k) * part, part), part)
        dn_ref[:, lanes] = (
            dot_nt(dgate, wg) + dot_nt(dconv, wc) + dot(draw, wstep_ref[:, lanes])
        )
    dn = dn_ref[...]
    x = tok_ref[...].astype(F32)
    scale = lax.rsqrt(jnp.mean(x * x, axis=1, keepdims=True) + 1e-05)
    unit = x * scale
    dgain_ref[0:1, :] += jnp.sum(dn * unit, axis=0, keepdims=True)
    dunit = dn * gain_ref[...]
    out_ref[...] = do_ref[...].astype(F32) + scale * (
        dunit - unit * jnp.mean(dunit * unit, axis=1, keepdims=True)
    )


def input_grad(index, tokens, dout, dgate, dx, gain, wstep_t, gate_shards, conv_shards, block=128):
    rows = tokens.shape[0]
    by_row = lambda v: pl.BlockSpec((block, v.shape[1]), lambda step, index: (step, 0))
    whole = lambda v: pl.BlockSpec(v.shape, lambda step, index: (0, 0))
    shards = list(gate_shards) + list(conv_shards)
    return pl.pallas_call(
        input_grad_kernel,
        grid_spec=pltpu.PrefetchScalarGridSpec(
            num_scalar_prefetch=1,
            grid=(rows // block,),
            in_specs=[by_row(v) for v in (tokens, dout, dgate, dx)]
            + [whole(v) for v in [gain, wstep_t] + shards],
            out_specs=[by_row(tokens), pl.BlockSpec((8, D), lambda step, index: (0, 0))],
            scratch_shapes=[pltpu.VMEM((block, D), F32)],
        ),
        out_shape=[
            jax.ShapeDtypeStruct((rows, D), F32),
            jax.ShapeDtypeStruct((8, D), F32),
        ],
        compiler_params=pltpu.CompilerParams(
            dimension_semantics=("arbitrary",), vmem_limit_bytes=VMEM_LIMIT
        ),
        name="input_grad",
    )(index, tokens, dout, dgate, dx, gain, wstep_t, *shards)


SWAP = [(0, 1), (1, 0)]
RING = 4


def y_shift(by):
    place = lambda y: (y % 2) * 2 + y // 2
    return [(place(y), place((y + by) % 4)) for y in range(4)]


def shift(by):
    return [(i, (i + by) % RING) for i in range(RING)]


def take_shards(shard):
    half = shard.shape[0] // 2
    core = lax.ppermute(shard, "core", SWAP)
    up = lax.ppermute(shard[:half], ("yl", "yh"), y_shift(1))
    down = lax.ppermute(shard[half:], ("yl", "yh"), y_shift(-1))
    cup = lax.ppermute(up, "core", SWAP)
    cdown = lax.ppermute(down, "core", SWAP)
    return (shard, core, up, down, cup, cdown)


def after(values, *others):
    return lax.optimization_barrier((values,) + others)[0]


def scatter_rows(part, axis):
    quarter = part.shape[1] // RING
    me = lax.axis_index(axis)

    def rows(owner):
        return lax.dynamic_slice_in_dim(part, owner * quarter, quarter, axis=1)

    total = rows(me).astype(F32)
    got = [
        lax.ppermute(rows(lax.rem(me + by, RING)), axis, shift(by)) for by in range(1, RING)
    ]
    for piece in got:
        total = total + piece.astype(F32)
    return total.astype(BF)


def gather_rows(part, axis):
    me = lax.axis_index(axis)
    got = [part] + [lax.ppermute(part, axis, shift(by)) for by in range(RING - 1, 0, -1)]
    stacked = jnp.stack(got, axis=0)
    return jnp.roll(stacked, me, axis=0).reshape((-1,) + part.shape[1:])


def sum_y(part):
    yl = lax.axis_index("yl")
    own = lax.dynamic_index_in_dim(part, yl, 0, keepdims=False)
    other = lax.dynamic_index_in_dim(part, 1 - yl, 0, keepdims=False)
    right = lax.ppermute(other, ("yl", "yh"), y_shift(1))
    left = lax.ppermute(other, ("yl", "yh"), y_shift(-1))
    across = lax.ppermute(own, "yh", SWAP)
    f = lambda v: v.astype(F32)
    return ((f(own) + f(across)) + (f(left) + f(right))).astype(BF)


def sum_core(grad):
    core = lax.axis_index("core")
    own = lax.dynamic_index_in_dim(grad, core, 1, keepdims=False)
    other = lax.dynamic_index_in_dim(grad, 1 - core, 1, keepdims=False)
    got = lax.ppermute(other, "core", SWAP)
    return (own.astype(F32) + got.astype(F32)).astype(BF)


def reduce_weight(grad):
    rows = grad.shape[0] // 4
    columns = grad.shape[1]
    cut = (columns // 256) * 128
    half = sum_core(grad.reshape(2, 2, rows, columns))
    outs = []
    for part, axes in ((half[..., :cut], ("x", "z")), (half[..., cut:], ("z", "x"))):
        part = scatter_rows(scatter_rows(part, axes[0]), axes[1])
        part = sum_y(part)
        outs.append(gather_rows(gather_rows(part, axes[1]), axes[0]))
    return jnp.concatenate(outs, axis=1).astype(F32)


def reduce_small(vector):
    total = sum_core(vector.astype(BF).reshape(2, 2, *vector.shape[1:]))
    for axis in ("x", "z"):
        got = [lax.ppermute(total, axis, shift(by)) for by in range(1, RING)]
        f = lambda v: v.astype(F32)
        total = ((f(total) + f(got[1])) + (f(got[0]) + f(got[2]))).astype(BF)
    return sum_y(total).astype(F32)


SMALL = (D // 4, CONV * CONVCH // 4, CONVCH // 4, HEADS // 4, HEADS // 4, HEADS // 4, INNER // 4, D // 4 * HEADS)
SMALL_ROWS = 96


def pack(pieces):
    flat = jnp.concatenate(pieces, axis=-1)
    pad = SMALL_ROWS * 128 - flat.shape[-1]
    flat = jnp.pad(flat, [(0, 0)] * (flat.ndim - 1) + [(0, pad)])
    return flat.reshape(flat.shape[:-1] + (SMALL_ROWS, 128))


def unpack(packed):
    flat = packed.reshape(packed.shape[:-2] + (-1,))
    out, at = [], 0
    for size in SMALL:
        out.append(flat[..., at : at + size])
        at += size
    return out


def local(
    tokens, norm_gain, in_proj, conv_weight, conv_bias, dt_bias, a_log, d_skip, gate_gain,
    out_proj, out_grad, lengths,
):
    slots = lengths.shape[0]
    me = lax.axis_index("yl") * 2 + lax.axis_index("core")
    index = me[None].astype(jnp.int32)

    packed = pack(
        [
            norm_gain, conv_weight.reshape(-1), conv_bias, dt_bias, a_log, d_skip, gate_gain,
            in_proj[:, INNER + CONVCH :].reshape(-1),
        ]
    )
    own, core, up, down, cup, cdown = take_shards(packed)
    relative = jnp.stack(
        [own, core, jnp.concatenate([up, down]), jnp.concatenate([cup, cdown])]
    )
    order = jnp.arange(4) ^ me
    whole = unpack(jnp.take(relative, order, axis=0))
    f = lambda v: v.astype(F32)
    gain = f(whole[0]).reshape(1, D)
    conv_w = f(whole[1]).reshape(4, CONV, CONVCH // 4).transpose(1, 0, 2).reshape(CONV, CONVCH)
    taps = jnp.concatenate(
        [conv_w, f(whole[2]).reshape(1, CONVCH), jnp.zeros((3, CONVCH), F32)], axis=0
    )
    pad = lambda v: jnp.pad(f(v).reshape(1, HEADS), ((0, 0), (0, 128 - HEADS)))
    dtb, alog = pad(whole[3]), pad(whole[4])
    skip = jnp.repeat(f(whole[5]).reshape(HEADS), INNER // HEADS)[None, :]
    gate_gain_all = f(whole[6]).reshape(1, INNER)
    wstep = jnp.pad(whole[7].reshape(D, HEADS), ((0, 0), (0, 128 - HEADS)))

    conv_shards = take_shards(in_proj[:, INNER : INNER + CONVCH])
    gate_shards = take_shards(after(in_proj[:, :INNER], conv_shards[2], conv_shards[3]))
    out_shards = take_shards(after(out_proj, gate_shards[2], gate_shards[3]))

    x = tokens.astype(F32)
    scale = lax.rsqrt(jnp.mean(x * x, axis=1, keepdims=True) + 1e-05)
    normed = lax.optimization_barrier((x * scale * gain).astype(BF))
    raw = dot(normed, wstep)
    xconv = project(index, normed, conv_shards, 768)
    summed, v, bc, step, cum = scan_forward(xconv, raw, taps, dtb, alog, slots)
    gate = project(index, normed, gate_shards, 512)
    block_out, mixed, dout, dscan, dgate, rowsum, sums = middle(
        index, lengths, summed, v, gate, tokens, out_grad, out_shards, gate_gain_all, skip
    )
    g_out = reduce_weight(dot_tn(mixed, dout).astype(BF))
    g_gate = reduce_weight(dot_tn(normed, dgate).astype(BF))
    dx, dtaps, dsmall = scan_backward(
        xconv, raw, taps, dtb, alog, skip, v, bc, step, cum, dscan, rowsum, slots
    )
    d_in = dot_tn(normed, dx)
    g_conv = reduce_weight(d_in[:, :CONVCH].astype(BF))
    tokens_grad, dgain = input_grad(
        index, tokens, dout, dgate, dx, gain, wstep.T, gate_shards, conv_shards
    )
    dtaps = jnp.sum(dtaps, axis=0)
    dsmall = jnp.sum(dsmall, axis=0)
    d_skip = jnp.sum(sums[1].reshape(HEADS, INNER // HEADS), axis=1)
    four = lambda v: v.reshape(4, -1)
    small = reduce_small(
        pack(
            [
                four(dgain[0]),
                dtaps[0:4].reshape(CONV, 4, CONVCH // 4).transpose(1, 0, 2).reshape(4, -1),
                four(dtaps[4]), four(dsmall[0, :HEADS]), four(dsmall[1, :HEADS]), four(d_skip),
                four(sums[0]), four(d_in[:, CONVCH : CONVCH + HEADS]),
            ]
        )
    )
    s_gain, s_taps, s_bias, s_dtb, s_alog, s_skip, s_gate, s_step = unpack(small)
    return (
        block_out,
        tokens_grad,
        s_gain,
        jnp.concatenate([g_gate, g_conv, s_step.reshape(D // 4, HEADS)], axis=1),
        s_taps.reshape(CONV, CONVCH // 4),
        s_bias, s_dtb, s_alog, s_skip, s_gate,
        g_out,
    )


def solution(mesh):
    names = ("yl", "core", "z", "x", "yh")
    fine = Mesh(mesh.devices.reshape(2, 2, 4, 4, 2), names)
    every = P(names, None)
    shard = P(("yl", "core"))
    rows = P(("yl", "core"), None)
    columns = P(None, ("yl", "core"))
    return jax.shard_map(
        local,
        mesh=fine,
        in_specs=(
            every, shard, rows, columns, shard, shard, shard, shard, shard, rows, every, P(names),
        ),
        out_specs=(
            every, every, shard, rows, columns, shard, shard, shard, shard, shard, rows,
        ),
        check_vma=False,
    )
```

```python
import functools
import jax
import jax.numpy as jnp
from jax import lax
from jax.experimental import pallas as pl
from jax.experimental.pallas import tpu as pltpu
from jax.sharding import Mesh, PartitionSpec as P

D = 1024
INNER = 2048
CONV = 4
LEN = 256
HEADS = 32
STATE = 128
CONVCH = 2304
HALF = 128
GROUPS = 4
GCOLS = INNER // GROUPS
GHEADS = HEADS // GROUPS
BF = jnp.bfloat16
F32 = jnp.float32
LOG2E = 1.4426950408889634
VMEM_LIMIT = 56 * 1024 * 1024


def cost(us):
    return pl.CostEstimate(
        flops=int(us * 1.0e9), transcendentals=0, bytes_accessed=int(us * 3.3e6)
    )


def dot(a, b):
    return lax.dot_general(a, b, (((1,), (0,)), ((), ())), preferred_element_type=F32)


def dot_nt(a, b):
    return lax.dot_general(a, b, (((1,), (1,)), ((), ())), preferred_element_type=F32)


def dot_tn(a, b):
    return lax.dot_general(a, b, (((0,), (0,)), ((), ())), preferred_element_type=F32)


def dot_exact(ones, v):
    hi = v.astype(BF)
    rest = v - hi.astype(F32)
    mid = rest.astype(BF)
    low = (rest - mid.astype(F32)).astype(BF)
    return dot(ones, hi) + dot(ones, mid) + dot(ones, low)


def dot_split(v, ones):
    hi = v.astype(BF)
    low = (v - hi.astype(F32)).astype(BF)
    return dot(hi, ones) + dot(low, ones)


def sigmoid(v):
    return 0.5 * jnp.tanh(0.5 * v) + 0.5


def rows_down(v, count):
    row = lax.broadcasted_iota(jnp.int32, v.shape, 0)
    return jnp.where(row >= count, pltpu.roll(v, count, axis=0), 0.0)


def rows_up(v, count):
    rows = v.shape[0]
    row = lax.broadcasted_iota(jnp.int32, v.shape, 0)
    return jnp.where(row < rows - count, pltpu.roll(v, rows - count, axis=0), 0.0)


def conv_forward(x, taps, bias):
    total = bias + taps[3:4] * x
    for back in range(1, CONV):
        total = total + taps[3 - back : 4 - back] * rows_down(x, back)
    return total


def conv_backward(x, taps, bias, dact, dtaps_ref, columns):
    v = conv_forward(x, taps, bias)
    sg = sigmoid(v)
    dv = dact * (sg * (1.0 + v * (1.0 - sg)))
    dx = taps[3:4] * dv
    sums = [jnp.sum(dv * x, axis=0, keepdims=True)]
    for back in range(1, CONV):
        dx = dx + taps[3 - back : 4 - back] * rows_up(dv, back)
        sums.insert(0, jnp.sum(dv * rows_down(x, back), axis=0, keepdims=True))
    sums.append(jnp.sum(dv, axis=0, keepdims=True))
    sums.append(jnp.zeros((3, x.shape[1]), F32))
    dtaps_ref[0, :, columns] = jnp.concatenate(sums, axis=0)
    return dx


def step_of(raw, bias):
    z = raw + bias
    return jnp.maximum(z, 0.0) + jnp.log1p(jnp.exp(-jnp.abs(z)))


def tri_masks():
    down = lax.broadcasted_iota(jnp.int32, (HALF, HALF), 0)
    across = lax.broadcasted_iota(jnp.int32, (HALF, HALF), 1)
    return down, across


def head_lanes(v, first):
    lane = lax.broadcasted_iota(jnp.int32, v.shape, 1)
    zero = jnp.zeros_like(v)
    return jnp.where(lane < 64, v, zero) if first else jnp.where(lane < 64, zero, v)


def scan_forward_kernel(
    xv_ref, xbc_ref, raw_ref, tv_ref, tbc_ref, dtb_ref, alog_ref,
    summed_ref, v_ref, bc_ref, step_ref, cum_ref,
    s_ref, cumt_ref, stept_ref,
):
    group = pl.program_id(1)

    @pl.when(group == 0)
    def _():
        act = conv_forward(xbc_ref[...], tbc_ref[0:4, :], tbc_ref[4:5, :])
        bc = (act * sigmoid(act)).astype(BF)
        bc_ref[...] = bc
        s_ref[...] = dot_nt(bc[:, STATE:], bc[:, :STATE])
        step = step_of(raw_ref[...], dtb_ref[...])
        logdecay = -step * jnp.exp(alog_ref[...])
        row = lax.broadcasted_iota(jnp.int32, (LEN, LEN), 0)
        col = lax.broadcasted_iota(jnp.int32, (LEN, LEN), 1)
        lower = jnp.where(row >= col, 1.0, 0.0).astype(BF)
        cum = dot_exact(lower, logdecay) * LOG2E
        step_ref[...] = step
        cum_ref[...] = cum
        cumt_ref[...] = cum.T
        stept_ref[...] = step.T

    act = conv_forward(xv_ref[...], tv_ref[0:4, :], tv_ref[4:5, :])
    v_ref[...] = (act * sigmoid(act)).astype(BF)
    cols = pltpu.roll(cum_ref[...], lax.rem(128 - GHEADS * group, 128), axis=1)
    first = pl.multiple_of(GHEADS * group, GHEADS)
    cum_rows = cumt_ref[pl.ds(first, GHEADS), :]
    step_rows = stept_ref[pl.ds(first, GHEADS), :]
    down, across = tri_masks()
    live = down >= across
    for pair in range(GHEADS // 2):
        lanes = slice(128 * pair, 128 * pair + 128)
        vp = v_ref[:, lanes]
        top = jnp.zeros((HALF, 128), F32)
        bottom = jnp.zeros((HALF, 128), F32)
        for side in range(2):
            head = 2 * pair + side
            vm = head_lanes(vp, side == 0)
            ci = cols[:, head : head + 1]
            cj = cum_rows[head : head + 1, :]
            sj = step_rows[head : head + 1, :]
            w00 = jnp.where(live, jnp.exp2(ci[:HALF] - cj[:, :HALF]), 0.0) * sj[:, :HALF]
            w10 = jnp.exp2(ci[HALF:] - cj[:, :HALF]) * sj[:, :HALF]
            w11 = jnp.where(live, jnp.exp2(ci[HALF:] - cj[:, HALF:]), 0.0) * sj[:, HALF:]
            m00 = (s_ref[:HALF, :HALF] * w00).astype(BF)
            m10 = (s_ref[HALF:, :HALF] * w10).astype(BF)
            m11 = (s_ref[HALF:, HALF:] * w11).astype(BF)
            top = top + dot(m00, vm[:HALF])
            bottom = bottom + dot(jnp.concatenate([m10, m11], axis=1), vm)
        summed_ref[:HALF, lanes] = top
        summed_ref[HALF:, lanes] = bottom


def scan_forward(xconv, raw, taps, dtb, alog, slots):
    rows = slots * LEN
    by_slot = lambda slot, group: (slot, 0)
    fixed = lambda slot, group: (0, 0)
    return pl.pallas_call(
        scan_forward_kernel,
        grid=(slots, GROUPS),
        in_specs=[
            pl.BlockSpec((LEN, GCOLS), lambda slot, group: (slot, group)),
            pl.BlockSpec((LEN, 2 * STATE), lambda slot, group: (slot, INNER // (2 * STATE))),
            pl.BlockSpec((LEN, 128), by_slot),
            pl.BlockSpec((8, GCOLS), lambda slot, group: (0, group)),
            pl.BlockSpec((8, 2 * STATE), lambda slot, group: (0, INNER // (2 * STATE))),
            pl.BlockSpec((1, 128), fixed),
            pl.BlockSpec((1, 128), fixed),
        ],
        out_specs=[
            pl.BlockSpec((LEN, GCOLS), lambda slot, group: (slot, group)),
            pl.BlockSpec((LEN, GCOLS), lambda slot, group: (slot, group)),
            pl.BlockSpec((LEN, 2 * STATE), by_slot),
            pl.BlockSpec((LEN, 128), by_slot),
            pl.BlockSpec((LEN, 128), by_slot),
        ],
        out_shape=[
            jax.ShapeDtypeStruct((rows, INNER), F32),
            jax.ShapeDtypeStruct((rows, INNER), BF),
            jax.ShapeDtypeStruct((rows, 2 * STATE), BF),
            jax.ShapeDtypeStruct((rows, 128), F32),
            jax.ShapeDtypeStruct((rows, 128), F32),
        ],
        scratch_shapes=[
            pltpu.VMEM((LEN, LEN), F32),
            pltpu.VMEM((128, LEN), F32),
            pltpu.VMEM((128, LEN), F32),
        ],
        compiler_params=pltpu.CompilerParams(
            dimension_semantics=("arbitrary", "arbitrary"), vmem_limit_bytes=VMEM_LIMIT
        ),
        name="scan_forward",
        cost_estimate=cost(12),
    )(xconv, xconv, raw, taps, taps, dtb, alog)


STRIP = 16
CHUNK = 512


def middle_kernel(
    index_ref, len_ref, summed_ref, v_ref, gate_ref, tok_ref, og_ref, gain_ref, skip_ref, *refs
):
    shards = refs[0:6]
    out_ref, m_ref, do_ref, dscan_ref, dgate_ref, rowsum_ref, sums_ref = refs[6:13]
    wo_ref, unit_ref, dm_ref, scale_ref, high_ref, low_ref, sems = refs[13:]
    step = pl.program_id(0)
    block = summed_ref.shape[0]
    per_slot = LEN // block
    count = len_ref[step // per_slot]
    row = lax.broadcasted_iota(jnp.int32, (block, 1), 0) + lax.rem(step, per_slot) * block
    live = row < count
    chunks = [slice(at, at + CHUNK) for at in range(0, INNER, CHUNK)]
    copies = shard_copies(index_ref[0], shards, wo_ref, sems, 0)

    @pl.when(step == 0)
    def _():
        sums_ref[...] = jnp.zeros_like(sums_ref)
        for copy in copies:
            copy.start()

    def fold(v):
        return sum(v[:, at : at + 128] for at in range(0, CHUNK, 128))

    def forward(at, carry):
        rows = pl.ds(pl.multiple_of(at * STRIP, STRIP), STRIP)
        total = jnp.zeros((STRIP, 128), F32)
        for c in chunks:
            scanned = summed_ref[rows, c] + skip_ref[:, c] * v_ref[rows, c].astype(F32)
            gate = gate_ref[rows, c]
            gated = scanned * (gate * sigmoid(gate))
            unit_ref[rows, c] = gated
            total = total + fold(gated * gated)
        scale = lax.rsqrt(jnp.sum(total, axis=1, keepdims=True) * (1.0 / INNER) + 1e-05)
        scale_ref[rows, :] = jnp.broadcast_to(scale, (STRIP, 128))
        for c in chunks:
            unit = unit_ref[rows, c] * scale
            unit_ref[rows, c] = unit
            m_ref[rows, c] = (unit * gain_ref[:, c]).astype(BF)
        return carry

    lax.fori_loop(0, block // STRIP, forward, 0)
    dout = jnp.where(live, og_ref[...].astype(F32), 0.0).astype(BF)
    do_ref[...] = dout

    @pl.when(step == 0)
    def _():
        for copy in copies:
            copy.wait()

    result = tok_ref[...].astype(F32) + dot(m_ref[...], wo_ref[...])
    out_ref[...] = jnp.where(live, result, 0.0).astype(BF)
    dm_ref[...] = dot_nt(dout, wo_ref[...])

    def backward(at, carry):
        rows = pl.ds(pl.multiple_of(at * STRIP, STRIP), STRIP)
        total = jnp.zeros((STRIP, 128), F32)
        for c in chunks:
            unit = unit_ref[rows, c]
            grown = dm_ref[rows, c] * unit
            sums_ref[0:8, c] += grown[0:8] + grown[8:16]
            total = total + fold(grown * gain_ref[:, c])
        mean = jnp.sum(total, axis=1, keepdims=True) * (1.0 / INNER)
        scale = scale_ref[rows, 0:1]
        for c in chunks:
            dgated = scale * (dm_ref[rows, c] * gain_ref[:, c] - unit_ref[rows, c] * mean)
            summed = summed_ref[rows, c]
            v = v_ref[rows, c].astype(F32)
            gate = gate_ref[rows, c]
            sg = sigmoid(gate)
            act = gate * sg
            dscan = dgated * act
            dscan_ref[rows, c] = dscan
            scanned = summed + skip_ref[:, c] * v
            dgate_ref[rows, c] = (dgated * scanned * (sg + act * (1.0 - sg))).astype(BF)
            skipped = dscan * v
            sums_ref[8:16, c] += skipped[0:8] + skipped[8:16]
            product = dscan.astype(BF).astype(F32) * summed
            high = product.astype(BF)
            high_ref[rows, c] = high
            low_ref[rows, c] = (product - high.astype(F32)).astype(BF)
        return carry

    lax.fori_loop(0, block // STRIP, backward, 0)
    channel = lax.broadcasted_iota(jnp.int32, (INNER, 128), 0)
    lane = lax.broadcasted_iota(jnp.int32, (INNER, 128), 1)
    heads = jnp.where(channel // 64 == lane, 1.0, 0.0).astype(BF)
    rowsum_ref[...] = dot(high_ref[...], heads) + dot(low_ref[...], heads)


def middle(index, lengths, summed, v, gate, tokens, out_grad, shards, gain, skip, block=256):
    rows = summed.shape[0]
    wide = pl.BlockSpec((block, INNER), lambda step, index, lens: (step, 0))
    narrow = pl.BlockSpec((block, D), lambda step, index, lens: (step, 0))
    vector = pl.BlockSpec((1, INNER), lambda step, index, lens: (0, 0))
    return pl.pallas_call(
        middle_kernel,
        grid_spec=pltpu.PrefetchScalarGridSpec(
            num_scalar_prefetch=2,
            grid=(rows // block,),
            in_specs=[wide, wide, wide, narrow, narrow, vector, vector]
            + [pl.BlockSpec(memory_space=pl.ANY) for _ in shards],
            out_specs=[
                narrow, wide, narrow, wide, wide,
                pl.BlockSpec((block, 128), lambda step, index, lens: (step, 0)),
                pl.BlockSpec((16, INNER), lambda step, index, lens: (0, 0)),
            ],
            scratch_shapes=[
                pltpu.VMEM((INNER, D), BF),
                pltpu.VMEM((block, INNER), F32),
                pltpu.VMEM((block, INNER), F32),
                pltpu.VMEM((block, 128), F32),
                pltpu.VMEM((block, INNER), BF),
                pltpu.VMEM((block, INNER), BF),
                pltpu.SemaphoreType.DMA((6,)),
            ],
        ),
        out_shape=[
            jax.ShapeDtypeStruct((rows, D), BF),
            jax.ShapeDtypeStruct((rows, INNER), BF),
            jax.ShapeDtypeStruct((rows, D), BF),
            jax.ShapeDtypeStruct((rows, INNER), F32),
            jax.ShapeDtypeStruct((rows, INNER), BF),
            jax.ShapeDtypeStruct((rows, 128), F32),
            jax.ShapeDtypeStruct((16, INNER), F32),
        ],
        compiler_params=pltpu.CompilerParams(
            dimension_semantics=("arbitrary",), vmem_limit_bytes=VMEM_LIMIT
        ),
        name="middle",
        cost_estimate=cost(15),
    )(index, lengths, summed, v, gate, tokens, out_grad, gain, skip, *shards)


def scan_backward_kernel(
    xv_ref, xbc_ref, raw_ref, tv_ref, tbc_ref, dtb_ref, alog_ref, skip_ref,
    v_ref, bc_ref, step_ref, cum_ref, dscan_ref, rowsum_ref,
    dx_ref, dtaps_ref, dsmall_ref,
    st_ref, dst_ref, cumt_ref, colsum_ref,
):
    group = pl.program_id(1)

    @pl.when(group == 0)
    def _():
        bc = bc_ref[...]
        st_ref[...] = dot_nt(bc[:, :STATE], bc[:, STATE:])
        dst_ref[...] = jnp.zeros_like(dst_ref)
        colsum_ref[...] = jnp.zeros_like(colsum_ref)
        cumt_ref[...] = cum_ref[...].T

    shift = lax.rem(128 - GHEADS * group, 128)
    cum_cols = pltpu.roll(cum_ref[...], shift, axis=1)
    step_cols = pltpu.roll(step_ref[...], shift, axis=1)
    cum_rows = cumt_ref[pl.ds(pl.multiple_of(GHEADS * group, GHEADS), GHEADS), :]
    down, across = tri_masks()
    live = across >= down
    dvs = []
    for pair in range(GHEADS // 2):
        lanes = slice(128 * pair, 128 * pair + 128)
        vp = v_ref[:, lanes]
        dsp = dscan_ref[:, lanes].astype(BF)
        top = jnp.zeros((HALF, 128), F32)
        bottom = jnp.zeros((HALF, 128), F32)
        d00 = dst_ref[:HALF, :HALF]
        d01 = dst_ref[:HALF, HALF:]
        d11 = dst_ref[HALF:, HALF:]
        for side in range(2):
            head = 2 * pair + side
            vm = head_lanes(vp, side == 0)
            dsm = head_lanes(dsp, side == 0)
            ci = cum_rows[head : head + 1, :]
            cj = cum_cols[:, head : head + 1]
            sj = step_cols[:, head : head + 1]
            w00 = jnp.where(live, jnp.exp2(ci[:, :HALF] - cj[:HALF]), 0.0) * sj[:HALF]
            w01 = jnp.exp2(ci[:, HALF:] - cj[:HALF]) * sj[:HALF]
            w11 = jnp.where(live, jnp.exp2(ci[:, HALF:] - cj[HALF:]), 0.0) * sj[HALF:]
            dtop = dot_nt(vm[:HALF], dsp)
            dbottom = dot_nt(vm[HALF:], dsp[HALF:])
            d00 = d00 + dtop[:, :HALF] * w00
            d01 = d01 + dtop[:, HALF:] * w01
            d11 = d11 + dbottom * w11
            m00 = (st_ref[:HALF, :HALF] * w00).astype(BF)
            m01 = (st_ref[:HALF, HALF:] * w01).astype(BF)
            m11 = (st_ref[HALF:, HALF:] * w11).astype(BF)
            top = top + dot(jnp.concatenate([m00, m01], axis=1), dsm)
            bottom = bottom + dot(m11, dsm[HALF:])
        dst_ref[:HALF, :HALF] = d00
        dst_ref[:HALF, HALF:] = d01
        dst_ref[HALF:, HALF:] = d11
        dvs.append(jnp.concatenate([top, bottom], axis=0))
    dv = jnp.concatenate(dvs, axis=1)
    channel = lax.broadcasted_iota(jnp.int32, (GCOLS, 128), 0)
    lane = lax.broadcasted_iota(jnp.int32, (GCOLS, 128), 1)
    heads = jnp.where(channel // 64 + GHEADS * group == lane, 1.0, 0.0).astype(BF)
    colsum_ref[...] += dot_split(v_ref[...].astype(F32) * dv, heads)
    dact = dv + skip_ref[...] * dscan_ref[...]
    columns = pl.ds(pl.multiple_of(GCOLS * group, GCOLS), GCOLS)
    dx = conv_backward(
        xv_ref[...], tv_ref[0:4, :], tv_ref[4:5, :], dact, dtaps_ref, columns
    )
    dx_ref[:, columns] = dx.astype(BF)

    @pl.when(group == GROUPS - 1)
    def _():
        bc = bc_ref[...]
        dst = dst_ref[...].astype(BF)
        db = dot(dst, bc[:, STATE:])
        dc = dot_tn(dst, bc[:, :STATE])
        dbc = conv_backward(
            xbc_ref[...], tbc_ref[0:4, :], tbc_ref[4:5, :],
            jnp.concatenate([db, dc], axis=1), dtaps_ref, slice(INNER, CONVCH),
        )
        dx_ref[:, INNER:CONVCH] = dbc.astype(BF)
        row = lax.broadcasted_iota(jnp.int32, (LEN, LEN), 0)
        col = lax.broadcasted_iota(jnp.int32, (LEN, LEN), 1)
        upper = jnp.where(col >= row, 1.0, 0.0).astype(BF)
        colsum = colsum_ref[...]
        dlog = dot_exact(upper, rowsum_ref[...] - colsum)
        step = step_ref[...]
        rate = jnp.exp(alog_ref[...])
        z = raw_ref[...] + dtb_ref[...]
        sg = 1.0 / (1.0 + jnp.exp(-z))
        tiny = z < -20.0
        ratio = jnp.where(tiny, 1.0, sg / jnp.where(tiny, 1.0, step))
        draw = colsum * ratio - dlog * rate * sg
        lane32 = lax.broadcasted_iota(jnp.int32, (LEN, 128), 1)
        draw = jnp.where(lane32 < HEADS, draw, 0.0)
        dx_ref[:, CONVCH:] = draw.astype(BF)
        dalog = -dlog * step * rate
        dsmall_ref[0] = jnp.concatenate(
            [
                jnp.sum(draw, axis=0, keepdims=True),
                jnp.sum(dalog, axis=0, keepdims=True),
                jnp.zeros((6, 128), F32),
            ],
            axis=0,
        )


def scan_backward(xconv, raw, taps, dtb, alog, skip, v, bc, step, cum, dscan, rowsum, slots):
    rows = slots * LEN
    by_slot = lambda slot, group: (slot, 0)
    fixed = lambda slot, group: (0, 0)
    by_group = pl.BlockSpec((LEN, GCOLS), lambda slot, group: (slot, group))
    last = INNER // (2 * STATE)
    return pl.pallas_call(
        scan_backward_kernel,
        grid=(slots, GROUPS),
        in_specs=[
            by_group,
            pl.BlockSpec((LEN, 2 * STATE), lambda slot, group: (slot, last)),
            pl.BlockSpec((LEN, 128), by_slot),
            pl.BlockSpec((8, GCOLS), lambda slot, group: (0, group)),
            pl.BlockSpec((8, 2 * STATE), lambda slot, group: (0, last)),
            pl.BlockSpec((1, 128), fixed),
            pl.BlockSpec((1, 128), fixed),
            pl.BlockSpec((1, GCOLS), lambda slot, group: (0, group)),
            by_group,
            pl.BlockSpec((LEN, 2 * STATE), by_slot),
            pl.BlockSpec((LEN, 128), by_slot),
            pl.BlockSpec((LEN, 128), by_slot),
            by_group,
            pl.BlockSpec((LEN, 128), by_slot),
        ],
        out_specs=[
            pl.BlockSpec((LEN, CONVCH + 128), by_slot),
            pl.BlockSpec((1, 8, CONVCH), lambda slot, group: (slot, 0, 0)),
            pl.BlockSpec((1, 8, 128), lambda slot, group: (slot, 0, 0)),
        ],
        out_shape=[
            jax.ShapeDtypeStruct((rows, CONVCH + 128), BF),
            jax.ShapeDtypeStruct((slots, 8, CONVCH), F32),
            jax.ShapeDtypeStruct((slots, 8, 128), F32),
        ],
        scratch_shapes=[
            pltpu.VMEM((LEN, LEN), F32),
            pltpu.VMEM((LEN, LEN), F32),
            pltpu.VMEM((128, LEN), F32),
            pltpu.VMEM((LEN, 128), F32),
        ],
        compiler_params=pltpu.CompilerParams(
            dimension_semantics=("arbitrary", "arbitrary"), vmem_limit_bytes=VMEM_LIMIT
        ),
        name="scan_backward",
        cost_estimate=cost(2),
    )(xconv, xconv, raw, taps, taps, dtb, alog, skip, v, bc, step, cum, dscan, rowsum)


def shard_copies(me, shards, whole, sems, axis, first=0, high=None):
    part = shards[0].shape[axis]
    half = part // 2
    copies = []
    for i, (src, k, at) in enumerate(
        zip(shards, (0, 1, 2, 2, 3, 3), (0, 0, 0, half, 0, half))
    ):
        place = pl.ds(pl.multiple_of((me ^ k) * part + at, half), src.shape[axis])
        if axis == 1:
            rows = pl.ds(first, src.shape[0] if high is None else high)
            copies.append(
                pltpu.make_async_copy(src.at[rows, :], whole.at[rows, place], sems.at[i])
            )
        else:
            copies.append(pltpu.make_async_copy(src, whole.at[place, :], sems.at[i]))
    return copies


def project_kernel(columns, block, tail, index_ref, n_ref, *refs):
    shards, (out_ref, *rest), (whole_ref, sems) = refs[0:6], refs[6:-2], refs[-2:]
    me = index_ref[0]
    step = pl.program_id(0)
    steps = columns // block

    def copies(at):
        return shard_copies(me, shards, whole_ref, sems.at[at], 1, at * block, block)

    @pl.when(step == 0)
    def _():
        if tail:
            whole_ref[columns:, :] = jnp.zeros((whole_ref.shape[0] - columns, D), BF)
            last = shard_copies(me, shards, whole_ref, sems.at[steps], 1, columns, HEADS)
            for copy in last:
                copy.start()
        for at in range(steps):
            for copy in copies(at):
                copy.start()
        if tail:
            for copy in last:
                copy.wait()
            rest[0][...] = dot_nt(n_ref[...], whole_ref[columns:, :])

    for at in range(steps):

        @pl.when(step == at)
        def _(at=at):
            for copy in copies(at):
                copy.wait()
            out_ref[...] = dot_nt(n_ref[...], whole_ref[at * block : (at + 1) * block, :])


def project(index, normed, shards, columns, block, tail):
    rows = normed.shape[0]
    out_specs = [pl.BlockSpec((rows, block), lambda step, index: (0, step))]
    out_shape = [jax.ShapeDtypeStruct((rows, columns), F32)]
    if tail:
        out_specs.append(pl.BlockSpec((rows, 128), lambda step, index: (0, 0)))
        out_shape.append(jax.ShapeDtypeStruct((rows, 128), F32))
    steps = columns // block
    return pl.pallas_call(
        functools.partial(project_kernel, columns, block, tail),
        grid_spec=pltpu.PrefetchScalarGridSpec(
            num_scalar_prefetch=1,
            grid=(steps,),
            in_specs=[pl.BlockSpec(normed.shape, lambda step, index: (0, 0))]
            + [pl.BlockSpec(memory_space=pl.ANY) for _ in shards],
            out_specs=out_specs,
            scratch_shapes=[
                pltpu.VMEM((columns + 128 if tail else columns, D), BF),
                pltpu.SemaphoreType.DMA((steps + 1 if tail else steps, 6)),
            ],
        ),
        out_shape=out_shape,
        compiler_params=pltpu.CompilerParams(
            dimension_semantics=("arbitrary",), vmem_limit_bytes=VMEM_LIMIT
        ),
        name="project",
        cost_estimate=cost(7),
    )(index, normed, *shards)


def input_grad_kernel(index_ref, tok_ref, do_ref, dgate_ref, dx_ref, gain_ref, *refs):
    out_ref, dgain_ref, dn_ref, gate_ref, conv_ref, sems = refs[12:]
    me = index_ref[0]
    gate_copies = shard_copies(me, refs[0:6], gate_ref, sems.at[0], 1)
    conv_copies = shard_copies(me, refs[6:12], conv_ref, sems.at[1], 1)
    for copy in gate_copies + conv_copies:
        copy.start()
    live = CONVCH + HEADS
    conv_ref[live:, :] = jnp.zeros((conv_ref.shape[0] - live, D), BF)
    for copy in gate_copies:
        copy.wait()
    dn_ref[...] = dot(dgate_ref[...], gate_ref[...])
    for copy in conv_copies:
        copy.wait()
    dn_ref[...] += dot(dx_ref[...], conv_ref[...])
    strip = 32

    def finish(at, dgain):
        rows = pl.ds(pl.multiple_of(at * strip, strip), strip)
        dn = dn_ref[rows, :]
        x = tok_ref[rows, :].astype(F32)
        scale = lax.rsqrt(jnp.mean(x * x, axis=1, keepdims=True) + 1e-05)
        unit = x * scale
        grown = dn * unit
        dunit = dn * gain_ref[...]
        out_ref[rows, :] = do_ref[rows, :].astype(F32) + scale * (
            dunit - unit * jnp.mean(dunit * unit, axis=1, keepdims=True)
        )
        return dgain + grown.reshape(strip // 8, 8, D).sum(axis=0)

    dgain = lax.fori_loop(0, tok_ref.shape[0] // strip, finish, jnp.zeros((8, D), F32))
    dgain_ref[...] = dgain


def input_grad(index, tokens, dout, dgate, dx, gain, gate_shards, conv_shards):
    rows = tokens.shape[0]
    whole = lambda v: pl.BlockSpec(v.shape, lambda step, index: (0, 0))
    shards = list(gate_shards) + list(conv_shards)
    return pl.pallas_call(
        input_grad_kernel,
        grid_spec=pltpu.PrefetchScalarGridSpec(
            num_scalar_prefetch=1,
            grid=(1,),
            in_specs=[whole(v) for v in (tokens, dout, dgate, dx, gain)]
            + [pl.BlockSpec(memory_space=pl.ANY) for _ in shards],
            out_specs=[
                pl.BlockSpec((rows, D), lambda step, index: (0, 0)),
                pl.BlockSpec((8, D), lambda step, index: (0, 0)),
            ],
            scratch_shapes=[
                pltpu.VMEM((rows, D), F32),
                pltpu.VMEM((INNER, D), BF),
                pltpu.VMEM((CONVCH + 128, D), BF),
                pltpu.SemaphoreType.DMA((2, 6)),
            ],
        ),
        out_shape=[
            jax.ShapeDtypeStruct((rows, D), F32),
            jax.ShapeDtypeStruct((8, D), F32),
        ],
        compiler_params=pltpu.CompilerParams(
            dimension_semantics=("arbitrary",), vmem_limit_bytes=VMEM_LIMIT
        ),
        name="input_grad",
        cost_estimate=cost(2),
    )(index, tokens, dout, dgate, dx, gain, *shards)


SWAP = [(0, 1), (1, 0)]


def y_shift(by):
    place = lambda y: (y % 2) * 2 + y // 2
    return [(place(y), place((y + by) % 4)) for y in range(4)]


def take_shards(shard, axis):
    half = shard.shape[axis] // 2
    first = lax.slice_in_dim(shard, 0, half, axis=axis)
    second = lax.slice_in_dim(shard, half, 2 * half, axis=axis)
    up = lax.ppermute(first, ("yl", "yh"), y_shift(1))
    down = lax.ppermute(second, ("yl", "yh"), y_shift(-1))
    core = lax.ppermute(shard, "core", SWAP)
    return (shard, core, up, down)


def take_rest(shards):
    cup = lax.ppermute(shards[2], "core", SWAP)
    cdown = lax.ppermute(shards[3], "core", SWAP)
    return shards + (cup, cdown)


def after(values, *others):
    return lax.optimization_barrier((values,) + others)[0]


def swap_core(blocks, axis):
    core = lax.axis_index("core")
    own = lax.dynamic_index_in_dim(blocks, core, axis, keepdims=False)
    other = lax.dynamic_index_in_dim(blocks, 1 - core, axis, keepdims=False)
    got = lax.ppermute(other, "core", SWAP)
    return (own.astype(F32) + got.astype(F32)).astype(BF)


def sum_core_lanes(grad):
    core = lax.axis_index("core")

    def pair(which):
        return jnp.stack(
            [
                lax.dynamic_slice_in_dim(grad, (2 * yl + which) * 256, 256, axis=1)
                for yl in range(2)
            ]
        )

    got = lax.ppermute(pair(1 - core), "core", SWAP)
    return (pair(core).astype(F32) + got.astype(F32)).astype(BF)


def exchange(half):
    got = lax.all_to_all(half, ("yl", "z", "x", "yh"), 0, 0, tiled=True)
    return jnp.sum(got.astype(F32), axis=0).astype(BF)


def spread_rows(rows):
    copies = jnp.broadcast_to(rows[None], (32,) + rows.shape)
    return lax.all_to_all(copies, ("z", "x", "yh"), 0, 0, tiled=True)


def lay_out(norm_gain, conv_weight, conv_bias, dt_bias, a_log, d_skip, gate_gain):
    quarter = CONVCH // 4
    wide = lambda v: jnp.pad(v, (0, quarter - v.shape[0]))[None, :]
    mixed = jnp.concatenate([norm_gain, dt_bias, a_log, d_skip])
    return jnp.concatenate(
        [conv_weight, conv_bias[None, :], wide(gate_gain), wide(mixed), jnp.zeros((1, quarter), conv_weight.dtype)],
        axis=0,
    )


def local(
    tokens, norm_gain, in_proj, conv_weight, conv_bias, dt_bias, a_log, d_skip, gate_gain,
    out_proj, out_grad, lengths,
):
    slots = lengths.shape[0]
    quarter = CONVCH // 4
    me = lax.axis_index("yl") * 2 + lax.axis_index("core")
    index = me[None].astype(jnp.int32)

    w_in = in_proj.T
    conv_shards = take_rest(take_shards(w_in[INNER:], 1))
    small = lay_out(norm_gain, conv_weight, conv_bias, dt_bias, a_log, d_skip, gate_gain)
    own = small
    core = lax.ppermute(own, "core", SWAP)
    other = lax.ppermute(own, "yl", SWAP)
    both = lax.ppermute(other, "core", SWAP)
    natural = jnp.take(jnp.stack([own, core, other, both]), jnp.arange(4) ^ me, axis=0)
    natural = lax.optimization_barrier(natural.astype(F32))
    taps = natural.transpose(1, 0, 2).reshape(8, CONVCH)
    gate_gain_all = natural[:, 5, : INNER // 4].reshape(1, INNER)
    gain = natural[:, 6, : D // 4].reshape(1, D)
    heads = natural[:, 6, D // 4 : D // 4 + 24].reshape(4, 3, 8).transpose(1, 0, 2).reshape(3, HEADS)
    skip = jnp.repeat(heads[2], INNER // HEADS)[None, :]
    heads = jnp.pad(heads, ((0, 0), (0, 128 - HEADS)))
    dtb, alog = heads[0:1], heads[1:2]

    x = tokens.astype(F32)
    scale = lax.rsqrt(jnp.mean(x * x, axis=1, keepdims=True) + 1e-05)
    normed = lax.optimization_barrier((x * scale * gain).astype(BF))
    gate_shards = take_shards(after(w_in[:INNER], conv_shards[2], conv_shards[3]), 1)
    xconv, raw = project(index, normed, conv_shards, CONVCH, 768, True)
    gate_shards = take_rest(lax.optimization_barrier(gate_shards + (raw,))[:4])
    out_shards = take_shards(after(out_proj, raw), 0)
    summed, v, bc, step, cum = scan_forward(xconv, raw, taps, dtb, alog, slots)
    out_shards = take_rest(lax.optimization_barrier(out_shards + (summed,))[:4])
    gate = project(index, normed, gate_shards, INNER, 512, False)[0]
    block_out, mixed, dout, dscan, dgate, rowsum, sums = middle(
        index, lengths, summed, v, gate, tokens, out_grad, out_shards, gate_gain_all, skip, 256
    )
    d_out = dot_tn(mixed, dout).astype(BF)
    h_out = swap_core(d_out.reshape(2, 2, INNER // 4, D), 1).reshape(64, INNER // 128, D)
    d_gate = dot_tn(dgate, after(normed, d_out)).astype(BF)
    h_gate = sum_core_lanes(d_gate).reshape(64, INNER // 32, D // 4)
    h_early = jnp.concatenate([h_out[..., 256 * j : 256 * j + 256] for j in range(4)] + [h_gate], axis=1)
    r_early = exchange(h_early)
    dx, dtaps, dsmall = scan_backward(
        xconv, raw, taps, dtb, alog, skip, v, bc, step, cum, after(dscan, h_early), rowsum, slots
    )
    d_in = dot_tn(dx, normed).astype(BF)
    h_conv = sum_core_lanes(d_in[:CONVCH]).reshape(64, CONVCH // 32, D // 4)
    tokens_grad, dgain = input_grad(
        index, tokens, dout, dgate, after(dx, d_in), gain, gate_shards, conv_shards
    )
    d_gain = jnp.sum(dgain, axis=0)
    dtaps = jnp.sum(dtaps, axis=0)
    dsmall = jnp.sum(dsmall, axis=0)
    sums = jnp.sum(sums.reshape(2, 8, INNER), axis=1)
    d_skip = jnp.sum(sums[1].reshape(HEADS, INNER // HEADS), axis=1)
    four = lambda v: v.reshape(4, -1)
    d_small = jax.vmap(lay_out)(
        four(d_gain),
        dtaps[0:4].reshape(CONV, 4, quarter).transpose(1, 0, 2),
        four(dtaps[4]), four(dsmall[0, :HEADS]), four(dsmall[1, :HEADS]), four(d_skip), four(sums[0]),
    )
    d_step = d_in[CONVCH : CONVCH + HEADS].reshape(HEADS, 4, 256).transpose(1, 0, 2)
    d_small = jnp.concatenate([d_step, d_small.reshape(4, 18, 256).astype(BF)], axis=1)
    d_small = jnp.pad(d_small, ((0, 0), (0, 256 - 50), (0, 0)))
    h_small = swap_core(d_small.reshape(2, 2, 256, 256), 1).reshape(64, 8, 256)
    r_conv = exchange(jnp.concatenate([h_conv, h_small], axis=1))
    whole = spread_rows(jnp.concatenate([r_early, r_conv], axis=0))
    g_out = jnp.concatenate(
        [whole[:, 16 * j : 16 * j + 16].reshape(INNER // 4, 256) for j in range(4)], axis=1
    )
    g_gate = whole[:, 64:128].reshape(INNER, D // 4)
    g_conv = whole[:, 128:200].reshape(CONVCH, D // 4)
    g_small = whole[:, 200:208].reshape(256, D // 4)
    g_in = jnp.concatenate([g_gate, g_conv, g_small[:HEADS]], axis=0).astype(F32)
    s = g_small[HEADS : HEADS + 18].astype(F32).reshape(8, quarter)
    return (
        block_out,
        tokens_grad,
        s[6, : D // 4],
        g_in.T,
        s[0:4],
        s[4],
        s[6, D // 4 : D // 4 + 8],
        s[6, D // 4 + 8 : D // 4 + 16],
        s[6, D // 4 + 16 : D // 4 + 24],
        s[5, : INNER // 4],
        g_out.astype(F32),
    )


def solution(mesh):
    names = ("yl", "core", "z", "x", "yh")
    fine = Mesh(mesh.devices.reshape(2, 2, 4, 4, 2), names)
    every = P(names, None)
    shard = P(("yl", "core"))
    rows = P(("yl", "core"), None)
    columns = P(None, ("yl", "core"))
    return jax.shard_map(
        local,
        mesh=fine,
        in_specs=(
            every, shard, rows, columns, shard, shard, shard, shard, shard, rows, every, P(names),
        ),
        out_specs=(
            every, every, shard, rows, columns, shard, shard, shard, shard, shard, rows,
        ),
        check_vma=False,
    )
```

```python
import functools
import jax
import jax.numpy as jnp
from jax import lax
from jax.experimental import pallas as pl
from jax.experimental.pallas import tpu as pltpu
from jax.sharding import Mesh, PartitionSpec as P

D = 1024
INNER = 2048
CONV = 4
LEN = 256
HEADS = 32
STATE = 128
CONVCH = 2304
HALF = 128
GROUPS = 4
GCOLS = INNER // GROUPS
GHEADS = HEADS // GROUPS
BF = jnp.bfloat16
F32 = jnp.float32
LOG2E = 1.4426950408889634
MIB = 1024 * 1024


def cost(us):
    return pl.CostEstimate(
        flops=int(us * 1.0e9), transcendentals=0, bytes_accessed=int(us * 3.3e6)
    )


def dot(a, b):
    return lax.dot_general(a, b, (((1,), (0,)), ((), ())), preferred_element_type=F32)


def dot_nt(a, b):
    return lax.dot_general(a, b, (((1,), (1,)), ((), ())), preferred_element_type=F32)


def dot_tn(a, b):
    return lax.dot_general(a, b, (((0,), (0,)), ((), ())), preferred_element_type=F32)


def add_low(a, b):
    return (a.astype(F32) + b.astype(F32)).astype(BF)


def dot_exact(ones, v):
    hi = v.astype(BF)
    rest = v - hi.astype(F32)
    mid = rest.astype(BF)
    low = (rest - mid.astype(F32)).astype(BF)
    return dot(ones, hi) + dot(ones, mid) + dot(ones, low)


def dot_split(v, ones):
    hi = v.astype(BF)
    low = (v - hi.astype(F32)).astype(BF)
    return dot(hi, ones) + dot(low, ones)


def sigmoid(v):
    return 0.5 * jnp.tanh(0.5 * v) + 0.5


def rows_down(v, count):
    row = lax.broadcasted_iota(jnp.int32, v.shape, 0)
    return jnp.where(row >= count, pltpu.roll(v, count, axis=0), 0.0)


def rows_up(v, count):
    rows = v.shape[0]
    row = lax.broadcasted_iota(jnp.int32, v.shape, 0)
    return jnp.where(row < rows - count, pltpu.roll(v, rows - count, axis=0), 0.0)


def conv_forward(x, taps, bias):
    total = bias + taps[3:4] * x
    for back in range(1, CONV):
        total = total + taps[3 - back : 4 - back] * rows_down(x, back)
    return total


def conv_backward(x, taps, bias, dact, dtaps_ref, columns):
    v = conv_forward(x, taps, bias)
    sg = sigmoid(v)
    dv = dact * (sg * (1.0 + v * (1.0 - sg)))
    dx = taps[3:4] * dv
    sums = [jnp.sum(dv * x, axis=0, keepdims=True)]
    for back in range(1, CONV):
        dx = dx + taps[3 - back : 4 - back] * rows_up(dv, back)
        sums.insert(0, jnp.sum(dv * rows_down(x, back), axis=0, keepdims=True))
    sums.append(jnp.sum(dv, axis=0, keepdims=True))
    sums.append(jnp.zeros((3, x.shape[1]), F32))
    dtaps_ref[0, :, columns] = jnp.concatenate(sums, axis=0)
    return dx


def step_of(raw, bias):
    z = raw + bias
    return jnp.maximum(z, 0.0) + jnp.log1p(jnp.exp(-jnp.abs(z)))


def tri_masks():
    down = lax.broadcasted_iota(jnp.int32, (HALF, HALF), 0)
    across = lax.broadcasted_iota(jnp.int32, (HALF, HALF), 1)
    return down, across


def head_lanes(v, first):
    lane = lax.broadcasted_iota(jnp.int32, v.shape, 1)
    zero = jnp.zeros_like(v)
    return jnp.where(lane < 64, v, zero) if first else jnp.where(lane < 64, zero, v)


def scan_forward_kernel(
    xv_ref, xbc_ref, raw_ref, tv_ref, tbc_ref, dtb_ref, alog_ref,
    summed_ref, v_ref, bc_ref, step_ref, cum_ref,
    s_ref, cumt_ref, stept_ref,
):
    group = pl.program_id(1)

    @pl.when(group == 0)
    def _():
        act = conv_forward(xbc_ref[...], tbc_ref[0:4, :], tbc_ref[4:5, :])
        bc = (act * sigmoid(act)).astype(BF)
        bc_ref[...] = bc
        s_ref[...] = dot_nt(bc[:, STATE:], bc[:, :STATE])
        step = step_of(raw_ref[...], dtb_ref[...])
        logdecay = -step * jnp.exp(alog_ref[...])
        row = lax.broadcasted_iota(jnp.int32, (LEN, LEN), 0)
        col = lax.broadcasted_iota(jnp.int32, (LEN, LEN), 1)
        lower = jnp.where(row >= col, 1.0, 0.0).astype(BF)
        cum = dot_exact(lower, logdecay) * LOG2E
        step_ref[...] = step
        cum_ref[...] = cum
        cumt_ref[...] = cum.T
        stept_ref[...] = step.T

    act = conv_forward(xv_ref[...], tv_ref[0:4, :], tv_ref[4:5, :])
    v_ref[...] = (act * sigmoid(act)).astype(BF)
    cols = pltpu.roll(cum_ref[...], lax.rem(128 - GHEADS * group, 128), axis=1)
    first = pl.multiple_of(GHEADS * group, GHEADS)
    cum_rows = cumt_ref[pl.ds(first, GHEADS), :]
    step_rows = stept_ref[pl.ds(first, GHEADS), :]
    down, across = tri_masks()
    live = down >= across
    for pair in range(GHEADS // 2):
        lanes = slice(128 * pair, 128 * pair + 128)
        vp = v_ref[:, lanes]
        top = jnp.zeros((HALF, 128), F32)
        bottom = jnp.zeros((HALF, 128), F32)
        for side in range(2):
            head = 2 * pair + side
            vm = head_lanes(vp, side == 0)
            ci = cols[:, head : head + 1]
            cj = cum_rows[head : head + 1, :]
            sj = step_rows[head : head + 1, :]
            w00 = jnp.where(live, jnp.exp2(ci[:HALF] - cj[:, :HALF]), 0.0) * sj[:, :HALF]
            w10 = jnp.exp2(ci[HALF:] - cj[:, :HALF]) * sj[:, :HALF]
            w11 = jnp.where(live, jnp.exp2(ci[HALF:] - cj[:, HALF:]), 0.0) * sj[:, HALF:]
            m00 = (s_ref[:HALF, :HALF] * w00).astype(BF)
            m10 = (s_ref[HALF:, :HALF] * w10).astype(BF)
            m11 = (s_ref[HALF:, HALF:] * w11).astype(BF)
            top = top + dot(m00, vm[:HALF])
            bottom = bottom + dot(jnp.concatenate([m10, m11], axis=1), vm)
        summed_ref[:HALF, lanes] = top
        summed_ref[HALF:, lanes] = bottom


def scan_forward(xconv, raw, taps, dtb, alog, slots):
    rows = slots * LEN
    by_slot = lambda slot, group: (slot, 0)
    fixed = lambda slot, group: (0, 0)
    return pl.pallas_call(
        scan_forward_kernel,
        grid=(slots, GROUPS),
        in_specs=[
            pl.BlockSpec((LEN, GCOLS), lambda slot, group: (slot, group)),
            pl.BlockSpec((LEN, 2 * STATE), lambda slot, group: (slot, INNER // (2 * STATE))),
            pl.BlockSpec((LEN, 128), by_slot),
            pl.BlockSpec((8, GCOLS), lambda slot, group: (0, group)),
            pl.BlockSpec((8, 2 * STATE), lambda slot, group: (0, INNER // (2 * STATE))),
            pl.BlockSpec((1, 128), fixed),
            pl.BlockSpec((1, 128), fixed),
        ],
        out_specs=[
            pl.BlockSpec((LEN, GCOLS), lambda slot, group: (slot, group)),
            pl.BlockSpec((LEN, GCOLS), lambda slot, group: (slot, group)),
            pl.BlockSpec((LEN, 2 * STATE), by_slot),
            pl.BlockSpec((LEN, 128), by_slot),
            pl.BlockSpec((LEN, 128), by_slot),
        ],
        out_shape=[
            jax.ShapeDtypeStruct((rows, INNER), F32),
            jax.ShapeDtypeStruct((rows, INNER), BF),
            jax.ShapeDtypeStruct((rows, 2 * STATE), BF),
            jax.ShapeDtypeStruct((rows, 128), F32),
            jax.ShapeDtypeStruct((rows, 128), F32),
        ],
        scratch_shapes=[
            pltpu.VMEM((LEN, LEN), F32),
            pltpu.VMEM((128, LEN), F32),
            pltpu.VMEM((128, LEN), F32),
        ],
        compiler_params=pltpu.CompilerParams(
            dimension_semantics=("arbitrary", "arbitrary"), vmem_limit_bytes=16 * MIB
        ),
        name="scan_forward",
        cost_estimate=cost(0.2),
    )(xconv, xconv, raw, taps, taps, dtb, alog)


STRIP = 64
CHUNK = 128


def middle_kernel(
    index_ref, len_ref, summed_ref, v_ref, gate_ref, tok_ref, og_ref, gain_ref, skip_ref, *refs
):
    shards = refs[0:6]
    out_ref, m_ref, do_ref, dscan_ref, dgate_ref, rowsum_ref, sums_ref = refs[6:13]
    wo_ref, unit_ref, dm_ref, scale_ref, high_ref, low_ref, sems = refs[13:]
    step = pl.program_id(0)
    block = summed_ref.shape[0]
    per_slot = LEN // block
    count = len_ref[step // per_slot]
    row = lax.broadcasted_iota(jnp.int32, (block, 1), 0) + lax.rem(step, per_slot) * block
    live = row < count
    chunks = [slice(at, at + CHUNK) for at in range(0, INNER, CHUNK)]
    copies = out_proj_copies(index_ref[0], shards, wo_ref, sems)

    @pl.when(step == 0)
    def _():
        sums_ref[...] = jnp.zeros_like(sums_ref)
        for copy in copies:
            copy.start()

    def fold_rows(v):
        return sum(v[at : at + 8] for at in range(0, STRIP, 8))

    def forward(at, carry):
        rows = pl.ds(pl.multiple_of(at * STRIP, STRIP), STRIP)
        total = jnp.zeros((STRIP, 128), F32)
        for c in chunks:
            scanned = summed_ref[rows, c] + skip_ref[:, c] * v_ref[rows, c].astype(F32)
            gate = gate_ref[rows, c]
            gated = scanned * (gate * sigmoid(gate))
            unit_ref[rows, c] = gated
            total = total + gated * gated
        scale = lax.rsqrt(jnp.sum(total, axis=1, keepdims=True) * (1.0 / INNER) + 1e-05)
        scale_ref[rows, :] = jnp.broadcast_to(scale, (STRIP, 128))
        for c in chunks:
            unit = unit_ref[rows, c] * scale
            unit_ref[rows, c] = unit
            m_ref[rows, c] = (unit * gain_ref[:, c]).astype(BF)
        return carry

    lax.fori_loop(0, block // STRIP, forward, 0)
    dout = jnp.where(live, og_ref[...].astype(F32), 0.0).astype(BF)
    do_ref[...] = dout

    @pl.when(step == 0)
    def _():
        for copy in copies:
            copy.wait()

    result = tok_ref[...].astype(F32) + dot(m_ref[...], wo_ref[...])
    out_ref[...] = jnp.where(live, result, 0.0).astype(BF)
    dm_ref[...] = dot_nt(dout, wo_ref[...])

    def backward(at, carry):
        rows = pl.ds(pl.multiple_of(at * STRIP, STRIP), STRIP)
        total = jnp.zeros((STRIP, 128), F32)
        for c in chunks:
            unit = unit_ref[rows, c]
            grown = dm_ref[rows, c] * unit
            sums_ref[0:8, c] += fold_rows(grown)
            total = total + grown * gain_ref[:, c]
        mean = jnp.sum(total, axis=1, keepdims=True) * (1.0 / INNER)
        scale = scale_ref[rows, 0:1]
        for c in chunks:
            dgated = scale * (dm_ref[rows, c] * gain_ref[:, c] - unit_ref[rows, c] * mean)
            summed = summed_ref[rows, c]
            v = v_ref[rows, c].astype(F32)
            gate = gate_ref[rows, c]
            sg = sigmoid(gate)
            act = gate * sg
            dscan = dgated * act
            dscan_ref[rows, c] = dscan
            scanned = summed + skip_ref[:, c] * v
            dgate_ref[rows, c] = (dgated * scanned * (sg + act * (1.0 - sg))).astype(BF)
            skipped = dscan * v
            sums_ref[8:16, c] += fold_rows(skipped)
            product = dscan.astype(BF).astype(F32) * summed
            high = product.astype(BF)
            high_ref[rows, c] = high
            low_ref[rows, c] = (product - high.astype(F32)).astype(BF)
        return carry

    lax.fori_loop(0, block // STRIP, backward, 0)
    channel = lax.broadcasted_iota(jnp.int32, (INNER, 128), 0)
    lane = lax.broadcasted_iota(jnp.int32, (INNER, 128), 1)
    heads = jnp.where(channel // 64 == lane, 1.0, 0.0).astype(BF)
    rowsum_ref[...] = dot(high_ref[...], heads) + dot(low_ref[...], heads)


def middle(index, lengths, summed, v, gate, tokens, out_grad, shards, gain, skip, block=256):
    rows = summed.shape[0]
    wide = pl.BlockSpec((block, INNER), lambda step, index, lens: (step, 0))
    narrow = pl.BlockSpec((block, D), lambda step, index, lens: (step, 0))
    vector = pl.BlockSpec((1, INNER), lambda step, index, lens: (0, 0))
    return pl.pallas_call(
        middle_kernel,
        grid_spec=pltpu.PrefetchScalarGridSpec(
            num_scalar_prefetch=2,
            grid=(rows // block,),
            in_specs=[wide, wide, wide, narrow, narrow, vector, vector]
            + [pl.BlockSpec(memory_space=pl.ANY) for _ in shards],
            out_specs=[
                narrow, wide, narrow, wide, wide,
                pl.BlockSpec((block, 128), lambda step, index, lens: (step, 0)),
                pl.BlockSpec((16, INNER), lambda step, index, lens: (0, 0)),
            ],
            scratch_shapes=[
                pltpu.VMEM((INNER, D), BF),
                pltpu.VMEM((block, INNER), F32),
                pltpu.VMEM((block, INNER), F32),
                pltpu.VMEM((block, 128), F32),
                pltpu.VMEM((block, INNER), BF),
                pltpu.VMEM((block, INNER), BF),
                pltpu.SemaphoreType.DMA((18,)),
            ],
        ),
        out_shape=[
            jax.ShapeDtypeStruct((rows, D), BF),
            jax.ShapeDtypeStruct((rows, INNER), BF),
            jax.ShapeDtypeStruct((rows, D), BF),
            jax.ShapeDtypeStruct((rows, INNER), F32),
            jax.ShapeDtypeStruct((rows, INNER), BF),
            jax.ShapeDtypeStruct((rows, 128), F32),
            jax.ShapeDtypeStruct((16, INNER), F32),
        ],
        compiler_params=pltpu.CompilerParams(
            dimension_semantics=("arbitrary",), vmem_limit_bytes=28 * MIB
        ),
        name="middle",
        cost_estimate=cost(0.2),
    )(index, lengths, summed, v, gate, tokens, out_grad, gain, skip, *shards)


def scan_backward_kernel(
    xv_ref, xbc_ref, raw_ref, tv_ref, tbc_ref, dtb_ref, alog_ref, skip_ref,
    v_ref, bc_ref, step_ref, cum_ref, dscan_ref, rowsum_ref,
    dx_ref, dtaps_ref, dsmall_ref,
    st_ref, dst_ref, cumt_ref, colsum_ref,
):
    group = pl.program_id(1)

    @pl.when(group == 0)
    def _():
        bc = bc_ref[...]
        st_ref[...] = dot_nt(bc[:, :STATE], bc[:, STATE:])
        dst_ref[...] = jnp.zeros_like(dst_ref)
        colsum_ref[...] = jnp.zeros_like(colsum_ref)
        cumt_ref[...] = cum_ref[...].T

    shift = lax.rem(128 - GHEADS * group, 128)
    cum_cols = pltpu.roll(cum_ref[...], shift, axis=1)
    step_cols = pltpu.roll(step_ref[...], shift, axis=1)
    cum_rows = cumt_ref[pl.ds(pl.multiple_of(GHEADS * group, GHEADS), GHEADS), :]
    down, across = tri_masks()
    live = across >= down
    dvs = []
    for pair in range(GHEADS // 2):
        lanes = slice(128 * pair, 128 * pair + 128)
        vp = v_ref[:, lanes]
        dsp = dscan_ref[:, lanes].astype(BF)
        top = jnp.zeros((HALF, 128), F32)
        bottom = jnp.zeros((HALF, 128), F32)
        d00 = dst_ref[:HALF, :HALF]
        d01 = dst_ref[:HALF, HALF:]
        d11 = dst_ref[HALF:, HALF:]
        for side in range(2):
            head = 2 * pair + side
            vm = head_lanes(vp, side == 0)
            dsm = head_lanes(dsp, side == 0)
            ci = cum_rows[head : head + 1, :]
            cj = cum_cols[:, head : head + 1]
            sj = step_cols[:, head : head + 1]
            w00 = jnp.where(live, jnp.exp2(ci[:, :HALF] - cj[:HALF]), 0.0) * sj[:HALF]
            w01 = jnp.exp2(ci[:, HALF:] - cj[:HALF]) * sj[:HALF]
            w11 = jnp.where(live, jnp.exp2(ci[:, HALF:] - cj[HALF:]), 0.0) * sj[HALF:]
            dtop = dot_nt(vm[:HALF], dsp)
            dbottom = dot_nt(vm[HALF:], dsp[HALF:])
            d00 = d00 + dtop[:, :HALF] * w00
            d01 = d01 + dtop[:, HALF:] * w01
            d11 = d11 + dbottom * w11
            m00 = (st_ref[:HALF, :HALF] * w00).astype(BF)
            m01 = (st_ref[:HALF, HALF:] * w01).astype(BF)
            m11 = (st_ref[HALF:, HALF:] * w11).astype(BF)
            top = top + dot(jnp.concatenate([m00, m01], axis=1), dsm)
            bottom = bottom + dot(m11, dsm[HALF:])
        dst_ref[:HALF, :HALF] = d00
        dst_ref[:HALF, HALF:] = d01
        dst_ref[HALF:, HALF:] = d11
        dvs.append(jnp.concatenate([top, bottom], axis=0))
    dv = jnp.concatenate(dvs, axis=1)
    channel = lax.broadcasted_iota(jnp.int32, (GCOLS, 128), 0)
    lane = lax.broadcasted_iota(jnp.int32, (GCOLS, 128), 1)
    heads = jnp.where(channel // 64 + GHEADS * group == lane, 1.0, 0.0).astype(BF)
    colsum_ref[...] += dot_split(v_ref[...].astype(F32) * dv, heads)
    dact = dv + skip_ref[...] * dscan_ref[...]
    columns = pl.ds(pl.multiple_of(GCOLS * group, GCOLS), GCOLS)
    dx = conv_backward(
        xv_ref[...], tv_ref[0:4, :], tv_ref[4:5, :], dact, dtaps_ref, columns
    )
    dx_ref[:, columns] = dx.astype(BF)

    @pl.when(group == GROUPS - 1)
    def _():
        bc = bc_ref[...]
        dst = dst_ref[...].astype(BF)
        db = dot(dst, bc[:, STATE:])
        dc = dot_tn(dst, bc[:, :STATE])
        dbc = conv_backward(
            xbc_ref[...], tbc_ref[0:4, :], tbc_ref[4:5, :],
            jnp.concatenate([db, dc], axis=1), dtaps_ref, slice(INNER, CONVCH),
        )
        dx_ref[:, INNER:CONVCH] = dbc.astype(BF)
        row = lax.broadcasted_iota(jnp.int32, (LEN, LEN), 0)
        col = lax.broadcasted_iota(jnp.int32, (LEN, LEN), 1)
        upper = jnp.where(col >= row, 1.0, 0.0).astype(BF)
        colsum = colsum_ref[...]
        dlog = dot_exact(upper, rowsum_ref[...] - colsum)
        step = step_ref[...]
        rate = jnp.exp(alog_ref[...])
        z = raw_ref[...] + dtb_ref[...]
        sg = 1.0 / (1.0 + jnp.exp(-z))
        tiny = z < -20.0
        ratio = jnp.where(tiny, 1.0, sg / jnp.where(tiny, 1.0, step))
        draw = colsum * ratio - dlog * rate * sg
        lane32 = lax.broadcasted_iota(jnp.int32, (LEN, 128), 1)
        draw = jnp.where(lane32 < HEADS, draw, 0.0)
        dx_ref[:, CONVCH:] = draw.astype(BF)
        dalog = -dlog * step * rate
        dsmall_ref[0] = jnp.concatenate(
            [
                jnp.sum(draw, axis=0, keepdims=True),
                jnp.sum(dalog, axis=0, keepdims=True),
                jnp.zeros((6, 128), F32),
            ],
            axis=0,
        )


def scan_backward(xconv, raw, taps, dtb, alog, skip, v, bc, step, cum, dscan, rowsum, slots):
    rows = slots * LEN
    by_slot = lambda slot, group: (slot, 0)
    fixed = lambda slot, group: (0, 0)
    by_group = pl.BlockSpec((LEN, GCOLS), lambda slot, group: (slot, group))
    last = INNER // (2 * STATE)
    return pl.pallas_call(
        scan_backward_kernel,
        grid=(slots, GROUPS),
        in_specs=[
            by_group,
            pl.BlockSpec((LEN, 2 * STATE), lambda slot, group: (slot, last)),
            pl.BlockSpec((LEN, 128), by_slot),
            pl.BlockSpec((8, GCOLS), lambda slot, group: (0, group)),
            pl.BlockSpec((8, 2 * STATE), lambda slot, group: (0, last)),
            pl.BlockSpec((1, 128), fixed),
            pl.BlockSpec((1, 128), fixed),
            pl.BlockSpec((1, GCOLS), lambda slot, group: (0, group)),
            by_group,
            pl.BlockSpec((LEN, 2 * STATE), by_slot),
            pl.BlockSpec((LEN, 128), by_slot),
            pl.BlockSpec((LEN, 128), by_slot),
            by_group,
            pl.BlockSpec((LEN, 128), by_slot),
        ],
        out_specs=[
            pl.BlockSpec((LEN, CONVCH + 128), by_slot),
            pl.BlockSpec((1, 8, CONVCH), lambda slot, group: (slot, 0, 0)),
            pl.BlockSpec((1, 8, 128), lambda slot, group: (slot, 0, 0)),
        ],
        out_shape=[
            jax.ShapeDtypeStruct((rows, CONVCH + 128), BF),
            jax.ShapeDtypeStruct((slots, 8, CONVCH), F32),
            jax.ShapeDtypeStruct((slots, 8, 128), F32),
        ],
        scratch_shapes=[
            pltpu.VMEM((LEN, LEN), F32),
            pltpu.VMEM((LEN, LEN), F32),
            pltpu.VMEM((128, LEN), F32),
            pltpu.VMEM((LEN, 128), F32),
        ],
        compiler_params=pltpu.CompilerParams(
            dimension_semantics=("arbitrary", "arbitrary"), vmem_limit_bytes=56 * MIB
        ),
        name="scan_backward",
        cost_estimate=cost(0.2),
    )(xconv, xconv, raw, taps, taps, dtb, alog, skip, v, bc, step, cum, dscan, rowsum)


def shard_copies(me, shards, whole, sems, first, high):
    part = shards[0].shape[1]
    half = part // 2
    copies = []
    for i, (src, k, at) in enumerate(
        zip(shards, (0, 1, 2, 2, 3, 3), (0, 0, 0, half, 0, half))
    ):
        place = pl.ds(pl.multiple_of((me ^ k) * part + at, half), src.shape[1])
        rows = pl.ds(first, high)
        copies.append(pltpu.make_async_copy(src.at[rows, :], whole.at[rows, place], sems.at[i]))
    return copies


def out_proj_copies(me, shards, whole, sems):
    part = shards[0].shape[0]
    place = lambda k: pl.ds(pl.multiple_of((me ^ k) * part, part), part)
    copies = [
        pltpu.make_async_copy(src, whole.at[place(k), :], sems.at[k])
        for k, src in enumerate(shards[:2])
    ]
    for i, src in enumerate(shards[2:]):
        for block in range(4):
            lanes = pl.ds((i % 2) * 512 + block * 128, 128)
            rows = pl.ds(INNER + block * part, part)
            copies.append(
                pltpu.make_async_copy(
                    src.at[rows, :], whole.at[place(2 + i // 2), lanes], sems.at[len(copies)]
                )
            )
    return copies


def project_kernel(columns, block, tail, index_ref, n_ref, *refs):
    shards, (out_ref, *rest), (whole_ref, sems) = refs[0:6], refs[6:-2], refs[-2:]
    me = index_ref[0]
    step = pl.program_id(0)
    steps = columns // block

    def copies(at):
        return shard_copies(me, shards, whole_ref, sems.at[at], at * block, block)

    @pl.when(step == 0)
    def _():
        if tail:
            whole_ref[columns:, :] = jnp.zeros((whole_ref.shape[0] - columns, D), BF)
            last = shard_copies(me, shards, whole_ref, sems.at[steps], columns, HEADS)
            for copy in last:
                copy.start()
        for at in range(steps):
            for copy in copies(at):
                copy.start()
        if tail:
            for copy in last:
                copy.wait()
            rest[0][...] = dot_nt(n_ref[...], whole_ref[columns:, :])

    for at in range(steps):

        @pl.when(step == at)
        def _(at=at):
            for copy in copies(at):
                copy.wait()
            out_ref[...] = dot_nt(n_ref[...], whole_ref[at * block : (at + 1) * block, :])


def project(index, normed, shards, columns, block, tail):
    rows = normed.shape[0]
    out_specs = [pl.BlockSpec((rows, block), lambda step, index: (0, step))]
    out_shape = [jax.ShapeDtypeStruct((rows, columns), F32)]
    if tail:
        out_specs.append(pl.BlockSpec((rows, 128), lambda step, index: (0, 0)))
        out_shape.append(jax.ShapeDtypeStruct((rows, 128), F32))
    steps = columns // block
    return pl.pallas_call(
        functools.partial(project_kernel, columns, block, tail),
        grid_spec=pltpu.PrefetchScalarGridSpec(
            num_scalar_prefetch=1,
            grid=(steps,),
            in_specs=[pl.BlockSpec(normed.shape, lambda step, index: (0, 0))]
            + [pl.BlockSpec(memory_space=pl.ANY) for _ in shards],
            out_specs=out_specs,
            scratch_shapes=[
                pltpu.VMEM((columns + 128 if tail else columns, D), BF),
                pltpu.SemaphoreType.DMA((steps + 1 if tail else steps, 6)),
            ],
        ),
        out_shape=out_shape,
        compiler_params=pltpu.CompilerParams(
            dimension_semantics=("arbitrary",), vmem_limit_bytes=18 * MIB
        ),
        name="project",
        cost_estimate=cost(0.2),
    )(index, normed, *shards)


def input_grad_kernel(index_ref, tok_ref, do_ref, dgate_ref, dx_ref, gain_ref, *refs):
    out_ref, dn_ref, gate_ref, conv_ref, sems = refs[12:]
    me = index_ref[0]
    gate_copies = shard_copies(me, refs[0:6], gate_ref, sems.at[0], 0, INNER)
    conv_copies = shard_copies(me, refs[6:12], conv_ref, sems.at[1], 0, CONVCH + HEADS)
    for copy in gate_copies + conv_copies:
        copy.start()
    live = CONVCH + HEADS
    conv_ref[live:, :] = jnp.zeros((conv_ref.shape[0] - live, D), BF)
    for copy in gate_copies:
        copy.wait()
    dn_ref[...] = dot(dgate_ref[...], gate_ref[...])
    for copy in conv_copies:
        copy.wait()
    dn_ref[...] += dot(dx_ref[...], conv_ref[...])
    chunks = [slice(at, at + CHUNK) for at in range(0, D, CHUNK)]

    def finish(at, carry):
        rows = pl.ds(pl.multiple_of(at * STRIP, STRIP), STRIP)
        squares = jnp.zeros((STRIP, CHUNK), F32)
        for c in chunks:
            x = tok_ref[rows, c].astype(F32)
            squares = squares + x * x
        scale = lax.rsqrt(jnp.sum(squares, axis=1, keepdims=True) * (1.0 / D) + 1e-05)
        total = jnp.zeros((STRIP, CHUNK), F32)
        for c in chunks:
            grown = dn_ref[rows, c] * (tok_ref[rows, c].astype(F32) * scale)
            total = total + grown * gain_ref[:, c]
        mean = jnp.sum(total, axis=1, keepdims=True) * (1.0 / D)
        for c in chunks:
            unit = tok_ref[rows, c].astype(F32) * scale
            out_ref[rows, c] = do_ref[rows, c].astype(F32) + scale * (
                dn_ref[rows, c] * gain_ref[:, c] - unit * mean
            )
        return carry

    lax.fori_loop(0, tok_ref.shape[0] // STRIP, finish, 0)


def input_grad(index, tokens, dout, dgate, dx, gain, gate_shards, conv_shards):
    rows = tokens.shape[0]
    whole = lambda v: pl.BlockSpec(v.shape, lambda step, index: (0, 0))
    shards = list(gate_shards) + list(conv_shards)
    return pl.pallas_call(
        input_grad_kernel,
        grid_spec=pltpu.PrefetchScalarGridSpec(
            num_scalar_prefetch=1,
            grid=(1,),
            in_specs=[whole(v) for v in (tokens, dout, dgate, dx, gain)]
            + [pl.BlockSpec(memory_space=pl.ANY) for _ in shards],
            out_specs=pl.BlockSpec((rows, D), lambda step, index: (0, 0)),
            scratch_shapes=[
                pltpu.VMEM((rows, D), F32),
                pltpu.VMEM((INNER, D), BF),
                pltpu.VMEM((CONVCH + 128, D), BF),
                pltpu.SemaphoreType.DMA((2, 6)),
            ],
        ),
        out_shape=jax.ShapeDtypeStruct((rows, D), F32),
        compiler_params=pltpu.CompilerParams(
            dimension_semantics=("arbitrary",), vmem_limit_bytes=34 * MIB
        ),
        name="input_grad",
        cost_estimate=cost(0.2),
    )(index, tokens, dout, dgate, dx, gain, *shards)


def out_grad_kernel(add, core_ref, m0_ref, m1_ref, do_ref, *refs):
    out_ref = refs[-1]
    for yl, m_ref in enumerate((m0_ref, m1_ref)):
        grad = dot_tn(m_ref[...], do_ref[...]).astype(BF)
        for j in range(4):
            at = (slice(32 * yl, 32 * yl + 32), slice(16 * j, 16 * j + 16))
            piece = grad[:, 256 * j : 256 * j + 256].reshape(32, 16, 256)
            if add:
                piece = add_low(piece, refs[0][at])
            out_ref[at] = piece


def gate_grad_kernel(add, core_ref, dgate_ref, n0_ref, n1_ref, *refs):
    out_ref = refs[-1]
    both = jnp.concatenate([n0_ref[...], n1_ref[...]], axis=1)
    grad = dot_tn(dgate_ref[...], both).astype(BF)
    for yl in range(2):
        at = slice(32 * yl, 32 * yl + 32)
        piece = grad[:, 256 * yl : 256 * yl + 256].reshape(32, 64, 256)
        if add:
            piece = add_low(piece, refs[0][at])
        out_ref[at] = piece


def conv_grad_kernel(add, core_ref, dx_ref, n0_ref, n1_ref, *refs):
    out_ref = refs[-1]
    both = jnp.concatenate([n0_ref[...], n1_ref[...]], axis=1)
    grad = dot_tn(dx_ref[...], both)
    for yl in range(2):
        piece = grad[:, 256 * yl : 256 * yl + 256].reshape(16, 72, 256).astype(BF)
        if add:
            piece = add_low(piece, refs[0][yl])
        out_ref[yl] = piece


def part_of(yl):
    return lambda step, core: (0, 2 * yl + core[0])


def at_block(*block):
    return lambda step, core: block


def grad_call(kernel, name, core, operands, specs, got, got_spec, out_spec, out_shape, into):
    operands, specs = list(operands), list(specs)
    if got is not None:
        operands.append(got)
        specs.append(got_spec)
    aliases = {}
    if into is not None:
        aliases = {1 + len(operands): 0}
        operands.append(into)
        specs.append(pl.BlockSpec(memory_space=pl.ANY))
    return pl.pallas_call(
        functools.partial(kernel, got is not None),
        grid_spec=pltpu.PrefetchScalarGridSpec(
            num_scalar_prefetch=1, grid=(1,), in_specs=specs, out_specs=out_spec
        ),
        out_shape=jax.ShapeDtypeStruct(out_shape, BF),
        input_output_aliases=aliases,
        compiler_params=pltpu.CompilerParams(
            dimension_semantics=("arbitrary",), vmem_limit_bytes=24 * MIB
        ),
        name=name,
        cost_estimate=cost(0.2),
    )(core, *operands)


def out_grad_pieces(core, mixed, dout, got=None):
    rows = mixed.shape[0]
    block = pl.BlockSpec((64, 64, 256), at_block(0, 0, 0))
    return grad_call(
        out_grad_kernel, "out_proj_grad", core, (mixed, mixed, dout),
        [
            pl.BlockSpec((rows, INNER // 4), part_of(0)),
            pl.BlockSpec((rows, INNER // 4), part_of(1)),
            pl.BlockSpec((rows, D), at_block(0, 0)),
        ],
        got, block, block, (64, 64 if got is None else 128, 256), None,
    )


def gate_grad_pieces(core, dgate, normed, got=None, into=None):
    rows = normed.shape[0]
    first = 0 if into is None else 1
    return grad_call(
        gate_grad_kernel, "gate_grad", core, (dgate, normed, normed),
        [
            pl.BlockSpec((rows, INNER), at_block(0, 0)),
            pl.BlockSpec((rows, D // 4), part_of(0)),
            pl.BlockSpec((rows, D // 4), part_of(1)),
        ],
        got, pl.BlockSpec((64, 64, 256), at_block(0, 0, 0)),
        pl.BlockSpec((64, 64, 256), at_block(0, first, 0)),
        (64, 64 if into is None else 128, 256), into,
    )


def conv_grad_pieces(core, half, dx, normed, got=None, into=None):
    rows = dx.shape[0]
    high = 16 if got is None else 32
    where = 0 if got is None else half
    return grad_call(
        conv_grad_kernel, "conv_grad", core, (dx, normed, normed),
        [
            pl.BlockSpec((rows, CONVCH // 2), at_block(0, half)),
            pl.BlockSpec((rows, D // 4), part_of(0)),
            pl.BlockSpec((rows, D // 4), part_of(1)),
        ],
        got, pl.BlockSpec((2, 16, 72, 256), at_block(0, 0, 0, 0)),
        pl.BlockSpec((2, 16, 72, 256), at_block(0, where, 0, 0)),
        (2, high, 72, 256), into,
    )


def finish_kernel(got_ref, w_ref, gain_ref, in_ref, out_ref, norm_ref, small_ref, sum_ref):
    step = pl.program_id(0)
    got = got_ref[...].astype(F32)
    pieces = got.shape[0]

    def put(rows, value):
        in_ref[rows, :] = value
        product = value * w_ref[rows, :].astype(F32)
        sum_ref[...] += product.reshape(-1, 8, D // 4).sum(axis=0)

    @pl.when(step == 0)
    def _():
        sum_ref[...] = jnp.zeros_like(sum_ref)
        small = got[0:7, 200:208].reshape(56, D // 4)
        small_ref[...] = small
        put(slice(INNER + CONVCH, INNER + CONVCH + HEADS), small[:HEADS])

    for j in range(4):
        out_ref[:, 256 * j : 256 * j + 256] = got[:, 16 * j : 16 * j + 16].reshape(16 * pieces, 256)
    put(pl.ds(pl.multiple_of(step * 64 * pieces, 64), 64 * pieces), got[:, 64:128].reshape(-1, 256))
    put(
        pl.ds(pl.multiple_of(INNER + step * 72 * pieces, 64), 72 * pieces),
        got[:, 128:200].reshape(-1, 256),
    )
    norm_ref[...] = jnp.sum(sum_ref[...], axis=0, keepdims=True) / gain_ref[...]


def finish(got, w_in, gain):
    high, wide = w_in.shape
    whole = lambda v: pl.BlockSpec(v, lambda step: (0, 0))
    return pl.pallas_call(
        finish_kernel,
        grid=(4,),
        in_specs=[
            pl.BlockSpec((8,) + got.shape[1:], lambda step: (step, 0, 0)),
            whole((high, wide)),
            whole((1, wide)),
        ],
        out_specs=[
            whole((high, wide)),
            pl.BlockSpec((INNER // 16, D), lambda step: (step, 0)),
            whole((1, wide)),
            whole((56, wide)),
        ],
        out_shape=[
            jax.ShapeDtypeStruct((high, wide), F32),
            jax.ShapeDtypeStruct((INNER // 4, D), F32),
            jax.ShapeDtypeStruct((1, wide), F32),
            jax.ShapeDtypeStruct((56, wide), F32),
        ],
        scratch_shapes=[pltpu.VMEM((8, wide), F32)],
        compiler_params=pltpu.CompilerParams(
            dimension_semantics=("arbitrary",), vmem_limit_bytes=28 * MIB
        ),
        name="finish",
        cost_estimate=cost(0.2),
    )(got, w_in, gain)


SWAP = [(0, 1), (1, 0)]


def y_shift(by):
    place = lambda y: (y % 2) * 2 + y // 2
    return [(place(y), place((y + by) % 4)) for y in range(4)]


def halves(shard):
    half = shard.shape[1] // 2
    return shard[:, :half], shard[:, half:]


def from_y(first, second):
    return (
        lax.ppermute(first, ("yl", "yh"), y_shift(1)),
        lax.ppermute(second, ("yl", "yh"), y_shift(-1)),
    )


def from_core(*values):
    return tuple(lax.ppermute(v, "core", SWAP) for v in values)


def blocks_of_lanes(v):
    return [v[:, at : at + 128] for at in range(0, v.shape[1], 128)]


def after(values, *others):
    return lax.optimization_barrier((values,) + others)[0]


def exchange(half):
    return lax.all_to_all(half, ("yl", "z", "x", "yh"), 0, 0, tiled=True)


def add_up(got):
    return jnp.sum(got.astype(F32), axis=0).astype(BF)


def spread_rows(rows):
    copies = jnp.broadcast_to(rows[None], (32,) + rows.shape)
    return lax.all_to_all(copies, ("z", "x", "yh"), 0, 0, tiled=True)


def lay_out(norm_gain, conv_weight, conv_bias, dt_bias, a_log, d_skip, gate_gain):
    quarter = CONVCH // 4
    wide = lambda v: jnp.pad(v, (0, quarter - v.shape[0]))[None, :]
    mixed = jnp.concatenate([norm_gain, dt_bias, a_log, d_skip])
    return jnp.concatenate(
        [conv_weight, conv_bias[None, :], wide(gate_gain), wide(mixed), jnp.zeros((1, quarter), conv_weight.dtype)],
        axis=0,
    )


def local(
    tokens, norm_gain, in_proj, conv_weight, conv_bias, dt_bias, a_log, d_skip, gate_gain,
    out_proj, out_grad, lengths,
):
    slots = lengths.shape[0]
    quarter = CONVCH // 4
    me = lax.axis_index("yl") * 2 + lax.axis_index("core")
    index = me[None].astype(jnp.int32)

    w_in = in_proj.T
    conv_own, gate_own = w_in[INNER:], w_in[:INNER]
    conv_halves = lax.optimization_barrier(halves(conv_own))
    conv_y = from_y(*conv_halves)
    conv_rest = from_core(conv_own, *conv_y)
    conv_shards = (conv_own, conv_rest[0]) + conv_y + conv_rest[1:]
    small_in = (norm_gain, conv_weight, conv_bias, dt_bias, a_log, d_skip, gate_gain)
    small_in = lax.optimization_barrier(small_in + conv_halves)[:7]
    small = lay_out(*small_in)
    own = small
    core = lax.ppermute(own, "core", SWAP)
    other = lax.ppermute(own, "yl", SWAP)
    both = lax.ppermute(other, "core", SWAP)
    natural = jnp.take(jnp.stack([own, core, other, both]), jnp.arange(4) ^ me, axis=0)
    natural = lax.optimization_barrier(natural.astype(F32))
    taps = natural.transpose(1, 0, 2).reshape(8, CONVCH)
    gate_gain_all = natural[:, 5, : INNER // 4].reshape(1, INNER)
    gain = natural[:, 6, : D // 4].reshape(1, D)
    heads = natural[:, 6, D // 4 : D // 4 + 24].reshape(4, 3, 8).transpose(1, 0, 2).reshape(3, HEADS)
    skip = jnp.repeat(heads[2], INNER // HEADS)[None, :]
    heads = jnp.pad(heads, ((0, 0), (0, 128 - HEADS)))
    dtb, alog = heads[0:1], heads[1:2]

    x = tokens.astype(F32)
    scale = lax.rsqrt(jnp.mean(x * x, axis=1, keepdims=True) + 1e-05)
    normed = lax.optimization_barrier((x * scale * gain).astype(BF))
    second_y = from_y(
        *[
            jnp.concatenate([g] + blocks_of_lanes(o), axis=0)
            for g, o in zip(halves(gate_own), halves(out_proj))
        ]
    )
    xconv, raw = project(index, normed, conv_shards, CONVCH, 768, True)
    summed, v, bc, step, cum = scan_forward(xconv, raw, taps, dtb, alog, slots)
    *second_y, _ = lax.optimization_barrier(second_y + (summed,))
    gate_core, out_core, *second_core = from_core(
        *lax.optimization_barrier((gate_own, out_proj, summed))[:2], *second_y
    )
    gate_shards = (gate_own, gate_core, *second_y, *second_core)
    out_shards = (out_proj, out_core, *second_y, *second_core)
    gate = project(index, normed, gate_shards, INNER, 512, False)[0]
    block_out, mixed, dout, dscan, dgate, rowsum, sums = middle(
        index, lengths, summed, v, gate, tokens, out_grad, out_shards, gate_gain_all, skip, 128
    )
    mine = lax.axis_index("core").astype(jnp.int32)[None]
    theirs = 1 - mine
    send_out = out_grad_pieces(theirs, mixed, dout)
    got_out = lax.ppermute(send_out, "core", SWAP)
    send_gate = gate_grad_pieces(after(theirs, send_out), dgate, normed)
    got_gate = lax.ppermute(send_gate, "core", SWAP)
    h_early = out_grad_pieces(after(mine, send_gate), mixed, dout, got_out)
    h_early = gate_grad_pieces(mine, dgate, normed, got_gate, h_early)
    raw_early = exchange(h_early)
    dx, dtaps, dsmall = scan_backward(
        xconv, raw, taps, dtb, alog, skip, v, bc, step, cum, after(dscan, h_early), rowsum, slots
    )
    send_first = conv_grad_pieces(theirs, 0, dx, normed)
    got_first = lax.ppermute(send_first, "core", SWAP)
    send_second = conv_grad_pieces(after(theirs, send_first), 1, dx, normed)
    got_second = lax.ppermute(send_second, "core", SWAP)
    h_conv = conv_grad_pieces(after(mine, send_second), 0, dx, normed, got_first)
    d_step = dot_tn(dx[:, CONVCH : CONVCH + HEADS], normed)
    dtaps = jnp.sum(dtaps, axis=0)
    dsmall = jnp.sum(dsmall, axis=0)
    sums = jnp.sum(sums.reshape(2, 8, INNER), axis=1)
    d_skip = jnp.sum(sums[1].reshape(HEADS, INNER // HEADS), axis=1)
    four = lambda v: v.reshape(4, -1)
    d_small = jax.vmap(lay_out)(
        jnp.zeros((4, D // 4), F32),
        dtaps[0:4].reshape(CONV, 4, quarter).transpose(1, 0, 2),
        four(dtaps[4]), four(dsmall[0, :HEADS]), four(dsmall[1, :HEADS]), four(d_skip), four(sums[0]),
    )
    d_step = d_step.reshape(HEADS, 4, 256).transpose(1, 0, 2)
    d_small = jnp.concatenate([d_step, d_small.reshape(4, 18, 256)], axis=1).astype(BF)
    d_small = d_small.reshape(2, 2, 50, 256)
    pick = lambda core: lax.dynamic_index_in_dim(d_small, core[0], 1, keepdims=False)
    h_small = add_low(pick(mine), lax.ppermute(pick(theirs), "core", SWAP))
    h_small = jnp.pad(h_small, ((0, 0), (0, 206), (0, 0))).reshape(64, 8, 256)
    h_conv = conv_grad_pieces(mine, 1, dx, normed, got_second, h_conv)
    h_late = jnp.concatenate([h_conv.reshape(64, CONVCH // 32, D // 4), h_small], axis=1)
    h_late, raw_early = lax.optimization_barrier((h_late, raw_early))
    raw_late = exchange(h_late)
    r_early = add_up(raw_early)
    tokens_grad = input_grad(
        index, tokens, dout, dgate, after(dx, h_late), gain, gate_shards, conv_shards
    )
    r_conv = add_up(raw_late)
    whole = spread_rows(jnp.concatenate([r_early, r_conv], axis=0))
    g_in, g_out, g_norm, g_small = finish(whole, w_in, norm_gain.astype(F32)[None, :])
    s = g_small[HEADS : HEADS + 18].reshape(8, quarter)
    return (
        block_out,
        tokens_grad,
        g_norm[0],
        g_in.T,
        s[0:4],
        s[4],
        s[6, D // 4 : D // 4 + 8],
        s[6, D // 4 + 8 : D // 4 + 16],
        s[6, D // 4 + 16 : D // 4 + 24],
        s[5, : INNER // 4],
        g_out,
    )


def solution(mesh):
    names = ("yl", "core", "z", "x", "yh")
    fine = Mesh(mesh.devices.reshape(2, 2, 4, 4, 2), names)
    every = P(names, None)
    shard = P(("yl", "core"))
    rows = P(("yl", "core"), None)
    columns = P(None, ("yl", "core"))
    return jax.shard_map(
        local,
        mesh=fine,
        in_specs=(
            every, shard, rows, columns, shard, shard, shard, shard, shard, rows, every, P(names),
        ),
        out_specs=(
            every, every, shard, rows, columns, shard, shard, shard, shard, shard, rows,
        ),
        check_vma=False,
    )
```

```python
import functools
import jax
import jax.numpy as jnp
from jax import lax
from jax.experimental import pallas as pl
from jax.experimental.pallas import tpu as pltpu
from jax.sharding import Mesh, PartitionSpec as P

D = 1024
INNER = 2048
CONV = 4
LEN = 256
HEADS = 32
STATE = 128
CONVCH = 2304
HALF = 128
GROUPS = 4
GCOLS = INNER // GROUPS
GHEADS = HEADS // GROUPS
BF = jnp.bfloat16
F32 = jnp.float32
LOG2E = 1.4426950408889634
MIB = 1024 * 1024


def cost(us):
    return pl.CostEstimate(
        flops=int(us * 1.0e9), transcendentals=0, bytes_accessed=int(us * 3.3e6)
    )


def dot(a, b):
    return lax.dot_general(a, b, (((1,), (0,)), ((), ())), preferred_element_type=F32)


def dot_nt(a, b):
    return lax.dot_general(a, b, (((1,), (1,)), ((), ())), preferred_element_type=F32)


def dot_tn(a, b):
    return lax.dot_general(a, b, (((0,), (0,)), ((), ())), preferred_element_type=F32)


def add_low(a, b):
    return (a.astype(F32) + b.astype(F32)).astype(BF)


def dot_exact(ones, v):
    hi = v.astype(BF)
    rest = v - hi.astype(F32)
    mid = rest.astype(BF)
    low = (rest - mid.astype(F32)).astype(BF)
    return dot(ones, hi) + dot(ones, mid) + dot(ones, low)


def dot_split(v, ones):
    hi = v.astype(BF)
    low = (v - hi.astype(F32)).astype(BF)
    return dot(hi, ones) + dot(low, ones)


def sigmoid(v):
    return 0.5 * jnp.tanh(0.5 * v) + 0.5


def rows_down(v, count):
    row = lax.broadcasted_iota(jnp.int32, v.shape, 0)
    return jnp.where(row >= count, pltpu.roll(v, count, axis=0), 0.0)


def rows_up(v, count):
    rows = v.shape[0]
    row = lax.broadcasted_iota(jnp.int32, v.shape, 0)
    return jnp.where(row < rows - count, pltpu.roll(v, rows - count, axis=0), 0.0)


def conv_forward(x, taps, bias):
    total = bias + taps[3:4] * x
    for back in range(1, CONV):
        total = total + taps[3 - back : 4 - back] * rows_down(x, back)
    return total


def conv_backward(x, taps, bias, dact, dtaps_ref, columns):
    v = conv_forward(x, taps, bias)
    sg = sigmoid(v)
    dv = dact * (sg * (1.0 + v * (1.0 - sg)))
    dx = taps[3:4] * dv
    sums = [jnp.sum(dv * x, axis=0, keepdims=True)]
    for back in range(1, CONV):
        dx = dx + taps[3 - back : 4 - back] * rows_up(dv, back)
        sums.insert(0, jnp.sum(dv * rows_down(x, back), axis=0, keepdims=True))
    sums.append(jnp.sum(dv, axis=0, keepdims=True))
    sums.append(jnp.zeros((3, x.shape[1]), F32))
    dtaps_ref[0, :, columns] = jnp.concatenate(sums, axis=0)
    return dx


def step_of(raw, bias):
    z = raw + bias
    return jnp.maximum(z, 0.0) + jnp.log1p(jnp.exp(-jnp.abs(z)))


def tri_masks():
    down = lax.broadcasted_iota(jnp.int32, (HALF, HALF), 0)
    across = lax.broadcasted_iota(jnp.int32, (HALF, HALF), 1)
    return down, across


def head_lanes(v, first):
    lane = lax.broadcasted_iota(jnp.int32, v.shape, 1)
    zero = jnp.zeros_like(v)
    return jnp.where(lane < 64, v, zero) if first else jnp.where(lane < 64, zero, v)


def scan_forward_kernel(
    xv_ref, xbc_ref, raw_ref, tv_ref, tbc_ref, dtb_ref, alog_ref,
    summed_ref, v_ref, bc_ref, step_ref, cum_ref,
    s_ref, cumt_ref, stept_ref,
):
    group = pl.program_id(1)

    @pl.when(group == 0)
    def _():
        act = conv_forward(xbc_ref[...], tbc_ref[0:4, :], tbc_ref[4:5, :])
        bc = (act * sigmoid(act)).astype(BF)
        bc_ref[...] = bc
        s_ref[...] = dot_nt(bc[:, STATE:], bc[:, :STATE])
        step = step_of(raw_ref[...], dtb_ref[...])
        logdecay = -step * jnp.exp(alog_ref[...])
        row = lax.broadcasted_iota(jnp.int32, (LEN, LEN), 0)
        col = lax.broadcasted_iota(jnp.int32, (LEN, LEN), 1)
        lower = jnp.where(row >= col, 1.0, 0.0).astype(BF)
        cum = dot_exact(lower, logdecay) * LOG2E
        step_ref[...] = step
        cum_ref[...] = cum
        cumt_ref[...] = cum.T
        stept_ref[...] = step.T

    act = conv_forward(xv_ref[...], tv_ref[0:4, :], tv_ref[4:5, :])
    v_ref[...] = (act * sigmoid(act)).astype(BF)
    cols = pltpu.roll(cum_ref[...], lax.rem(128 - GHEADS * group, 128), axis=1)
    first = pl.multiple_of(GHEADS * group, GHEADS)
    cum_rows = cumt_ref[pl.ds(first, GHEADS), :]
    step_rows = stept_ref[pl.ds(first, GHEADS), :]
    down, across = tri_masks()
    live = down >= across
    for pair in range(GHEADS // 2):
        lanes = slice(128 * pair, 128 * pair + 128)
        vp = v_ref[:, lanes]
        top = jnp.zeros((HALF, 128), F32)
        bottom = jnp.zeros((HALF, 128), F32)
        for side in range(2):
            head = 2 * pair + side
            vm = head_lanes(vp, side == 0)
            ci = cols[:, head : head + 1]
            cj = cum_rows[head : head + 1, :]
            sj = step_rows[head : head + 1, :]
            w00 = jnp.where(live, jnp.exp2(ci[:HALF] - cj[:, :HALF]), 0.0) * sj[:, :HALF]
            w10 = jnp.exp2(ci[HALF:] - cj[:, :HALF]) * sj[:, :HALF]
            w11 = jnp.where(live, jnp.exp2(ci[HALF:] - cj[:, HALF:]), 0.0) * sj[:, HALF:]
            m00 = (s_ref[:HALF, :HALF] * w00).astype(BF)
            m10 = (s_ref[HALF:, :HALF] * w10).astype(BF)
            m11 = (s_ref[HALF:, HALF:] * w11).astype(BF)
            top = top + dot(m00, vm[:HALF])
            bottom = bottom + dot(jnp.concatenate([m10, m11], axis=1), vm)
        summed_ref[:HALF, lanes] = top
        summed_ref[HALF:, lanes] = bottom


def scan_forward(xconv, raw, taps, dtb, alog, slots):
    rows = slots * LEN
    by_slot = lambda slot, group: (slot, 0)
    fixed = lambda slot, group: (0, 0)
    return pl.pallas_call(
        scan_forward_kernel,
        grid=(slots, GROUPS),
        in_specs=[
            pl.BlockSpec((LEN, GCOLS), lambda slot, group: (slot, group)),
            pl.BlockSpec((LEN, 2 * STATE), lambda slot, group: (slot, INNER // (2 * STATE))),
            pl.BlockSpec((LEN, 128), by_slot),
            pl.BlockSpec((8, GCOLS), lambda slot, group: (0, group)),
            pl.BlockSpec((8, 2 * STATE), lambda slot, group: (0, INNER // (2 * STATE))),
            pl.BlockSpec((1, 128), fixed),
            pl.BlockSpec((1, 128), fixed),
        ],
        out_specs=[
            pl.BlockSpec((LEN, GCOLS), lambda slot, group: (slot, group)),
            pl.BlockSpec((LEN, GCOLS), lambda slot, group: (slot, group)),
            pl.BlockSpec((LEN, 2 * STATE), by_slot),
            pl.BlockSpec((LEN, 128), by_slot),
            pl.BlockSpec((LEN, 128), by_slot),
        ],
        out_shape=[
            jax.ShapeDtypeStruct((rows, INNER), F32),
            jax.ShapeDtypeStruct((rows, INNER), BF),
            jax.ShapeDtypeStruct((rows, 2 * STATE), BF),
            jax.ShapeDtypeStruct((rows, 128), F32),
            jax.ShapeDtypeStruct((rows, 128), F32),
        ],
        scratch_shapes=[
            pltpu.VMEM((LEN, LEN), F32),
            pltpu.VMEM((128, LEN), F32),
            pltpu.VMEM((128, LEN), F32),
        ],
        compiler_params=pltpu.CompilerParams(
            dimension_semantics=("arbitrary", "arbitrary"), vmem_limit_bytes=16 * MIB
        ),
        name="scan_forward",
        cost_estimate=cost(0.2),
    )(xconv, xconv, raw, taps, taps, dtb, alog)


STRIP = 64
CHUNK = 128


def middle_kernel(
    index_ref, len_ref, summed_ref, v_ref, gate_ref, tok_ref, og_ref, gain_ref, skip_ref, *refs
):
    shards = refs[0:6]
    out_ref, m_ref, do_ref, dscan_ref, dgate_ref, rowsum_ref, sums_ref = refs[6:13]
    wo_ref, unit_ref, dm_ref, scale_ref, high_ref, low_ref, sems = refs[13:]
    step = pl.program_id(0)
    block = summed_ref.shape[0]
    per_slot = LEN // block
    count = len_ref[step // per_slot]
    row = lax.broadcasted_iota(jnp.int32, (block, 1), 0) + lax.rem(step, per_slot) * block
    live = row < count
    chunks = [slice(at, at + CHUNK) for at in range(0, INNER, CHUNK)]
    copies = out_proj_copies(index_ref[0], shards, wo_ref, sems)

    @pl.when(step == 0)
    def _():
        sums_ref[...] = jnp.zeros_like(sums_ref)
        for copy in copies:
            copy.start()

    def fold_rows(v):
        return sum(v[at : at + 8] for at in range(0, STRIP, 8))

    def forward(at, carry):
        rows = pl.ds(pl.multiple_of(at * STRIP, STRIP), STRIP)
        total = jnp.zeros((STRIP, 128), F32)
        for c in chunks:
            scanned = summed_ref[rows, c] + skip_ref[:, c] * v_ref[rows, c].astype(F32)
            gate = gate_ref[rows, c]
            gated = scanned * (gate * sigmoid(gate))
            unit_ref[rows, c] = gated
            total = total + gated * gated
        scale = lax.rsqrt(jnp.sum(total, axis=1, keepdims=True) * (1.0 / INNER) + 1e-05)
        scale_ref[rows, :] = jnp.broadcast_to(scale, (STRIP, 128))
        for c in chunks:
            unit = unit_ref[rows, c] * scale
            unit_ref[rows, c] = unit
            m_ref[rows, c] = (unit * gain_ref[:, c]).astype(BF)
        return carry

    lax.fori_loop(0, block // STRIP, forward, 0)
    dout = jnp.where(live, og_ref[...].astype(F32), 0.0).astype(BF)
    do_ref[...] = dout

    @pl.when(step == 0)
    def _():
        for copy in copies:
            copy.wait()

    result = tok_ref[...].astype(F32) + dot(m_ref[...], wo_ref[...])
    out_ref[...] = jnp.where(live, result, 0.0).astype(BF)
    dm_ref[...] = dot_nt(dout, wo_ref[...])

    def backward(at, carry):
        rows = pl.ds(pl.multiple_of(at * STRIP, STRIP), STRIP)
        total = jnp.zeros((STRIP, 128), F32)
        for c in chunks:
            unit = unit_ref[rows, c]
            grown = dm_ref[rows, c] * unit
            sums_ref[0:8, c] += fold_rows(grown)
            total = total + grown * gain_ref[:, c]
        mean = jnp.sum(total, axis=1, keepdims=True) * (1.0 / INNER)
        scale = scale_ref[rows, 0:1]
        for c in chunks:
            dgated = scale * (dm_ref[rows, c] * gain_ref[:, c] - unit_ref[rows, c] * mean)
            summed = summed_ref[rows, c]
            v = v_ref[rows, c].astype(F32)
            gate = gate_ref[rows, c]
            sg = sigmoid(gate)
            act = gate * sg
            dscan = dgated * act
            dscan_ref[rows, c] = dscan
            scanned = summed + skip_ref[:, c] * v
            dgate_ref[rows, c] = (dgated * scanned * (sg + act * (1.0 - sg))).astype(BF)
            skipped = dscan * v
            sums_ref[8:16, c] += fold_rows(skipped)
            product = dscan.astype(BF).astype(F32) * summed
            high = product.astype(BF)
            high_ref[rows, c] = high
            low_ref[rows, c] = (product - high.astype(F32)).astype(BF)
        return carry

    lax.fori_loop(0, block // STRIP, backward, 0)
    channel = lax.broadcasted_iota(jnp.int32, (INNER, 128), 0)
    lane = lax.broadcasted_iota(jnp.int32, (INNER, 128), 1)
    heads = jnp.where(channel // 64 == lane, 1.0, 0.0).astype(BF)
    rowsum_ref[...] = dot(high_ref[...], heads) + dot(low_ref[...], heads)


def middle(index, lengths, summed, v, gate, tokens, out_grad, shards, gain, skip, block=256):
    rows = summed.shape[0]
    wide = pl.BlockSpec((block, INNER), lambda step, index, lens: (step, 0))
    narrow = pl.BlockSpec((block, D), lambda step, index, lens: (step, 0))
    vector = pl.BlockSpec((1, INNER), lambda step, index, lens: (0, 0))
    return pl.pallas_call(
        middle_kernel,
        grid_spec=pltpu.PrefetchScalarGridSpec(
            num_scalar_prefetch=2,
            grid=(rows // block,),
            in_specs=[wide, wide, wide, narrow, narrow, vector, vector]
            + [pl.BlockSpec(memory_space=pl.ANY) for _ in shards],
            out_specs=[
                narrow, wide, narrow, wide, wide,
                pl.BlockSpec((block, 128), lambda step, index, lens: (step, 0)),
                pl.BlockSpec((16, INNER), lambda step, index, lens: (0, 0)),
            ],
            scratch_shapes=[
                pltpu.VMEM((INNER, D), BF),
                pltpu.VMEM((block, INNER), F32),
                pltpu.VMEM((block, INNER), F32),
                pltpu.VMEM((block, 128), F32),
                pltpu.VMEM((block, INNER), BF),
                pltpu.VMEM((block, INNER), BF),
                pltpu.SemaphoreType.DMA((18,)),
            ],
        ),
        out_shape=[
            jax.ShapeDtypeStruct((rows, D), BF),
            jax.ShapeDtypeStruct((rows, INNER), BF),
            jax.ShapeDtypeStruct((rows, D), BF),
            jax.ShapeDtypeStruct((rows, INNER), F32),
            jax.ShapeDtypeStruct((rows, INNER), BF),
            jax.ShapeDtypeStruct((rows, 128), F32),
            jax.ShapeDtypeStruct((16, INNER), F32),
        ],
        compiler_params=pltpu.CompilerParams(
            dimension_semantics=("arbitrary",), vmem_limit_bytes=44 * MIB
        ),
        name="middle",
        cost_estimate=cost(0.2),
    )(index, lengths, summed, v, gate, tokens, out_grad, gain, skip, *shards)


def scan_backward_kernel(
    xv_ref, xbc_ref, raw_ref, tv_ref, tbc_ref, dtb_ref, alog_ref, skip_ref,
    v_ref, bc_ref, step_ref, cum_ref, dscan_ref, rowsum_ref,
    dx_ref, dtaps_ref, dsmall_ref,
    st_ref, dst_ref, cumt_ref, colsum_ref,
):
    group = pl.program_id(1)

    @pl.when(group == 0)
    def _():
        bc = bc_ref[...]
        st_ref[...] = dot_nt(bc[:, :STATE], bc[:, STATE:])
        dst_ref[...] = jnp.zeros_like(dst_ref)
        colsum_ref[...] = jnp.zeros_like(colsum_ref)
        cumt_ref[...] = cum_ref[...].T

    shift = lax.rem(128 - GHEADS * group, 128)
    cum_cols = pltpu.roll(cum_ref[...], shift, axis=1)
    step_cols = pltpu.roll(step_ref[...], shift, axis=1)
    cum_rows = cumt_ref[pl.ds(pl.multiple_of(GHEADS * group, GHEADS), GHEADS), :]
    down, across = tri_masks()
    live = across >= down
    dvs = []
    for pair in range(GHEADS // 2):
        lanes = slice(128 * pair, 128 * pair + 128)
        vp = v_ref[:, lanes]
        dsp = dscan_ref[:, lanes].astype(BF)
        top = jnp.zeros((HALF, 128), F32)
        bottom = jnp.zeros((HALF, 128), F32)
        d00 = dst_ref[:HALF, :HALF]
        d01 = dst_ref[:HALF, HALF:]
        d11 = dst_ref[HALF:, HALF:]
        for side in range(2):
            head = 2 * pair + side
            vm = head_lanes(vp, side == 0)
            dsm = head_lanes(dsp, side == 0)
            ci = cum_rows[head : head + 1, :]
            cj = cum_cols[:, head : head + 1]
            sj = step_cols[:, head : head + 1]
            w00 = jnp.where(live, jnp.exp2(ci[:, :HALF] - cj[:HALF]), 0.0) * sj[:HALF]
            w01 = jnp.exp2(ci[:, HALF:] - cj[:HALF]) * sj[:HALF]
            w11 = jnp.where(live, jnp.exp2(ci[:, HALF:] - cj[HALF:]), 0.0) * sj[HALF:]
            dtop = dot_nt(vm[:HALF], dsp)
            dbottom = dot_nt(vm[HALF:], dsp[HALF:])
            d00 = d00 + dtop[:, :HALF] * w00
            d01 = d01 + dtop[:, HALF:] * w01
            d11 = d11 + dbottom * w11
            m00 = (st_ref[:HALF, :HALF] * w00).astype(BF)
            m01 = (st_ref[:HALF, HALF:] * w01).astype(BF)
            m11 = (st_ref[HALF:, HALF:] * w11).astype(BF)
            top = top + dot(jnp.concatenate([m00, m01], axis=1), dsm)
            bottom = bottom + dot(m11, dsm[HALF:])
        dst_ref[:HALF, :HALF] = d00
        dst_ref[:HALF, HALF:] = d01
        dst_ref[HALF:, HALF:] = d11
        dvs.append(jnp.concatenate([top, bottom], axis=0))
    dv = jnp.concatenate(dvs, axis=1)
    channel = lax.broadcasted_iota(jnp.int32, (GCOLS, 128), 0)
    lane = lax.broadcasted_iota(jnp.int32, (GCOLS, 128), 1)
    heads = jnp.where(channel // 64 + GHEADS * group == lane, 1.0, 0.0).astype(BF)
    colsum_ref[...] += dot_split(v_ref[...].astype(F32) * dv, heads)
    dact = dv + skip_ref[...] * dscan_ref[...]
    columns = pl.ds(pl.multiple_of(GCOLS * group, GCOLS), GCOLS)
    dx = conv_backward(
        xv_ref[...], tv_ref[0:4, :], tv_ref[4:5, :], dact, dtaps_ref, columns
    )
    dx_ref[:, columns] = dx.astype(BF)

    @pl.when(group == GROUPS - 1)
    def _():
        bc = bc_ref[...]
        dst = dst_ref[...].astype(BF)
        db = dot(dst, bc[:, STATE:])
        dc = dot_tn(dst, bc[:, :STATE])
        dbc = conv_backward(
            xbc_ref[...], tbc_ref[0:4, :], tbc_ref[4:5, :],
            jnp.concatenate([db, dc], axis=1), dtaps_ref, slice(INNER, CONVCH),
        )
        dx_ref[:, INNER:CONVCH] = dbc.astype(BF)
        row = lax.broadcasted_iota(jnp.int32, (LEN, LEN), 0)
        col = lax.broadcasted_iota(jnp.int32, (LEN, LEN), 1)
        upper = jnp.where(col >= row, 1.0, 0.0).astype(BF)
        colsum = colsum_ref[...]
        dlog = dot_exact(upper, rowsum_ref[...] - colsum)
        step = step_ref[...]
        rate = jnp.exp(alog_ref[...])
        z = raw_ref[...] + dtb_ref[...]
        sg = 1.0 / (1.0 + jnp.exp(-z))
        tiny = z < -20.0
        ratio = jnp.where(tiny, 1.0, sg / jnp.where(tiny, 1.0, step))
        draw = colsum * ratio - dlog * rate * sg
        lane32 = lax.broadcasted_iota(jnp.int32, (LEN, 128), 1)
        draw = jnp.where(lane32 < HEADS, draw, 0.0)
        dx_ref[:, CONVCH:] = draw.astype(BF)
        dalog = -dlog * step * rate
        dsmall_ref[0] = jnp.concatenate(
            [
                jnp.sum(draw, axis=0, keepdims=True),
                jnp.sum(dalog, axis=0, keepdims=True),
                jnp.zeros((6, 128), F32),
            ],
            axis=0,
        )


def scan_backward(xconv, raw, taps, dtb, alog, skip, v, bc, step, cum, dscan, rowsum, slots):
    rows = slots * LEN
    by_slot = lambda slot, group: (slot, 0)
    fixed = lambda slot, group: (0, 0)
    by_group = pl.BlockSpec((LEN, GCOLS), lambda slot, group: (slot, group))
    last = INNER // (2 * STATE)
    return pl.pallas_call(
        scan_backward_kernel,
        grid=(slots, GROUPS),
        in_specs=[
            by_group,
            pl.BlockSpec((LEN, 2 * STATE), lambda slot, group: (slot, last)),
            pl.BlockSpec((LEN, 128), by_slot),
            pl.BlockSpec((8, GCOLS), lambda slot, group: (0, group)),
            pl.BlockSpec((8, 2 * STATE), lambda slot, group: (0, last)),
            pl.BlockSpec((1, 128), fixed),
            pl.BlockSpec((1, 128), fixed),
            pl.BlockSpec((1, GCOLS), lambda slot, group: (0, group)),
            by_group,
            pl.BlockSpec((LEN, 2 * STATE), by_slot),
            pl.BlockSpec((LEN, 128), by_slot),
            pl.BlockSpec((LEN, 128), by_slot),
            by_group,
            pl.BlockSpec((LEN, 128), by_slot),
        ],
        out_specs=[
            pl.BlockSpec((LEN, CONVCH + 128), by_slot),
            pl.BlockSpec((1, 8, CONVCH), lambda slot, group: (slot, 0, 0)),
            pl.BlockSpec((1, 8, 128), lambda slot, group: (slot, 0, 0)),
        ],
        out_shape=[
            jax.ShapeDtypeStruct((rows, CONVCH + 128), BF),
            jax.ShapeDtypeStruct((slots, 8, CONVCH), F32),
            jax.ShapeDtypeStruct((slots, 8, 128), F32),
        ],
        scratch_shapes=[
            pltpu.VMEM((LEN, LEN), F32),
            pltpu.VMEM((LEN, LEN), F32),
            pltpu.VMEM((128, LEN), F32),
            pltpu.VMEM((LEN, 128), F32),
        ],
        compiler_params=pltpu.CompilerParams(
            dimension_semantics=("arbitrary", "arbitrary"), vmem_limit_bytes=56 * MIB
        ),
        name="scan_backward",
        cost_estimate=cost(0.2),
    )(xconv, xconv, raw, taps, taps, dtb, alog, skip, v, bc, step, cum, dscan, rowsum)


def shard_copies(me, shards, whole, sems, first, high):
    part = shards[0].shape[1]
    half = part // 2
    copies = []
    for i, (src, k, at) in enumerate(
        zip(shards, (0, 1, 2, 2, 3, 3), (0, 0, 0, half, 0, half))
    ):
        place = pl.ds(pl.multiple_of((me ^ k) * part + at, half), src.shape[1])
        rows = pl.ds(first, high)
        copies.append(pltpu.make_async_copy(src.at[rows, :], whole.at[rows, place], sems.at[i]))
    return copies


def out_proj_copies(me, shards, whole, sems):
    part = shards[0].shape[0]
    place = lambda k: pl.ds(pl.multiple_of((me ^ k) * part, part), part)
    copies = [
        pltpu.make_async_copy(src, whole.at[place(k), :], sems.at[k])
        for k, src in enumerate(shards[:2])
    ]
    for i, src in enumerate(shards[2:]):
        for block in range(4):
            lanes = pl.ds((i % 2) * 512 + block * 128, 128)
            rows = pl.ds(INNER + block * part, part)
            copies.append(
                pltpu.make_async_copy(
                    src.at[rows, :], whole.at[place(2 + i // 2), lanes], sems.at[len(copies)]
                )
            )
    return copies


def project_kernel(columns, block, tail, index_ref, n_ref, *refs):
    shards, (out_ref, *rest), (whole_ref, sems) = refs[0:6], refs[6:-2], refs[-2:]
    me = index_ref[0]
    step = pl.program_id(0)
    steps = columns // block

    def copies(at):
        return shard_copies(me, shards, whole_ref, sems.at[at], at * block, block)

    @pl.when(step == 0)
    def _():
        if tail:
            whole_ref[columns:, :] = jnp.zeros((whole_ref.shape[0] - columns, D), BF)
            last = shard_copies(me, shards, whole_ref, sems.at[steps], columns, HEADS)
            for copy in last:
                copy.start()
        for at in range(steps):
            for copy in copies(at):
                copy.start()
        if tail:
            for copy in last:
                copy.wait()
            rest[0][...] = dot_nt(n_ref[...], whole_ref[columns:, :])

    for at in range(steps):

        @pl.when(step == at)
        def _(at=at):
            for copy in copies(at):
                copy.wait()
            out_ref[...] = dot_nt(n_ref[...], whole_ref[at * block : (at + 1) * block, :])


def project(index, normed, shards, columns, block, tail):
    rows = normed.shape[0]
    out_specs = [pl.BlockSpec((rows, block), lambda step, index: (0, step))]
    out_shape = [jax.ShapeDtypeStruct((rows, columns), F32)]
    if tail:
        out_specs.append(pl.BlockSpec((rows, 128), lambda step, index: (0, 0)))
        out_shape.append(jax.ShapeDtypeStruct((rows, 128), F32))
    steps = columns // block
    return pl.pallas_call(
        functools.partial(project_kernel, columns, block, tail),
        grid_spec=pltpu.PrefetchScalarGridSpec(
            num_scalar_prefetch=1,
            grid=(steps,),
            in_specs=[pl.BlockSpec(normed.shape, lambda step, index: (0, 0))]
            + [pl.BlockSpec(memory_space=pl.ANY) for _ in shards],
            out_specs=out_specs,
            scratch_shapes=[
                pltpu.VMEM((columns + 128 if tail else columns, D), BF),
                pltpu.SemaphoreType.DMA((steps + 1 if tail else steps, 6)),
            ],
        ),
        out_shape=out_shape,
        compiler_params=pltpu.CompilerParams(
            dimension_semantics=("arbitrary",), vmem_limit_bytes=18 * MIB
        ),
        name="project",
        cost_estimate=cost(0.2),
    )(index, normed, *shards)


def input_grad_kernel(index_ref, tok_ref, do_ref, dgate_ref, dx_ref, gain_ref, *refs):
    out_ref, dn_ref, gate_ref, conv_ref, sems = refs[12:]
    me = index_ref[0]
    gate_copies = shard_copies(me, refs[0:6], gate_ref, sems.at[0], 0, INNER)
    conv_copies = shard_copies(me, refs[6:12], conv_ref, sems.at[1], 0, CONVCH + HEADS)
    for copy in gate_copies + conv_copies:
        copy.start()
    live = CONVCH + HEADS
    conv_ref[live:, :] = jnp.zeros((conv_ref.shape[0] - live, D), BF)
    for copy in gate_copies:
        copy.wait()
    dn_ref[...] = dot(dgate_ref[...], gate_ref[...])
    for copy in conv_copies:
        copy.wait()
    dn_ref[...] += dot(dx_ref[...], conv_ref[...])
    chunks = [slice(at, at + CHUNK) for at in range(0, D, CHUNK)]

    def finish(at, carry):
        rows = pl.ds(pl.multiple_of(at * STRIP, STRIP), STRIP)
        squares = jnp.zeros((STRIP, CHUNK), F32)
        for c in chunks:
            x = tok_ref[rows, c].astype(F32)
            squares = squares + x * x
        scale = lax.rsqrt(jnp.sum(squares, axis=1, keepdims=True) * (1.0 / D) + 1e-05)
        total = jnp.zeros((STRIP, CHUNK), F32)
        for c in chunks:
            grown = dn_ref[rows, c] * (tok_ref[rows, c].astype(F32) * scale)
            total = total + grown * gain_ref[:, c]
        mean = jnp.sum(total, axis=1, keepdims=True) * (1.0 / D)
        for c in chunks:
            unit = tok_ref[rows, c].astype(F32) * scale
            out_ref[rows, c] = do_ref[rows, c].astype(F32) + scale * (
                dn_ref[rows, c] * gain_ref[:, c] - unit * mean
            )
        return carry

    lax.fori_loop(0, tok_ref.shape[0] // STRIP, finish, 0)


def input_grad(index, tokens, dout, dgate, dx, gain, gate_shards, conv_shards):
    rows = tokens.shape[0]
    whole = lambda v: pl.BlockSpec(v.shape, lambda step, index: (0, 0))
    shards = list(gate_shards) + list(conv_shards)
    return pl.pallas_call(
        input_grad_kernel,
        grid_spec=pltpu.PrefetchScalarGridSpec(
            num_scalar_prefetch=1,
            grid=(1,),
            in_specs=[whole(v) for v in (tokens, dout, dgate, dx, gain)]
            + [pl.BlockSpec(memory_space=pl.ANY) for _ in shards],
            out_specs=pl.BlockSpec((rows, D), lambda step, index: (0, 0)),
            scratch_shapes=[
                pltpu.VMEM((rows, D), F32),
                pltpu.VMEM((INNER, D), BF),
                pltpu.VMEM((CONVCH + 128, D), BF),
                pltpu.SemaphoreType.DMA((2, 6)),
            ],
        ),
        out_shape=jax.ShapeDtypeStruct((rows, D), F32),
        compiler_params=pltpu.CompilerParams(
            dimension_semantics=("arbitrary",), vmem_limit_bytes=34 * MIB
        ),
        name="input_grad",
        cost_estimate=cost(0.2),
    )(index, tokens, dout, dgate, dx, gain, *shards)


def out_grad_kernel(add, core_ref, m0_ref, m1_ref, do_ref, *refs):
    out_ref = refs[-1]
    for yl, m_ref in enumerate((m0_ref, m1_ref)):
        grad = dot_tn(m_ref[...], do_ref[...]).astype(BF)
        for j in range(4):
            at = (slice(32 * yl, 32 * yl + 32), slice(16 * j, 16 * j + 16))
            piece = grad[:, 256 * j : 256 * j + 256].reshape(32, 16, 256)
            if add:
                piece = add_low(piece, refs[0][at])
            out_ref[at] = piece


def gate_grad_kernel(add, core_ref, dgate_ref, n0_ref, n1_ref, *refs):
    out_ref = refs[-1]
    both = jnp.concatenate([n0_ref[...], n1_ref[...]], axis=1)
    grad = dot_tn(dgate_ref[...], both).astype(BF)
    for yl in range(2):
        at = slice(32 * yl, 32 * yl + 32)
        piece = grad[:, 256 * yl : 256 * yl + 256].reshape(32, 64, 256)
        if add:
            piece = add_low(piece, refs[0][at])
        out_ref[at] = piece


def conv_grad_kernel(add, core_ref, dx_ref, n0_ref, n1_ref, *refs):
    out_ref = refs[-1]
    both = jnp.concatenate([n0_ref[...], n1_ref[...]], axis=1)
    grad = dot_tn(dx_ref[...], both)
    for yl in range(2):
        piece = grad[:, 256 * yl : 256 * yl + 256].reshape(16, 72, 256).astype(BF)
        if add:
            piece = add_low(piece, refs[0][yl])
        out_ref[yl] = piece


def part_of(yl):
    return lambda step, core: (0, 2 * yl + core[0])


def at_block(*block):
    return lambda step, core: block


def grad_call(kernel, name, core, operands, specs, got, got_spec, out_spec, out_shape, into):
    operands, specs = list(operands), list(specs)
    if got is not None:
        operands.append(got)
        specs.append(got_spec)
    aliases = {}
    if into is not None:
        aliases = {1 + len(operands): 0}
        operands.append(into)
        specs.append(pl.BlockSpec(memory_space=pl.ANY))
    return pl.pallas_call(
        functools.partial(kernel, got is not None),
        grid_spec=pltpu.PrefetchScalarGridSpec(
            num_scalar_prefetch=1, grid=(1,), in_specs=specs, out_specs=out_spec
        ),
        out_shape=jax.ShapeDtypeStruct(out_shape, BF),
        input_output_aliases=aliases,
        compiler_params=pltpu.CompilerParams(
            dimension_semantics=("arbitrary",), vmem_limit_bytes=24 * MIB
        ),
        name=name,
        cost_estimate=cost(0.2),
    )(core, *operands)


def out_grad_pieces(core, mixed, dout, got=None):
    rows = mixed.shape[0]
    block = pl.BlockSpec((64, 64, 256), at_block(0, 0, 0))
    return grad_call(
        out_grad_kernel, "out_proj_grad", core, (mixed, mixed, dout),
        [
            pl.BlockSpec((rows, INNER // 4), part_of(0)),
            pl.BlockSpec((rows, INNER // 4), part_of(1)),
            pl.BlockSpec((rows, D), at_block(0, 0)),
        ],
        got, block, block, (64, 64 if got is None else 128, 256), None,
    )


def gate_grad_pieces(core, dgate, normed, got=None, into=None):
    rows = normed.shape[0]
    first = 0 if into is None else 1
    return grad_call(
        gate_grad_kernel, "gate_grad", core, (dgate, normed, normed),
        [
            pl.BlockSpec((rows, INNER), at_block(0, 0)),
            pl.BlockSpec((rows, D // 4), part_of(0)),
            pl.BlockSpec((rows, D // 4), part_of(1)),
        ],
        got, pl.BlockSpec((64, 64, 256), at_block(0, 0, 0)),
        pl.BlockSpec((64, 64, 256), at_block(0, first, 0)),
        (64, 64 if into is None else 128, 256), into,
    )


def conv_grad_pieces(core, half, dx, normed, got=None, into=None):
    rows = dx.shape[0]
    high = 16 if got is None else 32
    where = 0 if got is None else half
    return grad_call(
        conv_grad_kernel, "conv_grad", core, (dx, normed, normed),
        [
            pl.BlockSpec((rows, CONVCH // 2), at_block(0, half)),
            pl.BlockSpec((rows, D // 4), part_of(0)),
            pl.BlockSpec((rows, D // 4), part_of(1)),
        ],
        got, pl.BlockSpec((2, 16, 72, 256), at_block(0, 0, 0, 0)),
        pl.BlockSpec((2, 16, 72, 256), at_block(0, where, 0, 0)),
        (2, high, 72, 256), into,
    )


def small_grads_kernel(core_ref, draw_ref, n_ref, dtaps_ref, dsmall_ref, sums_ref, out_ref):
    core = core_ref[0]
    out_ref[...] = jnp.zeros_like(out_ref)
    d_step = dot_tn(draw_ref[...], n_ref[...])[:HEADS]
    dtaps = dtaps_ref[0] + dtaps_ref[1]
    dsmall = dsmall_ref[0] + dsmall_ref[1]
    gate = jnp.sum(sums_ref[0:8, :], axis=0, keepdims=True)
    skip = jnp.sum(sums_ref[8:16, :], axis=0, keepdims=True)
    channel = lax.broadcasted_iota(jnp.int32, (INNER, 128), 0)
    lane = lax.broadcasted_iota(jnp.int32, (INNER, 128), 1)
    heads = jnp.where(channel // 64 == lane, 1.0, 0.0).astype(BF)
    skip = dot_split(jnp.broadcast_to(skip, (8, INNER)), heads)[0:1]
    blank = jnp.zeros((1, 128), F32)
    mixed = jnp.concatenate([dsmall[0:1], dsmall[1:2], skip, blank, blank, blank], axis=1)
    quarter = CONVCH // 4
    for q in range(4):
        yl, to = q // 2, (q % 2) ^ core
        step = d_step[:, 256 * q : 256 * q + 256].reshape(4, 8, 256)
        out_ref[to, yl, 0:4] = step.astype(BF)
        taps = jnp.concatenate(
            [dtaps[0:5, quarter * q : quarter * q + quarter], jnp.zeros((5, 192), F32)], axis=1
        )
        gain = jnp.concatenate(
            [gate[:, 512 * q : 512 * q + 512], jnp.zeros((1, 256), F32)], axis=1
        )
        rows = jnp.concatenate([taps, gain, mixed, jnp.zeros((1, 768), F32)], axis=0).astype(BF)
        for j in range(3):
            out_ref[to, yl, 4 + j] = rows[:, 256 * j : 256 * j + 256]


def small_grads(core, dx, normed, dtaps, dsmall, sums):
    rows = normed.shape[0]
    whole = lambda v: pl.BlockSpec(v.shape, at_block(*([0] * v.ndim)))
    shape = (2, 2, 32, 8, 256)
    return pl.pallas_call(
        small_grads_kernel,
        grid_spec=pltpu.PrefetchScalarGridSpec(
            num_scalar_prefetch=1,
            grid=(1,),
            in_specs=[pl.BlockSpec((rows, 128), at_block(0, CONVCH // 128))]
            + [whole(v) for v in (normed, dtaps, dsmall, sums)],
            out_specs=pl.BlockSpec(shape, at_block(0, 0, 0, 0, 0)),
        ),
        out_shape=jax.ShapeDtypeStruct(shape, BF),
        compiler_params=pltpu.CompilerParams(
            dimension_semantics=("arbitrary",), vmem_limit_bytes=24 * MIB
        ),
        name="small_grads",
        cost_estimate=cost(0.2),
    )(core, dx, normed, dtaps, dsmall, sums)


def finish_kernel(got_ref, w_ref, gain_ref, in_ref, out_ref, norm_ref, small_ref, sum_ref):
    step = pl.program_id(0)
    got = got_ref[...].astype(F32)
    pieces = got.shape[0]

    def put(rows, value):
        in_ref[rows, :] = value
        product = value * w_ref[rows, :].astype(F32)
        sum_ref[...] += product.reshape(-1, 8, D // 4).sum(axis=0)

    @pl.when(step == 0)
    def _():
        sum_ref[...] = jnp.zeros_like(sum_ref)
        put(
            slice(INNER + CONVCH, INNER + CONVCH + HEADS),
            got[0:4, 200:208].reshape(HEADS, D // 4),
        )
        for j in range(3):
            small_ref[:, 256 * j : 256 * j + 256] = got[4 + j, 200:208]

    for j in range(4):
        out_ref[:, 256 * j : 256 * j + 256] = got[:, 16 * j : 16 * j + 16].reshape(16 * pieces, 256)
    put(pl.ds(pl.multiple_of(step * 64 * pieces, 64), 64 * pieces), got[:, 64:128].reshape(-1, 256))
    put(
        pl.ds(pl.multiple_of(INNER + step * 72 * pieces, 64), 72 * pieces),
        got[:, 128:200].reshape(-1, 256),
    )
    norm_ref[...] = jnp.sum(sum_ref[...], axis=0, keepdims=True) / gain_ref[...]


def finish(got, w_in, gain):
    high, wide = w_in.shape
    whole = lambda v: pl.BlockSpec(v, lambda step: (0, 0))
    return pl.pallas_call(
        finish_kernel,
        grid=(4,),
        in_specs=[
            pl.BlockSpec((8,) + got.shape[1:], lambda step: (step, 0, 0)),
            whole((high, wide)),
            whole((1, wide)),
        ],
        out_specs=[
            whole((high, wide)),
            pl.BlockSpec((INNER // 16, D), lambda step: (step, 0)),
            whole((1, wide)),
            whole((8, 768)),
        ],
        out_shape=[
            jax.ShapeDtypeStruct((high, wide), F32),
            jax.ShapeDtypeStruct((INNER // 4, D), F32),
            jax.ShapeDtypeStruct((1, wide), F32),
            jax.ShapeDtypeStruct((8, 768), F32),
        ],
        scratch_shapes=[pltpu.VMEM((8, wide), F32)],
        compiler_params=pltpu.CompilerParams(
            dimension_semantics=("arbitrary",), vmem_limit_bytes=28 * MIB
        ),
        name="finish",
        cost_estimate=cost(0.2),
    )(got, w_in, gain)


SWAP = [(0, 1), (1, 0)]


def y_shift(by):
    place = lambda y: (y % 2) * 2 + y // 2
    return [(place(y), place((y + by) % 4)) for y in range(4)]


def halves(shard):
    half = shard.shape[1] // 2
    return shard[:, :half], shard[:, half:]


def from_y(first, second):
    return (
        lax.ppermute(first, ("yl", "yh"), y_shift(1)),
        lax.ppermute(second, ("yl", "yh"), y_shift(-1)),
    )


def from_core(*values):
    return tuple(lax.ppermute(v, "core", SWAP) for v in values)


def blocks_of_lanes(v):
    return [v[:, at : at + 128] for at in range(0, v.shape[1], 128)]


def after(values, *others):
    return lax.optimization_barrier((values,) + others)[0]


def exchange(half):
    return lax.all_to_all(half, ("yl", "z", "x", "yh"), 0, 0, tiled=True)


def add_up(got):
    return jnp.sum(got.astype(F32), axis=0).astype(BF)


def spread_rows(rows):
    copies = jnp.broadcast_to(rows[None], (32,) + rows.shape)
    return lax.all_to_all(copies, ("z", "x", "yh"), 0, 0, tiled=True)


def lay_out(norm_gain, conv_weight, conv_bias, dt_bias, a_log, d_skip, gate_gain):
    quarter = CONVCH // 4
    wide = lambda v: jnp.pad(v, (0, quarter - v.shape[0]))[None, :]
    mixed = jnp.concatenate([norm_gain, dt_bias, a_log, d_skip])
    return jnp.concatenate(
        [conv_weight, conv_bias[None, :], wide(gate_gain), wide(mixed), jnp.zeros((1, quarter), conv_weight.dtype)],
        axis=0,
    )


def local(
    tokens, norm_gain, in_proj, conv_weight, conv_bias, dt_bias, a_log, d_skip, gate_gain,
    out_proj, out_grad, lengths,
):
    slots = lengths.shape[0]
    quarter = CONVCH // 4
    me = lax.axis_index("yl") * 2 + lax.axis_index("core")
    index = me[None].astype(jnp.int32)

    w_in = in_proj.T
    conv_own, gate_own = w_in[INNER:], w_in[:INNER]
    conv_halves = lax.optimization_barrier(halves(conv_own))
    conv_y = from_y(*conv_halves)
    conv_rest = from_core(conv_own, *conv_y)
    conv_shards = (conv_own, conv_rest[0]) + conv_y + conv_rest[1:]
    small_in = (norm_gain, conv_weight, conv_bias, dt_bias, a_log, d_skip, gate_gain)
    small_in = lax.optimization_barrier(small_in + conv_halves)[:7]
    small = lay_out(*small_in)
    own = small
    core = lax.ppermute(own, "core", SWAP)
    other = lax.ppermute(own, "yl", SWAP)
    both = lax.ppermute(other, "core", SWAP)
    natural = jnp.take(jnp.stack([own, core, other, both]), jnp.arange(4) ^ me, axis=0)
    natural = lax.optimization_barrier(natural.astype(F32))
    taps = natural.transpose(1, 0, 2).reshape(8, CONVCH)
    gate_gain_all = natural[:, 5, : INNER // 4].reshape(1, INNER)
    gain = natural[:, 6, : D // 4].reshape(1, D)
    heads = natural[:, 6, D // 4 : D // 4 + 24].reshape(4, 3, 8).transpose(1, 0, 2).reshape(3, HEADS)
    skip = jnp.repeat(heads[2], INNER // HEADS)[None, :]
    heads = jnp.pad(heads, ((0, 0), (0, 128 - HEADS)))
    dtb, alog = heads[0:1], heads[1:2]

    x = tokens.astype(F32)
    scale = lax.rsqrt(jnp.mean(x * x, axis=1, keepdims=True) + 1e-05)
    normed = lax.optimization_barrier((x * scale * gain).astype(BF))
    second_y = from_y(
        *[
            jnp.concatenate([g] + blocks_of_lanes(o), axis=0)
            for g, o in zip(halves(gate_own), halves(out_proj))
        ]
    )
    xconv, raw = project(index, normed, conv_shards, CONVCH, 768, True)
    summed, v, bc, step, cum = scan_forward(xconv, raw, taps, dtb, alog, slots)
    *second_y, _ = lax.optimization_barrier(second_y + (summed,))
    gate_core, out_core, *second_core = from_core(
        *lax.optimization_barrier((gate_own, out_proj, summed))[:2], *second_y
    )
    gate_shards = (gate_own, gate_core, *second_y, *second_core)
    out_shards = (out_proj, out_core, *second_y, *second_core)
    gate = project(index, normed, gate_shards, INNER, 512, False)[0]
    block_out, mixed, dout, dscan, dgate, rowsum, sums = middle(
        index, lengths, summed, v, gate, tokens, out_grad, out_shards, gate_gain_all, skip, 256
    )
    mine = lax.axis_index("core").astype(jnp.int32)[None]
    theirs = 1 - mine
    send_out = out_grad_pieces(theirs, mixed, dout)
    got_out = lax.ppermute(send_out, "core", SWAP)
    send_gate = gate_grad_pieces(after(theirs, send_out), dgate, normed)
    got_gate = lax.ppermute(send_gate, "core", SWAP)
    h_early = out_grad_pieces(after(mine, send_gate), mixed, dout, got_out)
    h_early = gate_grad_pieces(mine, dgate, normed, got_gate, h_early)
    raw_early = exchange(h_early)
    dx, dtaps, dsmall = scan_backward(
        xconv, raw, taps, dtb, alog, skip, v, bc, step, cum, after(dscan, h_early), rowsum, slots
    )
    send_first = conv_grad_pieces(theirs, 0, dx, normed)
    got_first = lax.ppermute(send_first, "core", SWAP)
    send_second = conv_grad_pieces(after(theirs, send_first), 1, dx, normed)
    got_second = lax.ppermute(send_second, "core", SWAP)
    h_conv = conv_grad_pieces(after(mine, send_second), 0, dx, normed, got_first)
    small = small_grads(mine, dx, normed, dtaps, dsmall, sums)
    got_small = lax.ppermute(small[1], "core", SWAP)
    h_small = add_low(small[0], got_small).reshape(64, 8, 256)
    h_conv = conv_grad_pieces(mine, 1, dx, normed, got_second, h_conv)
    h_late = jnp.concatenate([h_conv.reshape(64, CONVCH // 32, D // 4), h_small], axis=1)
    h_late, raw_early = lax.optimization_barrier((h_late, raw_early))
    raw_late = exchange(h_late)
    r_early = add_up(raw_early)
    tokens_grad = input_grad(
        index, tokens, dout, dgate, after(dx, h_late), gain, gate_shards, conv_shards
    )
    r_conv = add_up(raw_late)
    whole = spread_rows(jnp.concatenate([r_early, r_conv], axis=0))
    g_in, g_out, g_norm, s = finish(whole, w_in, norm_gain.astype(F32)[None, :])
    of_heads = lambda at: lax.dynamic_slice_in_dim(s[6], at + HEADS // 4 * me, HEADS // 4, axis=0)
    return (
        block_out,
        tokens_grad,
        g_norm[0],
        g_in.T,
        s[0:4, :quarter],
        s[4, :quarter],
        of_heads(0),
        of_heads(128),
        of_heads(256),
        s[5, : INNER // 4],
        g_out,
    )


def solution(mesh):
    names = ("yl", "core", "z", "x", "yh")
    fine = Mesh(mesh.devices.reshape(2, 2, 4, 4, 2), names)
    every = P(names, None)
    shard = P(("yl", "core"))
    rows = P(("yl", "core"), None)
    columns = P(None, ("yl", "core"))
    return jax.shard_map(
        local,
        mesh=fine,
        in_specs=(
            every, shard, rows, columns, shard, shard, shard, shard, shard, rows, every, P(names),
        ),
        out_specs=(
            every, every, shard, rows, columns, shard, shard, shard, shard, shard, rows,
        ),
        check_vma=False,
    )
```

```python
import functools
import jax
import jax.numpy as jnp
from jax import lax
from jax.experimental import pallas as pl
from jax.experimental.pallas import tpu as pltpu
from jax.sharding import Mesh, PartitionSpec as P

D = 1024
INNER = 2048
CONV = 4
LEN = 256
HEADS = 32
STATE = 128
CONVCH = 2304
HALF = 128
GROUPS = 4
GCOLS = INNER // GROUPS
GHEADS = HEADS // GROUPS
BF = jnp.bfloat16
F32 = jnp.float32
LOG2E = 1.4426950408889634
MIB = 1024 * 1024


def cost(us):
    return pl.CostEstimate(
        flops=int(us * 1.0e9), transcendentals=0, bytes_accessed=int(us * 3.3e6)
    )


def dot(a, b):
    return lax.dot_general(a, b, (((1,), (0,)), ((), ())), preferred_element_type=F32)


def dot_nt(a, b):
    return lax.dot_general(a, b, (((1,), (1,)), ((), ())), preferred_element_type=F32)


def dot_tn(a, b):
    return lax.dot_general(a, b, (((0,), (0,)), ((), ())), preferred_element_type=F32)


def add_low(a, b):
    return (a.astype(F32) + b.astype(F32)).astype(BF)


def dot_exact(ones, v):
    hi = v.astype(BF)
    rest = v - hi.astype(F32)
    mid = rest.astype(BF)
    low = (rest - mid.astype(F32)).astype(BF)
    return dot(ones, hi) + dot(ones, mid) + dot(ones, low)


def dot_split(v, ones):
    hi = v.astype(BF)
    low = (v - hi.astype(F32)).astype(BF)
    return dot(hi, ones) + dot(low, ones)


def sigmoid(v):
    return 0.5 * jnp.tanh(0.5 * v) + 0.5


def rows_down(v, count):
    row = lax.broadcasted_iota(jnp.int32, v.shape, 0)
    return jnp.where(row >= count, pltpu.roll(v, count, axis=0), 0.0)


def rows_up(v, count):
    rows = v.shape[0]
    row = lax.broadcasted_iota(jnp.int32, v.shape, 0)
    return jnp.where(row < rows - count, pltpu.roll(v, rows - count, axis=0), 0.0)


def conv_forward(x, taps, bias):
    total = bias + taps[3:4] * x
    for back in range(1, CONV):
        total = total + taps[3 - back : 4 - back] * rows_down(x, back)
    return total


def conv_backward(x, taps, bias, dact, dtaps_ref, columns):
    v = conv_forward(x, taps, bias)
    sg = sigmoid(v)
    dv = dact * (sg * (1.0 + v * (1.0 - sg)))
    dx = taps[3:4] * dv
    sums = [jnp.sum(dv * x, axis=0, keepdims=True)]
    for back in range(1, CONV):
        dx = dx + taps[3 - back : 4 - back] * rows_up(dv, back)
        sums.insert(0, jnp.sum(dv * rows_down(x, back), axis=0, keepdims=True))
    sums.append(jnp.sum(dv, axis=0, keepdims=True))
    sums.append(jnp.zeros((3, x.shape[1]), F32))
    dtaps_ref[0, :, columns] = jnp.concatenate(sums, axis=0)
    return dx


def step_of(raw, bias):
    z = raw + bias
    return jnp.maximum(z, 0.0) + jnp.log1p(jnp.exp(-jnp.abs(z)))


def tri_masks():
    down = lax.broadcasted_iota(jnp.int32, (HALF, HALF), 0)
    across = lax.broadcasted_iota(jnp.int32, (HALF, HALF), 1)
    return down, across


def head_lanes(v, first):
    lane = lax.broadcasted_iota(jnp.int32, v.shape, 1)
    zero = jnp.zeros_like(v)
    return jnp.where(lane < 64, v, zero) if first else jnp.where(lane < 64, zero, v)


def scan_forward_kernel(
    xv_ref, xbc_ref, raw_ref, tv_ref, tbc_ref, dtb_ref, alog_ref,
    summed_ref, v_ref, bc_ref, step_ref, cum_ref,
    s_ref, cumt_ref, stept_ref,
):
    group = pl.program_id(1)

    @pl.when(group == 0)
    def _():
        act = conv_forward(xbc_ref[...], tbc_ref[0:4, :], tbc_ref[4:5, :])
        bc = (act * sigmoid(act)).astype(BF)
        bc_ref[...] = bc
        s_ref[...] = dot_nt(bc[:, STATE:], bc[:, :STATE])
        step = step_of(raw_ref[...], dtb_ref[...])
        logdecay = -step * jnp.exp(alog_ref[...])
        row = lax.broadcasted_iota(jnp.int32, (LEN, LEN), 0)
        col = lax.broadcasted_iota(jnp.int32, (LEN, LEN), 1)
        lower = jnp.where(row >= col, 1.0, 0.0).astype(BF)
        cum = dot_exact(lower, logdecay) * LOG2E
        step_ref[...] = step
        cum_ref[...] = cum
        cumt_ref[...] = cum.T
        stept_ref[...] = step.T

    act = conv_forward(xv_ref[...], tv_ref[0:4, :], tv_ref[4:5, :])
    v_ref[...] = (act * sigmoid(act)).astype(BF)
    cols = pltpu.roll(cum_ref[...], lax.rem(128 - GHEADS * group, 128), axis=1)
    first = pl.multiple_of(GHEADS * group, GHEADS)
    cum_rows = cumt_ref[pl.ds(first, GHEADS), :]
    step_rows = stept_ref[pl.ds(first, GHEADS), :]
    down, across = tri_masks()
    live = down >= across
    for pair in range(GHEADS // 2):
        lanes = slice(128 * pair, 128 * pair + 128)
        vp = v_ref[:, lanes]
        top = jnp.zeros((HALF, 128), F32)
        bottom = jnp.zeros((HALF, 128), F32)
        for side in range(2):
            head = 2 * pair + side
            vm = head_lanes(vp, side == 0)
            ci = cols[:, head : head + 1]
            cj = cum_rows[head : head + 1, :]
            sj = step_rows[head : head + 1, :]
            w00 = jnp.where(live, jnp.exp2(ci[:HALF] - cj[:, :HALF]), 0.0) * sj[:, :HALF]
            w10 = jnp.exp2(ci[HALF:] - cj[:, :HALF]) * sj[:, :HALF]
            w11 = jnp.where(live, jnp.exp2(ci[HALF:] - cj[:, HALF:]), 0.0) * sj[:, HALF:]
            m00 = (s_ref[:HALF, :HALF] * w00).astype(BF)
            m10 = (s_ref[HALF:, :HALF] * w10).astype(BF)
            m11 = (s_ref[HALF:, HALF:] * w11).astype(BF)
            top = top + dot(m00, vm[:HALF])
            bottom = bottom + dot(jnp.concatenate([m10, m11], axis=1), vm)
        summed_ref[:HALF, lanes] = top
        summed_ref[HALF:, lanes] = bottom


def scan_forward(xconv, raw, taps, dtb, alog, slots):
    rows = slots * LEN
    by_slot = lambda slot, group: (slot, 0)
    fixed = lambda slot, group: (0, 0)
    return pl.pallas_call(
        scan_forward_kernel,
        grid=(slots, GROUPS),
        in_specs=[
            pl.BlockSpec((LEN, GCOLS), lambda slot, group: (slot, group)),
            pl.BlockSpec((LEN, 2 * STATE), lambda slot, group: (slot, INNER // (2 * STATE))),
            pl.BlockSpec((LEN, 128), by_slot),
            pl.BlockSpec((8, GCOLS), lambda slot, group: (0, group)),
            pl.BlockSpec((8, 2 * STATE), lambda slot, group: (0, INNER // (2 * STATE))),
            pl.BlockSpec((1, 128), fixed),
            pl.BlockSpec((1, 128), fixed),
        ],
        out_specs=[
            pl.BlockSpec((LEN, GCOLS), lambda slot, group: (slot, group)),
            pl.BlockSpec((LEN, GCOLS), lambda slot, group: (slot, group)),
            pl.BlockSpec((LEN, 2 * STATE), by_slot),
            pl.BlockSpec((LEN, 128), by_slot),
            pl.BlockSpec((LEN, 128), by_slot),
        ],
        out_shape=[
            jax.ShapeDtypeStruct((rows, INNER), F32),
            jax.ShapeDtypeStruct((rows, INNER), BF),
            jax.ShapeDtypeStruct((rows, 2 * STATE), BF),
            jax.ShapeDtypeStruct((rows, 128), F32),
            jax.ShapeDtypeStruct((rows, 128), F32),
        ],
        scratch_shapes=[
            pltpu.VMEM((LEN, LEN), F32),
            pltpu.VMEM((128, LEN), F32),
            pltpu.VMEM((128, LEN), F32),
        ],
        compiler_params=pltpu.CompilerParams(
            dimension_semantics=("arbitrary", "arbitrary"), vmem_limit_bytes=16 * MIB
        ),
        name="scan_forward",
        cost_estimate=cost(0.2),
    )(xconv, xconv, raw, taps, taps, dtb, alog)


STRIP = 64
CHUNK = 128


def middle_kernel(
    index_ref, len_ref, summed_ref, v_ref, gate_ref, tok_ref, og_ref, gain_ref, skip_ref, *refs
):
    shards = refs[0:6]
    out_ref, m_ref, do_ref, dscan_ref, dgate_ref, rowsum_ref, sums_ref = refs[6:13]
    wo_ref, unit_ref, dm_ref, scale_ref, high_ref, low_ref, sems = refs[13:]
    step = pl.program_id(0)
    block = summed_ref.shape[0]
    per_slot = LEN // block
    count = len_ref[step // per_slot]
    row = lax.broadcasted_iota(jnp.int32, (block, 1), 0) + lax.rem(step, per_slot) * block
    live = row < count
    chunks = [slice(at, at + CHUNK) for at in range(0, INNER, CHUNK)]
    copies = out_proj_copies(index_ref[0], shards, wo_ref, sems)

    @pl.when(step == 0)
    def _():
        sums_ref[...] = jnp.zeros_like(sums_ref)
        for copy in copies:
            copy.start()

    def fold_rows(v):
        return sum(v[at : at + 8] for at in range(0, STRIP, 8))

    def forward(at, carry):
        rows = pl.ds(pl.multiple_of(at * STRIP, STRIP), STRIP)
        total = jnp.zeros((STRIP, 128), F32)
        for c in chunks:
            scanned = summed_ref[rows, c] + skip_ref[:, c] * v_ref[rows, c].astype(F32)
            gate = gate_ref[rows, c]
            gated = scanned * (gate * sigmoid(gate))
            unit_ref[rows, c] = gated
            total = total + gated * gated
        scale = lax.rsqrt(jnp.sum(total, axis=1, keepdims=True) * (1.0 / INNER) + 1e-05)
        scale_ref[rows, :] = jnp.broadcast_to(scale, (STRIP, 128))
        for c in chunks:
            unit = unit_ref[rows, c] * scale
            unit_ref[rows, c] = unit
            m_ref[rows, c] = (unit * gain_ref[:, c]).astype(BF)
        return carry

    lax.fori_loop(0, block // STRIP, forward, 0)
    dout = jnp.where(live, og_ref[...].astype(F32), 0.0).astype(BF)
    do_ref[...] = dout

    @pl.when(step == 0)
    def _():
        for copy in copies:
            copy.wait()

    result = tok_ref[...].astype(F32) + dot(m_ref[...], wo_ref[...])
    out_ref[...] = jnp.where(live, result, 0.0).astype(BF)
    dm_ref[...] = dot_nt(dout, wo_ref[...])

    def backward(at, carry):
        rows = pl.ds(pl.multiple_of(at * STRIP, STRIP), STRIP)
        total = jnp.zeros((STRIP, 128), F32)
        for c in chunks:
            unit = unit_ref[rows, c]
            grown = dm_ref[rows, c] * unit
            sums_ref[0:8, c] += fold_rows(grown)
            total = total + grown * gain_ref[:, c]
        mean = jnp.sum(total, axis=1, keepdims=True) * (1.0 / INNER)
        scale = scale_ref[rows, 0:1]
        for c in chunks:
            dgated = scale * (dm_ref[rows, c] * gain_ref[:, c] - unit_ref[rows, c] * mean)
            summed = summed_ref[rows, c]
            v = v_ref[rows, c].astype(F32)
            gate = gate_ref[rows, c]
            sg = sigmoid(gate)
            act = gate * sg
            dscan = dgated * act
            dscan_ref[rows, c] = dscan
            scanned = summed + skip_ref[:, c] * v
            dgate_ref[rows, c] = (dgated * scanned * (sg + act * (1.0 - sg))).astype(BF)
            skipped = dscan * v
            sums_ref[8:16, c] += fold_rows(skipped)
            product = dscan.astype(BF).astype(F32) * summed
            high = product.astype(BF)
            high_ref[rows, c] = high
            low_ref[rows, c] = (product - high.astype(F32)).astype(BF)
        return carry

    lax.fori_loop(0, block // STRIP, backward, 0)
    channel = lax.broadcasted_iota(jnp.int32, (INNER, 128), 0)
    lane = lax.broadcasted_iota(jnp.int32, (INNER, 128), 1)
    heads = jnp.where(channel // 64 == lane, 1.0, 0.0).astype(BF)
    rowsum_ref[...] = dot(high_ref[...], heads) + dot(low_ref[...], heads)


def middle(index, lengths, summed, v, gate, tokens, out_grad, shards, gain, skip, block=256):
    rows = summed.shape[0]
    wide = pl.BlockSpec((block, INNER), lambda step, index, lens: (step, 0))
    narrow = pl.BlockSpec((block, D), lambda step, index, lens: (step, 0))
    vector = pl.BlockSpec((1, INNER), lambda step, index, lens: (0, 0))
    return pl.pallas_call(
        middle_kernel,
        grid_spec=pltpu.PrefetchScalarGridSpec(
            num_scalar_prefetch=2,
            grid=(rows // block,),
            in_specs=[wide, wide, wide, narrow, narrow, vector, vector]
            + [pl.BlockSpec(memory_space=pl.ANY) for _ in shards],
            out_specs=[
                narrow, wide, narrow, wide, wide,
                pl.BlockSpec((block, 128), lambda step, index, lens: (step, 0)),
                pl.BlockSpec((16, INNER), lambda step, index, lens: (0, 0)),
            ],
            scratch_shapes=[
                pltpu.VMEM((INNER, D), BF),
                pltpu.VMEM((block, INNER), F32),
                pltpu.VMEM((block, INNER), F32),
                pltpu.VMEM((block, 128), F32),
                pltpu.VMEM((block, INNER), BF),
                pltpu.VMEM((block, INNER), BF),
                pltpu.SemaphoreType.DMA((18,)),
            ],
        ),
        out_shape=[
            jax.ShapeDtypeStruct((rows, D), BF),
            jax.ShapeDtypeStruct((rows, INNER), BF),
            jax.ShapeDtypeStruct((rows, D), BF),
            jax.ShapeDtypeStruct((rows, INNER), F32),
            jax.ShapeDtypeStruct((rows, INNER), BF),
            jax.ShapeDtypeStruct((rows, 128), F32),
            jax.ShapeDtypeStruct((16, INNER), F32),
        ],
        compiler_params=pltpu.CompilerParams(
            dimension_semantics=("arbitrary",), vmem_limit_bytes=44 * MIB
        ),
        name="middle",
        cost_estimate=cost(0.2),
    )(index, lengths, summed, v, gate, tokens, out_grad, gain, skip, *shards)


def scan_backward_kernel(
    xv_ref, xbc_ref, raw_ref, tv_ref, tbc_ref, dtb_ref, alog_ref, skip_ref,
    v_ref, bc_ref, step_ref, cum_ref, dscan_ref, rowsum_ref,
    dx_ref, dtaps_ref, dsmall_ref,
    st_ref, dst_ref, cumt_ref, colsum_ref,
):
    group = pl.program_id(1)

    @pl.when(group == 0)
    def _():
        bc = bc_ref[...]
        st_ref[...] = dot_nt(bc[:, :STATE], bc[:, STATE:])
        dst_ref[...] = jnp.zeros_like(dst_ref)
        colsum_ref[...] = jnp.zeros_like(colsum_ref)
        cumt_ref[...] = cum_ref[...].T

    shift = lax.rem(128 - GHEADS * group, 128)
    cum_cols = pltpu.roll(cum_ref[...], shift, axis=1)
    step_cols = pltpu.roll(step_ref[...], shift, axis=1)
    cum_rows = cumt_ref[pl.ds(pl.multiple_of(GHEADS * group, GHEADS), GHEADS), :]
    down, across = tri_masks()
    live = across >= down
    dvs = []
    for pair in range(GHEADS // 2):
        lanes = slice(128 * pair, 128 * pair + 128)
        vp = v_ref[:, lanes]
        dsp = dscan_ref[:, lanes].astype(BF)
        top = jnp.zeros((HALF, 128), F32)
        bottom = jnp.zeros((HALF, 128), F32)
        d00 = dst_ref[:HALF, :HALF]
        d01 = dst_ref[:HALF, HALF:]
        d11 = dst_ref[HALF:, HALF:]
        for side in range(2):
            head = 2 * pair + side
            vm = head_lanes(vp, side == 0)
            dsm = head_lanes(dsp, side == 0)
            ci = cum_rows[head : head + 1, :]
            cj = cum_cols[:, head : head + 1]
            sj = step_cols[:, head : head + 1]
            w00 = jnp.where(live, jnp.exp2(ci[:, :HALF] - cj[:HALF]), 0.0) * sj[:HALF]
            w01 = jnp.exp2(ci[:, HALF:] - cj[:HALF]) * sj[:HALF]
            w11 = jnp.where(live, jnp.exp2(ci[:, HALF:] - cj[HALF:]), 0.0) * sj[HALF:]
            dtop = dot_nt(vm[:HALF], dsp)
            dbottom = dot_nt(vm[HALF:], dsp[HALF:])
            d00 = d00 + dtop[:, :HALF] * w00
            d01 = d01 + dtop[:, HALF:] * w01
            d11 = d11 + dbottom * w11
            m00 = (st_ref[:HALF, :HALF] * w00).astype(BF)
            m01 = (st_ref[:HALF, HALF:] * w01).astype(BF)
            m11 = (st_ref[HALF:, HALF:] * w11).astype(BF)
            top = top + dot(jnp.concatenate([m00, m01], axis=1), dsm)
            bottom = bottom + dot(m11, dsm[HALF:])
        dst_ref[:HALF, :HALF] = d00
        dst_ref[:HALF, HALF:] = d01
        dst_ref[HALF:, HALF:] = d11
        dvs.append(jnp.concatenate([top, bottom], axis=0))
    dv = jnp.concatenate(dvs, axis=1)
    channel = lax.broadcasted_iota(jnp.int32, (GCOLS, 128), 0)
    lane = lax.broadcasted_iota(jnp.int32, (GCOLS, 128), 1)
    heads = jnp.where(channel // 64 + GHEADS * group == lane, 1.0, 0.0).astype(BF)
    colsum_ref[...] += dot_split(v_ref[...].astype(F32) * dv, heads)
    dact = dv + skip_ref[...] * dscan_ref[...]
    columns = pl.ds(pl.multiple_of(GCOLS * group, GCOLS), GCOLS)
    dx = conv_backward(
        xv_ref[...], tv_ref[0:4, :], tv_ref[4:5, :], dact, dtaps_ref, columns
    )
    dx_ref[:, columns] = dx.astype(BF)

    @pl.when(group == GROUPS - 1)
    def _():
        bc = bc_ref[...]
        dst = dst_ref[...].astype(BF)
        db = dot(dst, bc[:, STATE:])
        dc = dot_tn(dst, bc[:, :STATE])
        dbc = conv_backward(
            xbc_ref[...], tbc_ref[0:4, :], tbc_ref[4:5, :],
            jnp.concatenate([db, dc], axis=1), dtaps_ref, slice(INNER, CONVCH),
        )
        dx_ref[:, INNER:CONVCH] = dbc.astype(BF)
        row = lax.broadcasted_iota(jnp.int32, (LEN, LEN), 0)
        col = lax.broadcasted_iota(jnp.int32, (LEN, LEN), 1)
        upper = jnp.where(col >= row, 1.0, 0.0).astype(BF)
        colsum = colsum_ref[...]
        dlog = dot_exact(upper, rowsum_ref[...] - colsum)
        step = step_ref[...]
        rate = jnp.exp(alog_ref[...])
        z = raw_ref[...] + dtb_ref[...]
        sg = 1.0 / (1.0 + jnp.exp(-z))
        tiny = z < -20.0
        ratio = jnp.where(tiny, 1.0, sg / jnp.where(tiny, 1.0, step))
        draw = colsum * ratio - dlog * rate * sg
        lane32 = lax.broadcasted_iota(jnp.int32, (LEN, 128), 1)
        draw = jnp.where(lane32 < HEADS, draw, 0.0)
        dx_ref[:, CONVCH:] = draw.astype(BF)
        dalog = -dlog * step * rate
        dsmall_ref[0] = jnp.concatenate(
            [
                jnp.sum(draw, axis=0, keepdims=True),
                jnp.sum(dalog, axis=0, keepdims=True),
                jnp.zeros((6, 128), F32),
            ],
            axis=0,
        )


def scan_backward(xconv, raw, taps, dtb, alog, skip, v, bc, step, cum, dscan, rowsum, slots):
    rows = slots * LEN
    by_slot = lambda slot, group: (slot, 0)
    fixed = lambda slot, group: (0, 0)
    by_group = pl.BlockSpec((LEN, GCOLS), lambda slot, group: (slot, group))
    last = INNER // (2 * STATE)
    return pl.pallas_call(
        scan_backward_kernel,
        grid=(slots, GROUPS),
        in_specs=[
            by_group,
            pl.BlockSpec((LEN, 2 * STATE), lambda slot, group: (slot, last)),
            pl.BlockSpec((LEN, 128), by_slot),
            pl.BlockSpec((8, GCOLS), lambda slot, group: (0, group)),
            pl.BlockSpec((8, 2 * STATE), lambda slot, group: (0, last)),
            pl.BlockSpec((1, 128), fixed),
            pl.BlockSpec((1, 128), fixed),
            pl.BlockSpec((1, GCOLS), lambda slot, group: (0, group)),
            by_group,
            pl.BlockSpec((LEN, 2 * STATE), by_slot),
            pl.BlockSpec((LEN, 128), by_slot),
            pl.BlockSpec((LEN, 128), by_slot),
            by_group,
            pl.BlockSpec((LEN, 128), by_slot),
        ],
        out_specs=[
            pl.BlockSpec((LEN, CONVCH + 128), by_slot),
            pl.BlockSpec((1, 8, CONVCH), lambda slot, group: (slot, 0, 0)),
            pl.BlockSpec((1, 8, 128), lambda slot, group: (slot, 0, 0)),
        ],
        out_shape=[
            jax.ShapeDtypeStruct((rows, CONVCH + 128), BF),
            jax.ShapeDtypeStruct((slots, 8, CONVCH), F32),
            jax.ShapeDtypeStruct((slots, 8, 128), F32),
        ],
        scratch_shapes=[
            pltpu.VMEM((LEN, LEN), F32),
            pltpu.VMEM((LEN, LEN), F32),
            pltpu.VMEM((128, LEN), F32),
            pltpu.VMEM((LEN, 128), F32),
        ],
        compiler_params=pltpu.CompilerParams(
            dimension_semantics=("arbitrary", "arbitrary"), vmem_limit_bytes=56 * MIB
        ),
        name="scan_backward",
        cost_estimate=cost(0.2),
    )(xconv, xconv, raw, taps, taps, dtb, alog, skip, v, bc, step, cum, dscan, rowsum)


def shard_copies(me, shards, whole, sems, first, high):
    part = shards[0].shape[1]
    half = part // 2
    copies = []
    for i, (src, k, at) in enumerate(
        zip(shards, (0, 1, 2, 2, 3, 3), (0, 0, 0, half, 0, half))
    ):
        place = pl.ds(pl.multiple_of((me ^ k) * part + at, half), src.shape[1])
        rows = pl.ds(first, high)
        copies.append(pltpu.make_async_copy(src.at[rows, :], whole.at[rows, place], sems.at[i]))
    return copies


def out_proj_copies(me, shards, whole, sems):
    part = shards[0].shape[0]
    place = lambda k: pl.ds(pl.multiple_of((me ^ k) * part, part), part)
    copies = [
        pltpu.make_async_copy(src, whole.at[place(k), :], sems.at[k])
        for k, src in enumerate(shards[:2])
    ]
    for i, src in enumerate(shards[2:]):
        for block in range(4):
            lanes = pl.ds((i % 2) * 512 + block * 128, 128)
            rows = pl.ds(INNER + block * part, part)
            copies.append(
                pltpu.make_async_copy(
                    src.at[rows, :], whole.at[place(2 + i // 2), lanes], sems.at[len(copies)]
                )
            )
    return copies


def project_kernel(columns, block, tail, index_ref, n_ref, *refs):
    shards, (out_ref, *rest), (whole_ref, sems) = refs[0:6], refs[6:-2], refs[-2:]
    me = index_ref[0]
    step = pl.program_id(0)
    steps = columns // block

    def copies(at):
        return shard_copies(me, shards, whole_ref, sems.at[at], at * block, block)

    @pl.when(step == 0)
    def _():
        if tail:
            whole_ref[columns:, :] = jnp.zeros((whole_ref.shape[0] - columns, D), BF)
            last = shard_copies(me, shards, whole_ref, sems.at[steps], columns, HEADS)
            for copy in last:
                copy.start()
        for at in range(steps):
            for copy in copies(at):
                copy.start()
        if tail:
            for copy in last:
                copy.wait()
            rest[0][...] = dot_nt(n_ref[...], whole_ref[columns:, :])

    for at in range(steps):

        @pl.when(step == at)
        def _(at=at):
            for copy in copies(at):
                copy.wait()
            out_ref[...] = dot_nt(n_ref[...], whole_ref[at * block : (at + 1) * block, :])


def project(index, normed, shards, columns, block, tail):
    rows = normed.shape[0]
    out_specs = [pl.BlockSpec((rows, block), lambda step, index: (0, step))]
    out_shape = [jax.ShapeDtypeStruct((rows, columns), F32)]
    if tail:
        out_specs.append(pl.BlockSpec((rows, 128), lambda step, index: (0, 0)))
        out_shape.append(jax.ShapeDtypeStruct((rows, 128), F32))
    steps = columns // block
    return pl.pallas_call(
        functools.partial(project_kernel, columns, block, tail),
        grid_spec=pltpu.PrefetchScalarGridSpec(
            num_scalar_prefetch=1,
            grid=(steps,),
            in_specs=[pl.BlockSpec(normed.shape, lambda step, index: (0, 0))]
            + [pl.BlockSpec(memory_space=pl.ANY) for _ in shards],
            out_specs=out_specs,
            scratch_shapes=[
                pltpu.VMEM((columns + 128 if tail else columns, D), BF),
                pltpu.SemaphoreType.DMA((steps + 1 if tail else steps, 6)),
            ],
        ),
        out_shape=out_shape,
        compiler_params=pltpu.CompilerParams(
            dimension_semantics=("arbitrary",), vmem_limit_bytes=18 * MIB
        ),
        name="project",
        cost_estimate=cost(0.2),
    )(index, normed, *shards)


def input_grad_kernel(index_ref, tok_ref, do_ref, dgate_ref, dx_ref, gain_ref, *refs):
    out_ref, dn_ref, gate_ref, conv_ref, sems = refs[12:]
    me = index_ref[0]
    gate_copies = shard_copies(me, refs[0:6], gate_ref, sems.at[0], 0, INNER)
    conv_copies = shard_copies(me, refs[6:12], conv_ref, sems.at[1], 0, CONVCH + HEADS)
    for copy in gate_copies + conv_copies:
        copy.start()
    live = CONVCH + HEADS
    conv_ref[live:, :] = jnp.zeros((conv_ref.shape[0] - live, D), BF)
    for copy in gate_copies:
        copy.wait()
    dn_ref[...] = dot(dgate_ref[...], gate_ref[...])
    for copy in conv_copies:
        copy.wait()
    dn_ref[...] += dot(dx_ref[...], conv_ref[...])
    chunks = [slice(at, at + CHUNK) for at in range(0, D, CHUNK)]

    def finish(at, carry):
        rows = pl.ds(pl.multiple_of(at * STRIP, STRIP), STRIP)
        squares = jnp.zeros((STRIP, CHUNK), F32)
        for c in chunks:
            x = tok_ref[rows, c].astype(F32)
            squares = squares + x * x
        scale = lax.rsqrt(jnp.sum(squares, axis=1, keepdims=True) * (1.0 / D) + 1e-05)
        total = jnp.zeros((STRIP, CHUNK), F32)
        for c in chunks:
            grown = dn_ref[rows, c] * (tok_ref[rows, c].astype(F32) * scale)
            total = total + grown * gain_ref[:, c]
        mean = jnp.sum(total, axis=1, keepdims=True) * (1.0 / D)
        for c in chunks:
            unit = tok_ref[rows, c].astype(F32) * scale
            out_ref[rows, c] = do_ref[rows, c].astype(F32) + scale * (
                dn_ref[rows, c] * gain_ref[:, c] - unit * mean
            )
        return carry

    lax.fori_loop(0, tok_ref.shape[0] // STRIP, finish, 0)


def input_grad(index, tokens, dout, dgate, dx, gain, gate_shards, conv_shards):
    rows = tokens.shape[0]
    whole = lambda v: pl.BlockSpec(v.shape, lambda step, index: (0, 0))
    shards = list(gate_shards) + list(conv_shards)
    return pl.pallas_call(
        input_grad_kernel,
        grid_spec=pltpu.PrefetchScalarGridSpec(
            num_scalar_prefetch=1,
            grid=(1,),
            in_specs=[whole(v) for v in (tokens, dout, dgate, dx, gain)]
            + [pl.BlockSpec(memory_space=pl.ANY) for _ in shards],
            out_specs=pl.BlockSpec((rows, D), lambda step, index: (0, 0)),
            scratch_shapes=[
                pltpu.VMEM((rows, D), F32),
                pltpu.VMEM((INNER, D), BF),
                pltpu.VMEM((CONVCH + 128, D), BF),
                pltpu.SemaphoreType.DMA((2, 6)),
            ],
        ),
        out_shape=jax.ShapeDtypeStruct((rows, D), F32),
        compiler_params=pltpu.CompilerParams(
            dimension_semantics=("arbitrary",), vmem_limit_bytes=34 * MIB
        ),
        name="input_grad",
        cost_estimate=cost(0.2),
    )(index, tokens, dout, dgate, dx, gain, *shards)


def out_grad_kernel(add, core_ref, m0_ref, m1_ref, do_ref, *refs):
    out_ref = refs[-1]
    for yl, m_ref in enumerate((m0_ref, m1_ref)):
        grad = dot_tn(m_ref[...], do_ref[...]).astype(BF)
        for j in range(4):
            at = (slice(32 * yl, 32 * yl + 32), slice(16 * j, 16 * j + 16))
            piece = grad[:, 256 * j : 256 * j + 256].reshape(32, 16, 256)
            if add:
                piece = add_low(piece, refs[0][at])
            out_ref[at] = piece


def gate_grad_kernel(add, core_ref, dgate_ref, n0_ref, n1_ref, *refs):
    out_ref = refs[-1]
    both = jnp.concatenate([n0_ref[...], n1_ref[...]], axis=1)
    grad = dot_tn(dgate_ref[...], both).astype(BF)
    for yl in range(2):
        at = slice(32 * yl, 32 * yl + 32)
        piece = grad[:, 256 * yl : 256 * yl + 256].reshape(32, 64, 256)
        if add:
            piece = add_low(piece, refs[0][at])
        out_ref[at] = piece


def conv_grad_kernel(add, core_ref, dx_ref, n0_ref, n1_ref, *refs):
    out_ref = refs[-1]
    both = jnp.concatenate([n0_ref[...], n1_ref[...]], axis=1)
    grad = dot_tn(dx_ref[...], both)
    for yl in range(2):
        piece = grad[:, 256 * yl : 256 * yl + 256].reshape(16, 72, 256).astype(BF)
        if add:
            piece = add_low(piece, refs[0][yl])
        out_ref[yl] = piece


def part_of(yl):
    return lambda step, core: (0, 2 * yl + core[0])


def at_block(*block):
    return lambda step, core: block


def grad_call(kernel, name, core, operands, specs, got, got_spec, out_spec, out_shape, into):
    operands, specs = list(operands), list(specs)
    if got is not None:
        operands.append(got)
        specs.append(got_spec)
    aliases = {}
    if into is not None:
        aliases = {1 + len(operands): 0}
        operands.append(into)
        specs.append(pl.BlockSpec(memory_space=pl.ANY))
    return pl.pallas_call(
        functools.partial(kernel, got is not None),
        grid_spec=pltpu.PrefetchScalarGridSpec(
            num_scalar_prefetch=1, grid=(1,), in_specs=specs, out_specs=out_spec
        ),
        out_shape=jax.ShapeDtypeStruct(out_shape, BF),
        input_output_aliases=aliases,
        compiler_params=pltpu.CompilerParams(
            dimension_semantics=("arbitrary",), vmem_limit_bytes=24 * MIB
        ),
        name=name,
        cost_estimate=cost(0.2),
    )(core, *operands)


def out_grad_pieces(core, mixed, dout, got=None):
    rows = mixed.shape[0]
    block = pl.BlockSpec((64, 64, 256), at_block(0, 0, 0))
    return grad_call(
        out_grad_kernel, "out_proj_grad", core, (mixed, mixed, dout),
        [
            pl.BlockSpec((rows, INNER // 4), part_of(0)),
            pl.BlockSpec((rows, INNER // 4), part_of(1)),
            pl.BlockSpec((rows, D), at_block(0, 0)),
        ],
        got, block, block, (64, 64 if got is None else 128, 256), None,
    )


def gate_grad_pieces(core, dgate, normed, got=None, into=None):
    rows = normed.shape[0]
    first = 0 if into is None else 1
    return grad_call(
        gate_grad_kernel, "gate_grad", core, (dgate, normed, normed),
        [
            pl.BlockSpec((rows, INNER), at_block(0, 0)),
            pl.BlockSpec((rows, D // 4), part_of(0)),
            pl.BlockSpec((rows, D // 4), part_of(1)),
        ],
        got, pl.BlockSpec((64, 64, 256), at_block(0, 0, 0)),
        pl.BlockSpec((64, 64, 256), at_block(0, first, 0)),
        (64, 64 if into is None else 128, 256), into,
    )


def conv_grad_pieces(core, half, dx, normed, got=None, into=None):
    rows = dx.shape[0]
    high = 16 if got is None else 32
    where = 0 if got is None else half
    return grad_call(
        conv_grad_kernel, "conv_grad", core, (dx, normed, normed),
        [
            pl.BlockSpec((rows, CONVCH // 2), at_block(0, half)),
            pl.BlockSpec((rows, D // 4), part_of(0)),
            pl.BlockSpec((rows, D // 4), part_of(1)),
        ],
        got, pl.BlockSpec((2, 16, 72, 256), at_block(0, 0, 0, 0)),
        pl.BlockSpec((2, 16, 72, 256), at_block(0, where, 0, 0)),
        (2, high, 72, 256), into,
    )


def small_grads_kernel(core_ref, draw_ref, n_ref, dtaps_ref, dsmall_ref, sums_ref, out_ref):
    core = core_ref[0]
    out_ref[...] = jnp.zeros_like(out_ref)
    d_step = dot_tn(draw_ref[...], n_ref[...])[:HEADS]
    dtaps = dtaps_ref[0] + dtaps_ref[1]
    dsmall = dsmall_ref[0] + dsmall_ref[1]
    gate = jnp.sum(sums_ref[0:8, :], axis=0, keepdims=True)
    skip = jnp.sum(sums_ref[8:16, :], axis=0, keepdims=True)
    channel = lax.broadcasted_iota(jnp.int32, (INNER, 128), 0)
    lane = lax.broadcasted_iota(jnp.int32, (INNER, 128), 1)
    heads = jnp.where(channel // 64 == lane, 1.0, 0.0).astype(BF)
    skip = dot_split(jnp.broadcast_to(skip, (8, INNER)), heads)[0:1]
    blank = jnp.zeros((1, 128), F32)
    mixed = jnp.concatenate([dsmall[0:1], dsmall[1:2], skip, blank, blank, blank], axis=1)
    quarter = CONVCH // 4
    for q in range(4):
        yl, to = q // 2, (q % 2) ^ core
        step = d_step[:, 256 * q : 256 * q + 256].reshape(4, 8, 256)
        out_ref[to, yl, 0:4] = step.astype(BF)
        taps = jnp.concatenate(
            [dtaps[0:5, quarter * q : quarter * q + quarter], jnp.zeros((5, 192), F32)], axis=1
        )
        gain = jnp.concatenate(
            [gate[:, 512 * q : 512 * q + 512], jnp.zeros((1, 256), F32)], axis=1
        )
        rows = jnp.concatenate([taps, gain, mixed, jnp.zeros((1, 768), F32)], axis=0).astype(BF)
        for j in range(3):
            out_ref[to, yl, 4 + j] = rows[:, 256 * j : 256 * j + 256]


def small_grads(core, dx, normed, dtaps, dsmall, sums):
    rows = normed.shape[0]
    whole = lambda v: pl.BlockSpec(v.shape, at_block(*([0] * v.ndim)))
    shape = (2, 2, 32, 8, 256)
    return pl.pallas_call(
        small_grads_kernel,
        grid_spec=pltpu.PrefetchScalarGridSpec(
            num_scalar_prefetch=1,
            grid=(1,),
            in_specs=[pl.BlockSpec((rows, 128), at_block(0, CONVCH // 128))]
            + [whole(v) for v in (normed, dtaps, dsmall, sums)],
            out_specs=pl.BlockSpec(shape, at_block(0, 0, 0, 0, 0)),
        ),
        out_shape=jax.ShapeDtypeStruct(shape, BF),
        compiler_params=pltpu.CompilerParams(
            dimension_semantics=("arbitrary",), vmem_limit_bytes=24 * MIB
        ),
        name="small_grads",
        cost_estimate=cost(0.2),
    )(core, dx, normed, dtaps, dsmall, sums)


def finish_kernel(place_ref, *refs):
    got_refs, (w_ref, gain_ref), (in_ref, out_ref, norm_ref, small_ref, sum_ref) = (
        refs[0:8], refs[8:10], refs[10:],
    )
    sum_ref[...] = jnp.zeros_like(sum_ref)
    for i, got_ref in enumerate(got_refs):
        half, far = i // 4, i % 4
        lanes = slice(128 * half, 128 * half + 128)

        def one(at, carry, got_ref=got_ref, half=half, far=far, lanes=lanes):
            near, yh = at // 2, at % 2
            steps = (near, far) if half == 0 else (far, near)
            z = (place_ref[0] + steps[0]) & 3
            x = (place_ref[1] + steps[1]) & 3
            piece = z * 8 + x * 2 + yh
            got = got_ref[near, yh].astype(F32)

            def put(rows, value):
                in_ref[rows, lanes] = value
                product = value * w_ref[rows, lanes].astype(F32)
                sum_ref[:, lanes] += product.reshape(-1, 8, 128).sum(axis=0)

            for j in range(4):
                out_ref[
                    pl.ds(pl.multiple_of(piece * 16, 16), 16),
                    256 * j + 128 * half : 256 * j + 128 * half + 128,
                ] = got[16 * j : 16 * j + 16]
            put(pl.ds(pl.multiple_of(piece * 64, 64), 64), got[64:128])
            put(pl.ds(pl.multiple_of(INNER + piece * 72, 8), 72), got[128:200])

            @pl.when(piece < 4)
            def _():
                put(pl.ds(pl.multiple_of(INNER + CONVCH + piece * 8, 8), 8), got[200:208])

            @pl.when((piece >= 4) & (piece < 7))
            def _():
                small_ref[piece - 4, :, lanes] = got[200:208]

            return carry

        lax.fori_loop(0, 8, one, 0)
    norm_ref[...] = jnp.sum(sum_ref[...], axis=0, keepdims=True) / gain_ref[...]


def finish(place, got, w_in, gain):
    high, wide = w_in.shape
    whole = lambda *v: pl.BlockSpec(v, lambda step, place: (0,) * len(v))
    return pl.pallas_call(
        finish_kernel,
        grid_spec=pltpu.PrefetchScalarGridSpec(
            num_scalar_prefetch=1,
            grid=(1,),
            in_specs=[whole(*v.shape) for v in got] + [whole(high, wide), whole(1, wide)],
            out_specs=[
                whole(high, wide), whole(INNER // 4, D), whole(1, wide), whole(3, 8, wide),
            ],
            scratch_shapes=[pltpu.VMEM((8, wide), F32)],
        ),
        out_shape=[
            jax.ShapeDtypeStruct((high, wide), F32),
            jax.ShapeDtypeStruct((INNER // 4, D), F32),
            jax.ShapeDtypeStruct((1, wide), F32),
            jax.ShapeDtypeStruct((3, 8, wide), F32),
        ],
        compiler_params=pltpu.CompilerParams(
            dimension_semantics=("arbitrary",), vmem_limit_bytes=34 * MIB
        ),
        name="finish",
        cost_estimate=cost(0.2),
    )(place, *got, w_in, gain)


SWAP = [(0, 1), (1, 0)]


def y_shift(by):
    place = lambda y: (y % 2) * 2 + y // 2
    return [(place(y), place((y + by) % 4)) for y in range(4)]


def halves(shard):
    half = shard.shape[1] // 2
    return shard[:, :half], shard[:, half:]


def from_y(first, second):
    return (
        lax.ppermute(first, ("yl", "yh"), y_shift(1)),
        lax.ppermute(second, ("yl", "yh"), y_shift(-1)),
    )


def from_core(*values):
    return tuple(lax.ppermute(v, "core", SWAP) for v in values)


def blocks_of_lanes(v):
    return [v[:, at : at + 128] for at in range(0, v.shape[1], 128)]


def after(values, *others):
    return lax.optimization_barrier((values,) + others)[0]


def exchange(half):
    return lax.all_to_all(half, ("yl", "z", "x", "yh"), 0, 0, tiled=True)


def add_up(got):
    return jnp.sum(got.astype(F32), axis=0).astype(BF)


def from_ring(value, axis):
    return [
        lax.ppermute(value, axis, [(i, (i - by) % 4) for i in range(4)]) for by in (1, 2, 3)
    ]


def spread_rows(rows):
    other = lax.ppermute(rows, "yh", SWAP)
    first = lax.axis_index("yh") == 0
    pair = jnp.stack([jnp.where(first, rows, other), jnp.where(first, other, rows)])
    pair = lax.optimization_barrier((pair[..., :128], pair[..., 128:]))
    sides = [
        jnp.stack([half] + from_ring(half, axis)) for half, axis in zip(pair, ("z", "x"))
    ]
    sides = lax.optimization_barrier(tuple(sides))
    return [
        [side] + from_ring(side, axis) for side, axis in zip(sides, ("x", "z"))
    ]


def lay_out(norm_gain, conv_weight, conv_bias, dt_bias, a_log, d_skip, gate_gain):
    quarter = CONVCH // 4
    wide = lambda v: jnp.pad(v, (0, quarter - v.shape[0]))[None, :]
    mixed = jnp.concatenate([norm_gain, dt_bias, a_log, d_skip])
    return jnp.concatenate(
        [conv_weight, conv_bias[None, :], wide(gate_gain), wide(mixed), jnp.zeros((1, quarter), conv_weight.dtype)],
        axis=0,
    )


def local(
    tokens, norm_gain, in_proj, conv_weight, conv_bias, dt_bias, a_log, d_skip, gate_gain,
    out_proj, out_grad, lengths,
):
    slots = lengths.shape[0]
    quarter = CONVCH // 4
    me = lax.axis_index("yl") * 2 + lax.axis_index("core")
    index = me[None].astype(jnp.int32)

    w_in = in_proj.T
    conv_own, gate_own = w_in[INNER:], w_in[:INNER]
    conv_halves = lax.optimization_barrier(halves(conv_own))
    conv_y = from_y(*conv_halves)
    conv_rest = from_core(conv_own, *conv_y)
    conv_shards = (conv_own, conv_rest[0]) + conv_y + conv_rest[1:]
    small_in = (norm_gain, conv_weight, conv_bias, dt_bias, a_log, d_skip, gate_gain)
    small_in = lax.optimization_barrier(small_in + conv_halves)[:7]
    small = lay_out(*small_in)
    own = small
    core = lax.ppermute(own, "core", SWAP)
    other = lax.ppermute(own, "yl", SWAP)
    both = lax.ppermute(other, "core", SWAP)
    natural = jnp.take(jnp.stack([own, core, other, both]), jnp.arange(4) ^ me, axis=0)
    natural = lax.optimization_barrier(natural.astype(F32))
    taps = natural.transpose(1, 0, 2).reshape(8, CONVCH)
    gate_gain_all = natural[:, 5, : INNER // 4].reshape(1, INNER)
    gain = natural[:, 6, : D // 4].reshape(1, D)
    heads = natural[:, 6, D // 4 : D // 4 + 24].reshape(4, 3, 8).transpose(1, 0, 2).reshape(3, HEADS)
    skip = jnp.repeat(heads[2], INNER // HEADS)[None, :]
    heads = jnp.pad(heads, ((0, 0), (0, 128 - HEADS)))
    dtb, alog = heads[0:1], heads[1:2]

    x = tokens.astype(F32)
    scale = lax.rsqrt(jnp.mean(x * x, axis=1, keepdims=True) + 1e-05)
    normed = lax.optimization_barrier((x * scale * gain).astype(BF))
    second_y = from_y(
        *[
            jnp.concatenate([g] + blocks_of_lanes(o), axis=0)
            for g, o in zip(halves(gate_own), halves(out_proj))
        ]
    )
    xconv, raw = project(index, normed, conv_shards, CONVCH, 768, True)
    summed, v, bc, step, cum = scan_forward(xconv, raw, taps, dtb, alog, slots)
    *second_y, _ = lax.optimization_barrier(second_y + (summed,))
    gate_core, out_core, *second_core = from_core(
        *lax.optimization_barrier((gate_own, out_proj, summed))[:2], *second_y
    )
    gate_shards = (gate_own, gate_core, *second_y, *second_core)
    out_shards = (out_proj, out_core, *second_y, *second_core)
    gate = project(index, normed, gate_shards, INNER, 512, False)[0]
    block_out, mixed, dout, dscan, dgate, rowsum, sums = middle(
        index, lengths, summed, v, gate, tokens, out_grad, out_shards, gate_gain_all, skip, 256
    )
    mine = lax.axis_index("core").astype(jnp.int32)[None]
    theirs = 1 - mine
    send_out = out_grad_pieces(theirs, mixed, dout)
    got_out = lax.ppermute(send_out, "core", SWAP)
    send_gate = gate_grad_pieces(after(theirs, send_out), dgate, normed)
    got_gate = lax.ppermute(send_gate, "core", SWAP)
    h_early = out_grad_pieces(after(mine, send_gate), mixed, dout, got_out)
    h_early = gate_grad_pieces(mine, dgate, normed, got_gate, h_early)
    raw_early = exchange(h_early)
    dx, dtaps, dsmall = scan_backward(
        xconv, raw, taps, dtb, alog, skip, v, bc, step, cum, after(dscan, h_early), rowsum, slots
    )
    send_first = conv_grad_pieces(theirs, 0, dx, normed)
    got_first = lax.ppermute(send_first, "core", SWAP)
    send_second = conv_grad_pieces(after(theirs, send_first), 1, dx, normed)
    got_second = lax.ppermute(send_second, "core", SWAP)
    h_conv = conv_grad_pieces(after(mine, send_second), 0, dx, normed, got_first)
    small = small_grads(mine, dx, normed, dtaps, dsmall, sums)
    got_small = lax.ppermute(small[1], "core", SWAP)
    h_small = add_low(small[0], got_small).reshape(64, 8, 256)
    h_conv = conv_grad_pieces(mine, 1, dx, normed, got_second, h_conv)
    h_late = jnp.concatenate([h_conv.reshape(64, CONVCH // 32, D // 4), h_small], axis=1)
    h_late, raw_early = lax.optimization_barrier((h_late, raw_early))
    raw_late = exchange(h_late)
    r_early = add_up(raw_early)
    tokens_grad = input_grad(
        index, tokens, dout, dgate, after(dx, h_late), gain, gate_shards, conv_shards
    )
    r_conv = add_up(raw_late)
    r_late, tokens_grad = lax.optimization_barrier((r_conv, tokens_grad))
    by_x, by_z = spread_rows(jnp.concatenate([r_early, r_late], axis=0))
    place = jnp.stack([lax.axis_index("z"), lax.axis_index("x")]).astype(jnp.int32)
    g_in, g_out, g_norm, small = finish(
        place, by_x + by_z, w_in, norm_gain.astype(F32)[None, :]
    )
    s = jnp.concatenate([small[0], small[1], small[2]], axis=1)
    of_heads = lambda at: lax.dynamic_slice_in_dim(s[6], at + HEADS // 4 * me, HEADS // 4, axis=0)
    return (
        block_out,
        tokens_grad,
        g_norm[0],
        g_in.T,
        s[0:4, :quarter],
        s[4, :quarter],
        of_heads(0),
        of_heads(128),
        of_heads(256),
        s[5, : INNER // 4],
        g_out,
    )


def solution(mesh):
    names = ("yl", "core", "z", "x", "yh")
    fine = Mesh(mesh.devices.reshape(2, 2, 4, 4, 2), names)
    every = P(names, None)
    shard = P(("yl", "core"))
    rows = P(("yl", "core"), None)
    columns = P(None, ("yl", "core"))
    return jax.shard_map(
        local,
        mesh=fine,
        in_specs=(
            every, shard, rows, columns, shard, shard, shard, shard, shard, rows, every, P(names),
        ),
        out_specs=(
            every, every, shard, rows, columns, shard, shard, shard, shard, shard, rows,
        ),
        check_vma=False,
    )
```
